128 devices in a mesh: expert: 4 (over z), dp: 32 (over x, y, core).
Axes of the slice: x: 4, y: 4, z: 4, core: 2. Of those that a mesh axis runs over, the one named last changes fastest.
Arguments:
- grad_terms: bfloat16 [32, 4, 7168, 1024], P('dp', None, 'expert'), may hold values from -1000 to 1000
- momentum: float32 [4, 2, 4, 1792, 1024], P('expert', None, None, 'dp'), may hold values from -6 to 6
- weights: float32 [4, 7168, 1024], P(None, ('expert', 'dp')), may hold values from -4 to 4
- owner_list: int32 [4], replicated, may hold values from 0 to 3, as said below
Outputs:
- new_weights: float32 [4, 7168, 1024], P(None, ('expert', 'dp'))
- update: bfloat16 [4, 7168, 1024], P(None, ('expert', 'dp'))
- new_momentum: float32 [4, 2, 4, 1792, 1024], P('expert', None, None, 'dp')
- direction_rms: float32 [4], replicated
The draws below stay inside these ranges and needn't reach their ends.
Inputs may be any that keep to these rules, and one draw needn't show every extreme that they name: `owner_list`: each of the 4 groups owns at most 2 of the 4 matrices, and some group owns exactly 2.
All inputs are finite; a program needn't handle non-finite values.
Results may differ from the reference program's by a relative error of at most 0.035.
Values may be sent and summed in bfloat16 or wider, within the bound.
A program may use at most 128 MiB of HBM per device.

```python
import math
import jax
import jax.numpy as jnp
from jax import lax

D = 7168
FF = 1024
SLOTS = 2
ITERS = 3
MATS = 4
ROWB = 1792
FSDP_ROWS = 56
N_EXPERT = 4
N_DP = 32


def draw_grad_terms(key, part):
    key = jax.random.fold_in(key, 3)
    row_key, col_key, base_key = jax.random.split(key, 3)
    row_scale = 10.0 ** jax.random.uniform(row_key, (1, MATS, D, 1), jnp.float32)
    col_scale = 10.0 ** jax.random.uniform(col_key, (1, MATS, 1, FF), jnp.float32)
    ramp_scale = (3.0 ** (jnp.arange(D, dtype=jnp.float32) / D)).reshape(1, 1, D, 1)
    base_values = jnp.clip(jax.random.normal(base_key, (N_DP, MATS, D, FF), jnp.float32), -6.0, 6.0)
    return (0.5 * base_values * row_scale * col_scale * ramp_scale).astype(jnp.bfloat16)


def draw_owner_list(key, part):
    key = jax.random.fold_in(key, 11)
    order_key, heavy_key, remaining_key = jax.random.split(key, 3)
    order_list = jax.random.permutation(order_key, MATS)
    largest_group = jax.random.randint(heavy_key, (1,), 0, MATS)
    offsets = jax.random.randint(remaining_key, (MATS - SLOTS,), 1, MATS)
    rest_groups = (largest_group + offsets) % MATS
    groups_drawn = jnp.concatenate([jnp.repeat(largest_group, SLOTS), rest_groups]).astype(jnp.int32)
    return jnp.zeros((MATS,), jnp.int32).at[order_list].set(groups_drawn)


def steps_of(stream_key, extent, shards, least, high):
    loudness = 1.0
    for axis_at, blocks in shards:
        draws = jax.random.uniform(jax.random.fold_in(jax.random.fold_in(stream_key, 6), axis_at), (blocks,), jnp.float32, least / len(shards), high / len(shards))
        loudness = loudness * jnp.repeat(jnp.exp(draws), extent[axis_at] // blocks).reshape((-1,) + (1,) * (len(extent) - 1 - axis_at))
    return loudness


def scatter_about(own_key, extent, width, limit, cuts=(), held_as=jnp.bfloat16):
    result = jax.random.normal(own_key, extent, jnp.float32) * width
    if len(cuts) > 0:
        result = steps_of(own_key, extent, cuts, -0.22, 0.18) * result
    return jnp.clip(result, min=-limit, max=limit).astype(held_as)


def setup_inputs(seed: int = 0) -> dict:
    splits = jax.random.split(jax.random.key(seed), 5)
    grad_terms = draw_grad_terms(jax.random.fold_in(splits[4], 71), 0)
    momentum = scatter_about(splits[1], (N_EXPERT, SLOTS, N_EXPERT, ROWB, FF), 1.0, 6.0, ((0, 4), (3, 32)), jnp.float32)
    weights = scatter_about(splits[2], (MATS, D, FF), 0.25, 4.0, ((1, 128),), jnp.float32)
    owner_list = draw_owner_list(jax.random.fold_in(splits[4], 71), 0)
    return dict(grad_terms=grad_terms, momentum=momentum, weights=weights, owner_list=owner_list)


MOMENT = 0.95
CLIP_RMS = 1.0
LEARN = 0.1
DECAY = 0.1
COEF_A = 3.4445
COEF_B = -4.775
COEF_C = 2.0315
NORM_EPS = 1e-07
MEAN_EPS = 1e-06

def reference(grad_terms, momentum, weights, owner_list):

    def accumulate(running, term):
        return (running + term.astype(jnp.float32), None)
    summed, ignored_out = lax.scan(accumulate, jnp.zeros(grad_terms.shape[1:], jnp.float32), grad_terms)
    gradient_input = summed.astype(jnp.bfloat16)
    grad_f32 = gradient_input.astype(jnp.float32)
    mean_sq = jnp.mean(jnp.square(grad_f32))
    factor = jnp.minimum(1.0, CLIP_RMS / jnp.sqrt(mean_sq + MEAN_EPS))
    indices = jnp.arange(MATS)
    same_owner = owner_list[:, None] == owner_list[None, :]
    earlier = indices[None, :] < indices[:, None]
    slot_index = lax.optimization_barrier(jnp.sum(jnp.where(same_owner & earlier, 1, 0), axis=1)).astype(jnp.int32)
    new_moment = MOMENT * momentum
    scale_rms = 0.2 * math.sqrt(max(D, FF))
    orthogonal_list = []
    rms_list = []
    for matrix in range(MATS):
        owner_group = owner_list[matrix]
        slot_number = slot_index[matrix]
        moment_old = momentum[owner_group, slot_number]
        grad_matrix = grad_f32[matrix].reshape(N_EXPERT, ROWB, FF)
        moment_latest = MOMENT * moment_old + factor * grad_matrix
        new_moment = new_moment.at[owner_group, slot_number].set(moment_latest)
        direction = factor * grad_matrix + MOMENT * moment_latest
        square_total = jnp.sum(jnp.square(direction))
        rms_list.append(jnp.sqrt(square_total / float(D * FF)))
        norm_value = jnp.sqrt(square_total) + NORM_EPS
        current = (direction / norm_value).astype(jnp.bfloat16).reshape(D, FF)
        for iteration in range(ITERS):
            blocks = current.reshape(N_EXPERT, N_DP, FSDP_ROWS, FF).astype(jnp.float32)
            partial_value = jnp.einsum('eprf,eprg->pfg', blocks, blocks)
            rounded = lax.optimization_barrier(partial_value.astype(jnp.bfloat16))
            gram_matrix = lax.optimization_barrier(jnp.sum(rounded.astype(jnp.float32), axis=0)).astype(jnp.bfloat16)
            product_one = jnp.dot(current, gram_matrix, preferred_element_type=jnp.float32).astype(jnp.bfloat16)
            product_two = jnp.dot(product_one, gram_matrix, preferred_element_type=jnp.float32)
            current = (COEF_A * current.astype(jnp.float32) + COEF_B * product_one.astype(jnp.float32) + COEF_C * product_two).astype(jnp.bfloat16)
        orthogonal_list.append(current.astype(jnp.float32))
    orthogonal = jnp.stack(orthogonal_list)
    update = (scale_rms * orthogonal).astype(jnp.bfloat16)
    new_weights = weights * (1.0 - LEARN * DECAY) - LEARN * scale_rms * orthogonal
    direction_rms = jnp.stack(rms_list)
    return (new_weights, update, new_moment, direction_rms)
```

```python
import functools
import math

import jax
import jax.numpy as jnp
from jax import lax
from jax.experimental import pallas as pl
from jax.experimental.pallas import tpu as pltpu
from jax.sharding import PartitionSpec as P

D = 7168
FF = 1024
MATS = 4
SLOTS = 2
GROUPS = 4
SIDE = 4
BLOCK = 112
HALF = FF // 2
LANES = 128
CHUNKS = HALF // LANES
PANEL = 256
PART = 80

MOMENT = 0.95
CLIP_RMS = 1.0
LEARN = 0.1
DECAY = 0.1
COEF_A = 3.4445
COEF_B = -4.775
COEF_C = 2.0315
NORM_EPS = 1e-07
MEAN_EPS = 1e-06
F32 = jnp.float32
BF16 = jnp.bfloat16


def place():
    e = lax.axis_index("expert")
    p = lax.axis_index("dp")
    return e, p // 8, (p // 2) % 4, p % 2


def target(e, x, y, c):
    return {"expert": e, "dp": x * 8 + y * 2 + c}


def wrap(v):
    return lax.rem(v + 4, 4)


def greet(e, x, y, c):
    barrier = pltpu.get_barrier_semaphore()
    others = [target(e, wrap(x + dx), wrap(y + dy), c) for dx in range(4) for dy in range(4) if dx + dy]
    others += [target(wrap(e + dz), x, y, lax.rem(c + dc, 2)) for dz in range(4) for dc in range(2) if dz + dc]
    for other in others:
        pl.semaphore_signal(barrier, inc=1, device_id=other)
    pl.semaphore_wait(barrier, len(others))


def remote(src, dst, send, recv, device):
    return pltpu.make_async_remote_copy(src_ref=src, dst_ref=dst, send_sem=send, recv_sem=recv, device_id=device)


def lanes_sum(v):
    return jnp.sum(jnp.sum(v, axis=0, keepdims=True), axis=1, keepdims=True)


def reduce_kernel(table, g, mom, zin, mom_sib, total, own, sib, tr1, dr1, cb1, mid, tr2, dr2, cb2, res, zout,
                  acc, column, plane, own_s, sib_s, sib_r, s1, r1, s2, r2, zs, zr, zl, ms, cs, cr, ps, pr):
    e, x, y, c = place()
    other = 1 - c

    def own_copy(k, m):
        cols = pl.ds(pl.multiple_of(c * HALF + k * LANES, LANES), LANES)
        return pltpu.make_async_copy(g.at[m, :, :, :, cols], own.at[k, m], own_s.at[k, m])

    def sib_copy(k, m):
        cols = pl.ds(pl.multiple_of(other * HALF + k * LANES, LANES), LANES)
        return remote(g.at[m, :, :, :, cols], sib.at[k, m], sib_s.at[k, m], sib_r.at[k, m], target(e, x, y, other))

    for k in range(CHUNKS):
        for m in range(MATS):
            own_copy(k, m).start()
    greet(e, x, y, c)
    for k in range(CHUNKS):
        for m in range(MATS):
            sib_copy(k, m).start()
    mom_copy = remote(mom.at[other], mom_sib, ms.at[0], ms.at[1], target(e, x, y, other))
    mom_copy.start()
    acc[...] = jnp.zeros_like(acc)

    def along(m, first, step):
        on_x = (m < 2) == first
        pos = x if on_x else y
        dev = target(e, wrap(x + step), y, c) if on_x else target(e, x, wrap(y + step), c)
        return pos, dev

    def sign(m):
        return 1 if m % 2 else -1

    def group(ref, k, m, i):
        return ref.at[k, m, i] if m < 2 else ref.at[k, m, :, i]

    def copies1(k, m):
        d = sign(m)
        pos, ahead = along(m, True, d)
        _, back = along(m, True, -d)
        return (
            remote(group(own, k, m, wrap(pos + 2)), tr1.at[k, m], s1.at[k, m, 0], r1.at[k, m, 0], ahead),
            remote(group(own, k, m, wrap(pos - d)), dr1.at[k, m], s1.at[k, m, 1], r1.at[k, m, 1], back),
            remote(group(own, k, m, wrap(pos + d)), cb1.at[k, m], s1.at[k, m, 2], r1.at[k, m, 2], ahead),
        )

    def copies2(k, m):
        d = sign(m)
        pos, ahead = along(m, False, d)
        _, back = along(m, False, -d)
        return (
            remote(mid.at[k, m, wrap(pos + 2)], tr2.at[k, m], s2.at[k, m, 0], r2.at[k, m, 0], ahead),
            remote(mid.at[k, m, wrap(pos - d)], dr2.at[k, m], s2.at[k, m, 1], r2.at[k, m, 1], back),
            remote(mid.at[k, m, wrap(pos + d)], cb2.at[k, m], s2.at[k, m, 2], r2.at[k, m, 2], ahead),
        )

    def z_copy(k, dz, dc):
        j = 2 * dz + dc
        dst = zin.at[e, c, :, pl.ds(pl.multiple_of(k * LANES, LANES), LANES)]
        if j == 0:
            return pltpu.make_async_copy(zout.at[k, 0], dst, zl.at[k])
        return remote(zout.at[k, j], dst, zs.at[k, j], zr.at[k, j], target(wrap(e + dz), x, y, lax.rem(c + dc, 2)))

    def stage_a(k):
        for m in range(MATS):
            own_copy(k, m).wait()
            sib_copy(k, m).wait_recv()
            pos, _ = along(m, True, 1)
            i = wrap(pos + 2)
            to, more = group(own, k, m, i), group(sib, k, m, i)
            for j in range(SIDE):
                to[j] = (to[j].astype(F32) + more[j].astype(F32)).astype(BF16)
            copies1(k, m)[0].start()
        for m in range(MATS):
            pos, _ = along(m, True, 1)
            i = wrap(pos - sign(m))
            to, more = group(own, k, m, i), group(sib, k, m, i)
            for j in range(SIDE):
                to[j] = (to[j].astype(F32) + more[j].astype(F32)).astype(BF16)
            copies1(k, m)[1].start()

    def stage_b(k):
        for m in range(MATS):
            copies = copies1(k, m)
            copies[0].wait_recv()
            pos, _ = along(m, True, 1)
            i = wrap(pos + sign(m))
            to, more, came = group(own, k, m, i), group(sib, k, m, i), tr1.at[k, m]
            for j in range(SIDE):
                to[j] = (to[j].astype(F32) + more[j].astype(F32) + came[j].astype(F32)).astype(BF16)
            copies[2].start()

    def stage_c(k):
        for m in range(MATS):
            copies = copies1(k, m)
            copies[1].wait_recv()
            copies[2].wait_recv()
            pos, _ = along(m, True, 1)
            to, more, came, came2 = group(own, k, m, pos), group(sib, k, m, pos), dr1.at[k, m], cb1.at[k, m]
            for j in range(SIDE):
                v = (to[j].astype(F32) + more[j].astype(F32)) + (came[j].astype(F32) + came2[j].astype(F32))
                mid[k, m, j] = v.astype(BF16)
            copies = copies2(k, m)
            copies[0].start()
            copies[1].start()

    def stage_d(k):
        for m in range(MATS):
            copies = copies2(k, m)
            copies[0].wait_recv()
            pos, _ = along(m, False, 1)
            i = wrap(pos + sign(m))
            mid[k, m, i] = (mid[k, m, i].astype(F32) + tr2[k, m].astype(F32)).astype(BF16)
            copies[2].start()

    def stage_e(k):
        for m in range(MATS):
            copies = copies2(k, m)
            copies[1].wait_recv()
            copies[2].wait_recv()
            pos, _ = along(m, False, 1)
            v = mid[k, m, pos].astype(F32) + (dr2[k, m].astype(F32) + cb2[k, m].astype(F32))
            v = v.astype(BF16).astype(F32)
            res[m] = v
            acc[...] += jnp.sum(jnp.square(v).reshape(BLOCK // 8, 8, LANES), axis=0)
        for dz in (2, 1, 3, 0):
            for dc in range(2):
                slot = wrap(e + dz) * SLOTS + lax.rem(c + dc, 2)
                v = table[slot, 0] * res[0]
                for m in range(1, MATS):
                    v = v + table[slot, m] * res[m]
                zout[k, 2 * dz + dc] = v.astype(BF16)
                z_copy(k, dz, dc).start()

    stages = (stage_a, stage_b, stage_c, stage_d, stage_e)

    def step(t, carry):
        for lag, stage in enumerate(stages):
            @pl.when((t >= lag) & (t < CHUNKS + lag))
            def _():
                stage(t - lag)
        return carry

    lax.fori_loop(0, CHUNKS + len(stages) - 1, step, 0)

    me_col = 2 * e + c
    column[me_col] = acc[...]
    sums = []
    for dz in range(4):
        for dc in range(2):
            if dz + dc:
                j = 2 * dz + dc
                sums.append(remote(acc, column.at[me_col], cs.at[j], cr.at[j],
                                   target(wrap(e + dz), x, y, lax.rem(c + dc, 2))))
    for copy in sums:
        copy.start()
    for copy in sums:
        copy.wait()
    v = column[0]
    for j in range(1, 8):
        v = v + column[j]
    acc[...] = v
    me_plane = 4 * x + y
    plane[me_plane] = v
    sums = []
    for dx in range(4):
        for dy in range(4):
            if dx + dy:
                j = 4 * dx + dy
                sums.append(remote(acc, plane.at[me_plane], ps.at[j], pr.at[j],
                                   target(e, wrap(x + dx), wrap(y + dy), c)))
    for copy in sums:
        copy.start()
    for copy in sums:
        copy.wait()
    v = plane[0]
    for j in range(1, 16):
        v = v + plane[j]
    total[...] = v

    def drain(k, carry):
        for m in range(MATS):
            sib_copy(k, m).wait_send()
            for copy in copies1(k, m) + copies2(k, m):
                copy.wait_send()
        for dz in range(4):
            for dc in range(2):
                z_copy(k, dz, dc).wait()
        return carry

    lax.fori_loop(0, CHUNKS, drain, 0)
    mom_copy.wait()


def gram_kernel(zin, total, mom, mom_sib, new_mom, ret, squares, buf, X, packed, full, rs1, cb, rs1b, mid, rs2, out2, G, A,
                B, Y, back, acc, plane, sq_in, ls, ns, s1, r1, s2, r2, s3, r3, s4, r4, ps, pr, qs, qr, bs, br):
    e, x, y, c = place()
    other = 1 - c
    loads = [
        pltpu.make_async_copy(mom.at[c], buf.at[:, pl.ds(pl.multiple_of(56 * c, 8), 56)], ls.at[0]),
        pltpu.make_async_copy(mom_sib, buf.at[:, pl.ds(pl.multiple_of(56 * other, 8), 56)], ls.at[1]),
    ]
    for copy in loads:
        copy.start()
    greet(e, x, y, c)
    mean = lanes_sum(total[...]) / float(MATS * D * FF)
    factor = jnp.minimum(1.0, CLIP_RMS / jnp.sqrt(mean + MEAN_EPS))
    for copy in loads:
        copy.wait()
    acc[...] = jnp.zeros_like(acc)

    def direction(i, carry):
        for h in range(2):
            cols = pl.ds(h * HALF, HALF)
            grad = factor * zin[i, h].astype(F32)
            moved = MOMENT * buf[i, :, cols] + grad
            buf[i, :, cols] = moved
            v = grad + MOMENT * moved
            X[i, :, cols] = v.astype(BF16)
            sq = jnp.sum(jnp.square(v).reshape(BLOCK // 8, 8, HALF), axis=0)
            acc[...] += sq[:, :128] + sq[:, 128:256] + sq[:, 256:384] + sq[:, 384:]
        return carry

    lax.fori_loop(0, 4, direction, 0)
    new_copies = [
        pltpu.make_async_copy(buf.at[:, pl.ds(pl.multiple_of(56 * c, 8), 56)], new_mom.at[c], ns.at[0]),
        remote(buf.at[:, pl.ds(pl.multiple_of(56 * other, 8), 56)], new_mom.at[c], ns.at[1], ns.at[2],
               target(e, x, y, other)),
    ]
    me_plane = 4 * x + y
    plane[me_plane] = acc[...]
    sums = []
    for dx in range(4):
        for dy in range(4):
            if dx + dy:
                j = 4 * dx + dy
                sums.append(remote(acc, plane.at[me_plane], ps.at[j], pr.at[j],
                                   target(e, wrap(x + dx), wrap(y + dy), c)))
    for copy in sums:
        copy.start()

    rows = X[...].reshape(4 * BLOCK, FF)
    at = 0
    for i in range(4):
        left = rows[:, i * PANEL:(i + 1) * PANEL]
        for j in range(i, 4):
            block = lax.dot_general(left, rows[:, j * PANEL:(j + 1) * PANEL], (((0,), (0,)), ((), ())),
                                    preferred_element_type=F32).astype(BF16)
            packed[at:at + PANEL] = block[:, :LANES]
            packed[at + PANEL:at + 2 * PANEL] = block[:, LANES:]
            at += 2 * PANEL

    def sign(r):
        return 1 if r % 2 else -1

    def along(r, first, step):
        on_x = (r < 2) == first
        pos = x if on_x else y
        dev = target(e, wrap(x + step), y, c) if on_x else target(e, x, wrap(y + step), c)
        return pos, dev

    def group(ref, r, i):
        return ref.at[pl.ds(pl.multiple_of((4 * r + i) * 4 * PART, 16), 4 * PART)]

    def single(ref, r, i, j):
        return ref.at[pl.ds(pl.multiple_of((16 * r + 4 * i + j) * PART, 16), PART)]

    def first_copies(r):
        d = sign(r)
        pos, ahead = along(r, True, d)
        _, back_dev = along(r, True, -d)
        return (
            remote(group(packed, r, wrap(pos + 2)), rs1.at[r, 0], s1.at[r, 0], r1.at[r, 0], ahead),
            remote(group(packed, r, wrap(pos - d)), rs1.at[r, 1], s1.at[r, 1], r1.at[r, 1], back_dev),
            remote(cb.at[r], rs1.at[r, 2], s1.at[r, 2], r1.at[r, 2], ahead),
        )

    def second_copies(r):
        pos, _ = along(r, False, 1)
        out = []
        for step in (2, 1, 3):
            _, dev = along(r, False, step)
            src = mid.at[r, pl.ds(pl.multiple_of(wrap(pos + step) * PART, 16), PART)]
            out.append(remote(src, rs2.at[r, step - 1], s2.at[r, step - 1], r2.at[r, step - 1], dev))
        return out

    def third_copies(r):
        pos1, _ = along(r, True, 1)
        pos2, _ = along(r, False, 1)
        out = []
        for step in (2, 1, 3):
            _, dev = along(r, False, step)
            out.append(remote(out2.at[r], single(full, r, pos1, pos2), s3.at[r, step - 1], r3.at[r, step - 1], dev))
        return out

    def fourth_copies(r):
        d = sign(r)
        pos, ahead = along(r, True, d)
        _, back_dev = along(r, True, -d)
        own = group(full, r, pos)
        passed = group(full, r, wrap(pos - d))
        return (
            remote(own, own, s4.at[r, 0], r4.at[r, 0], ahead),
            remote(own, own, s4.at[r, 1], r4.at[r, 1], back_dev),
            remote(passed, passed, s4.at[r, 2], r4.at[r, 2], ahead),
        )

    ROUTES = (0, 2, 1, 3)
    for r in ROUTES:
        copies = first_copies(r)
        copies[0].start()
        copies[1].start()
    for copy in new_copies:
        copy.start()
    for r in ROUTES:
        copies = first_copies(r)
        copies[0].wait_recv()
        pos, _ = along(r, True, 1)
        mine = group(packed, r, wrap(pos + sign(r)))
        cb[r] = (mine[...].astype(F32) + rs1[r, 0].astype(F32)).astype(BF16)
        copies[2].start()
    for r in ROUTES:
        copies = first_copies(r)
        copies[1].wait_recv()
        copies[2].wait_recv()
        pos, _ = along(r, True, 1)
        mine = group(packed, r, pos)
        mid[r] = (mine[...].astype(F32) + (rs1[r, 1].astype(F32) + rs1[r, 2].astype(F32))).astype(BF16)
        for copy in second_copies(r):
            copy.start()
    for r in ROUTES:
        for copy in second_copies(r):
            copy.wait_recv()
        pos, _ = along(r, False, 1)
        v = mid[r, pl.ds(pl.multiple_of(pos * PART, 16), PART)].astype(F32) + rs2[r, 0].astype(F32)
        v = v + (rs2[r, 1].astype(F32) + rs2[r, 2].astype(F32))
        out2[r] = v.astype(BF16)
    for r in ROUTES:
        pos1, _ = along(r, True, 1)
        pos2, _ = along(r, False, 1)
        single(full, r, pos1, pos2)[...] = out2[r]
        for copy in third_copies(r):
            copy.start()
    for copy in sums:
        copy.wait()
    v = plane[0]
    for j in range(1, 16):
        v = v + plane[j]
    acc[...] = v
    sq_copies = []
    for dz in range(4):
        for dc in range(2):
            if dz + dc:
                j = 2 * dz + dc
                sq_copies.append(remote(acc, sq_in.at[2 * e + c], qs.at[j], qr.at[j],
                                        target(wrap(e + dz), x, y, lax.rem(c + dc, 2))))
    sq_in[2 * e + c] = v
    for copy in sq_copies:
        copy.start()
    norm = jnp.sqrt(lanes_sum(v)) + NORM_EPS
    inv = 1.0 / norm
    inv2 = inv * inv
    for r in ROUTES:
        for copy in third_copies(r):
            copy.wait_recv()
        copies = fourth_copies(r)
        copies[0].start()
        copies[1].start()
    for r in ROUTES:
        copies = fourth_copies(r)
        copies[0].wait_recv()
        copies[2].start()
    for r in ROUTES:
        copies = fourth_copies(r)
        copies[1].wait_recv()
        copies[2].wait_recv()

    at = 0
    for i in range(4):
        for j in range(i, 4):
            for h in range(2):
                block = full[at:at + PANEL]
                G[i * PANEL:(i + 1) * PANEL, j * PANEL + h * LANES:j * PANEL + (h + 1) * LANES] = block
                if i != j:
                    G[j * PANEL + h * LANES:j * PANEL + (h + 1) * LANES, i * PANEL:(i + 1) * PANEL] = block.T
                at += PANEL

    def product(lhs, rhs, out, finish):
        def body(i, carry):
            rows_i = pl.ds(pl.multiple_of(i * PANEL, PANEL), PANEL)
            for j in range(2):
                cols = pl.ds(j * HALF, HALF)
                v = jnp.dot(lhs[rows_i], rhs[:, cols], preferred_element_type=F32)
                out[rows_i, cols] = finish(v, rows_i, cols).astype(BF16)
            return carry
        lax.fori_loop(0, 4, body, 0)

    def advance(rhs, scale):
        for i in range(4):
            v = X[i]
            X[i] = (scale * (COEF_A * v.astype(F32) + jnp.dot(v, rhs[...], preferred_element_type=F32))).astype(BF16)

    def polynomial(src, q, t, out, scale):
        b_s = COEF_B * scale
        c_s = COEF_C * scale * scale
        product(src, src, q, lambda v, i, j: b_s * src[i, j].astype(F32) + c_s * v)
        product(src, q, t, lambda v, i, j: scale * (COEF_A * src[i, j].astype(F32) + v))
        product(t, q, out, lambda v, i, j: COEF_A * t[i, j].astype(F32) + v)

    polynomial(G, A, B, G, inv2)
    advance(A, inv)
    polynomial(G, A, B, G, 1.0)
    advance(A, 1.0)

    def finish(i, carry):
        v = X[i]
        w = jnp.dot(v, G[...], preferred_element_type=F32).astype(BF16)
        z = jnp.dot(w, G[...], preferred_element_type=F32)
        out = COEF_A * v.astype(F32) + COEF_B * w.astype(F32) + COEF_C * z
        Y[...] = out
        for h in range(2):
            for k in range(2):
                back[i, h, k * 56:(k + 1) * 56] = Y[h * 56:(h + 1) * 56, k * HALF:(k + 1) * HALF].astype(BF16)
        return carry

    lax.fori_loop(0, 4, finish, 0)
    returns = []
    for dz in (2, 1, 3, 0):
        for dc in range(2):
            j = 2 * dz + dc
            src = back.at[wrap(e + dz), lax.rem(c + dc, 2)]
            dst = ret.at[e, c]
            if j == 0:
                returns.append(pltpu.make_async_copy(src, dst, bs.at[0]))
            else:
                returns.append(remote(src, dst, bs.at[j], br.at[j], target(wrap(e + dz), x, y, lax.rem(c + dc, 2))))
    for copy in returns:
        copy.start()
    for copy in sq_copies:
        copy.wait()
    squares[...] = sq_in[...]
    for r in ROUTES:
        for copy in second_copies(r) + third_copies(r):
            copy.wait_send()
        for copy in first_copies(r):
            copy.wait_send()
        for copy in fourth_copies(r):
            copy.wait_send()
    for copy in new_copies:
        copy.wait()
    for copy in returns:
        copy.wait()


def assignment(owner_list):
    positions = jnp.arange(MATS)
    same_owner = owner_list[:, None] == owner_list[None, :]
    earlier = positions[None, :] < positions[:, None]
    slot_number = jnp.sum(jnp.where(same_owner & earlier, 1, 0), axis=1).astype(jnp.int32)
    place_of = owner_list * SLOTS + slot_number
    return place_of, (place_of[None, :] == jnp.arange(GROUPS * SLOTS)[:, None]).astype(F32)


ANY = pl.BlockSpec(memory_space=pl.ANY)
VMEM = pl.BlockSpec(memory_space=pltpu.VMEM)
SMEM = pl.BlockSpec(memory_space=pltpu.SMEM)
DMA = pltpu.SemaphoreType.DMA


def per_device(grad_terms, momentum, weights, owner_list):
    place_of, table = assignment(owner_list)
    mom = momentum[0]
    small = (CHUNKS, MATS, BLOCK, LANES)
    large = (CHUNKS, MATS, SIDE, BLOCK, LANES)
    whole = (CHUNKS, MATS, SIDE, SIDE, BLOCK, LANES)
    zin, mom_sib, total = pl.pallas_call(
        reduce_kernel,
        name="reduce_terms",
        out_shape=(
            jax.ShapeDtypeStruct((GROUPS, 2, BLOCK, HALF), BF16),
            jax.ShapeDtypeStruct((GROUPS, 56, FF), F32),
            jax.ShapeDtypeStruct((8, LANES), F32),
        ),
        in_specs=[SMEM, ANY, ANY],
        out_specs=(ANY, ANY, VMEM),
        scratch_shapes=[
            pltpu.VMEM(whole, BF16), pltpu.VMEM(whole, BF16),
            pltpu.VMEM(large, BF16), pltpu.VMEM(large, BF16), pltpu.VMEM(large, BF16), pltpu.VMEM(large, BF16),
            pltpu.VMEM(small, BF16), pltpu.VMEM(small, BF16), pltpu.VMEM(small, BF16),
            pltpu.VMEM((MATS, BLOCK, LANES), F32),
            pltpu.VMEM((CHUNKS, 8, BLOCK, LANES), BF16),
            pltpu.VMEM((8, LANES), F32), pltpu.VMEM((8, 8, LANES), F32), pltpu.VMEM((16, 8, LANES), F32),
            DMA((CHUNKS, MATS)), DMA((CHUNKS, MATS)), DMA((CHUNKS, MATS)),
            DMA((CHUNKS, MATS, 3)), DMA((CHUNKS, MATS, 3)), DMA((CHUNKS, MATS, 3)), DMA((CHUNKS, MATS, 3)),
            DMA((CHUNKS, 8)), DMA((CHUNKS, 8)), DMA((CHUNKS,)), DMA((2,)),
            DMA((8,)), DMA((8,)), DMA((16,)), DMA((16,)),
        ],
        compiler_params=pltpu.CompilerParams(collective_id=0, has_side_effects=True, vmem_limit_bytes=56 << 20),
    )(table, grad_terms.reshape(MATS, SIDE, SIDE, BLOCK, FF), mom)

    new_mom, ret, squares = pl.pallas_call(
        gram_kernel,
        name="orthogonalize",
        out_shape=(
            jax.ShapeDtypeStruct((SLOTS, GROUPS, 56, FF), F32),
            jax.ShapeDtypeStruct((GROUPS, SLOTS, BLOCK, HALF), BF16),
            jax.ShapeDtypeStruct((GROUPS * SLOTS, 8, LANES), F32),
        ),
        in_specs=[VMEM, VMEM, ANY, ANY],
        out_specs=(ANY, ANY, VMEM),
        scratch_shapes=[
            pltpu.VMEM((GROUPS, BLOCK, FF), F32),
            pltpu.VMEM((GROUPS, BLOCK, FF), BF16),
            pltpu.VMEM((64 * PART, LANES), BF16), pltpu.VMEM((64 * PART, LANES), BF16),
            pltpu.VMEM((4, 3, 4 * PART, LANES), BF16),
            pltpu.VMEM((4, 4 * PART, LANES), BF16),
            pltpu.VMEM((8, LANES), F32),
            pltpu.VMEM((4, 4 * PART, LANES), BF16),
            pltpu.VMEM((4, 3, PART, LANES), BF16),
            pltpu.VMEM((4, PART, LANES), BF16),
            pltpu.VMEM((FF, FF), BF16), pltpu.VMEM((FF, FF), BF16), pltpu.VMEM((FF, FF), BF16),
            pltpu.VMEM((BLOCK, FF), F32),
            pltpu.VMEM((GROUPS, 2, BLOCK, HALF), BF16),
            pltpu.VMEM((8, LANES), F32), pltpu.VMEM((16, 8, LANES), F32), pltpu.VMEM((8, 8, LANES), F32),
            DMA((2,)), DMA((3,)),
            DMA((4, 3)), DMA((4, 3)), DMA((4, 3)), DMA((4, 3)), DMA((4, 3)), DMA((4, 3)), DMA((4, 3)), DMA((4, 3)),
            DMA((16,)), DMA((16,)), DMA((8,)), DMA((8,)), DMA((8,)), DMA((8,)),
        ],
        compiler_params=pltpu.CompilerParams(collective_id=1, has_side_effects=True, vmem_limit_bytes=56 << 20),
    )(zin, total, mom, mom_sib)

    rows = ret.reshape(GROUPS * SLOTS, 2, 56, HALF)[place_of]
    rows = rows.transpose(0, 2, 1, 3).reshape(MATS, 56, FF).astype(F32)
    direction_rms = jnp.sqrt(jnp.sum(squares, axis=(1, 2))[place_of] / float(D * FF))
    scale_rms = 0.2 * math.sqrt(max(D, FF))
    update = (scale_rms * rows).astype(BF16)
    new_weights = weights * (1.0 - LEARN * DECAY) - LEARN * scale_rms * rows
    return (new_weights, update, new_mom[None], direction_rms)


def solution(mesh):
    placed = (
        P("dp", None, "expert", None),
        P("expert", None, None, "dp", None),
        P(None, ("expert", "dp"), None),
        P(),
    )
    return jax.shard_map(
        per_device,
        mesh=mesh,
        in_specs=placed,
        out_specs=(
            P(None, ("expert", "dp"), None),
            P(None, ("expert", "dp"), None),
            P("expert", None, None, "dp", None),
            P(),
        ),
        check_vma=False,
    )
```

```python
import math

import jax
import jax.numpy as jnp
from jax import lax
from jax.experimental import pallas as pl
from jax.experimental.pallas import tpu as pltpu
from jax.sharding import PartitionSpec as P

D = 7168
FF = 1024
MATS = 4
SLOTS = 2
GROUPS = 4
SIDE = 4
BLOCK = 112
ROWS = 56
HALF = FF // 2
LANES = 128
CHUNKS = HALF // LANES
LAST = CHUNKS - 1
PANEL = 256
PART = 80

MOMENT = 0.95
CLIP_RMS = 1.0
LEARN = 0.1
DECAY = 0.1
COEF_A = 3.4445
COEF_B = -4.775
COEF_C = 2.0315
NORM_EPS = 1e-07
MEAN_EPS = 1e-06
F32 = jnp.float32
BF16 = jnp.bfloat16

COLUMN = ((2, 0), (2, 1), (1, 0), (1, 1), (3, 0), (3, 1), (0, 1))
PLANE = tuple((dx, dy) for dx in range(4) for dy in range(4) if dx + dy)


def wrap(v):
    return lax.rem(v + 4, 4)


def remote(src, dst, send, recv, device):
    return pltpu.make_async_remote_copy(src_ref=src, dst_ref=dst, send_sem=send, recv_sem=recv, device_id=device)


def whole_sum(v):
    return jnp.sum(jnp.sum(v, axis=0, keepdims=True), axis=1, keepdims=True)


def sign(m):
    return 1 if m % 2 else -1


def muon_kernel(owners, g, mom, new_mom, rows_out, rms_out,
                own, sib, tr1, dr1, cb1, mid, tr2, dr2, cb2, res, zout, zin, buf, X, packed, full, rs1, cbg, midg, rs2,
                out2, G, A, B, T, X2, back, ret, acc, acc2, acc3, acc4, column, plane, plane2, sq_in,
                own_s, sib_s, sib_r, s1, r1, s2, r2, zs, zr, zl, ms, cs, cr, ps, pr, ns, g1s, g1r, g2s, g2r, g3s, g3r,
                g4s, g4r, ps2, pr2, qs, qr, bs, br):
    e = lax.axis_index("expert")
    p = lax.axis_index("dp")
    x, y, c = p // 8, (p // 2) % 4, p % 2
    other = 1 - c

    def target(te, tx, ty, tc):
        return {"expert": te, "dp": tx * 8 + ty * 2 + tc}

    def in_column(dz, dc):
        return target(wrap(e + dz), x, y, lax.rem(c + dc, 2))

    def in_plane(dx, dy):
        return target(e, wrap(x + dx), wrap(y + dy), c)

    places = []
    for m in range(MATS):
        number = jnp.int32(0)
        for m2 in range(m):
            number = number + jnp.where(owners[m2] == owners[m], 1, 0)
        places.append(owners[m] * SLOTS + number)

    def mask(m, slot):
        return jnp.where(places[m] == slot, 1.0, 0.0).astype(F32)

    def own_copy(k, m):
        cols = pl.ds(pl.multiple_of(c * HALF + k * LANES, LANES), LANES)
        return pltpu.make_async_copy(g.at[m, :, :, :, cols], own.at[k, m], own_s.at[k, m])

    def sib_copy(k, m):
        cols = pl.ds(pl.multiple_of(other * HALF + k * LANES, LANES), LANES)
        return remote(g.at[m, :, :, :, cols], sib.at[k, m], sib_s.at[k, m], sib_r.at[k, m], in_column(0, 1))

    def along(m, first, step):
        on_x = (m < 2) == first
        return (x, in_plane(step, 0)) if on_x else (y, in_plane(0, step))

    def group(ref, k, m, i):
        return ref.at[k, m, i] if m < 2 else ref.at[k, m, :, i]

    def copy1(k, m, which):
        d = sign(m)
        pos, dev = along(m, True, -d if which == 1 else d)
        i = wrap(pos + (2, -d, d)[which])
        return remote(group(own, k, m, i), (tr1, dr1, cb1)[which].at[k, m], s1.at[k, m, which], r1.at[k, m, which], dev)

    def copy2(k, m, which):
        d = sign(m)
        pos, dev = along(m, False, -d if which == 1 else d)
        i = wrap(pos + (2, -d, d)[which])
        return remote(mid.at[k, m, i], (tr2, dr2, cb2)[which].at[k, m], s2.at[k, m, which], r2.at[k, m, which], dev)

    def copy2_last(m, which):
        step = (2, 1, 3)[which]
        pos, dev = along(m, False, step)
        return remote(mid.at[LAST, m, wrap(pos + step)], (tr2, dr2, cb2)[which].at[LAST, m], s2.at[LAST, m, which],
                      r2.at[LAST, m, which], dev)

    def z_copy(k, dz, dc):
        j = 2 * dz + dc
        dst = zin.at[e, c, :, pl.ds(pl.multiple_of(k * LANES, LANES), LANES)]
        if j == 0:
            return pltpu.make_async_copy(zout.at[k, 0], dst, zl.at[k])
        return remote(zout.at[k, j], dst, zs.at[k, j], zr.at[k, j], in_column(dz, dc))

    mine_rows = pl.ds(pl.multiple_of(ROWS * c, 8), ROWS)
    other_rows = pl.ds(pl.multiple_of(ROWS * other, 8), ROWS)
    mom_own = pltpu.make_async_copy(mom.at[c], buf.at[:, mine_rows], ms.at[0])
    mom_sib = remote(mom.at[other], buf.at[:, mine_rows], ms.at[1], ms.at[2], in_column(0, 1))

    for k in range(CHUNKS):
        for m in range(MATS):
            own_copy(k, m).start()
    mom_own.start()
    barrier = pltpu.get_barrier_semaphore()
    for dz, dc in COLUMN:
        pl.semaphore_signal(barrier, inc=1, device_id=in_column(dz, dc))
    for dx, dy in PLANE:
        pl.semaphore_signal(barrier, inc=1, device_id=in_plane(dx, dy))
    pl.semaphore_wait(barrier, len(COLUMN) + len(PLANE))
    for k in range(CHUNKS):
        for m in range(MATS):
            sib_copy(k, m).start()
    mom_sib.start()
    acc[...] = jnp.zeros_like(acc)
    acc3[...] = jnp.zeros_like(acc3)

    def pair_sum(k, m, i):
        to, more = group(own, k, m, i), group(sib, k, m, i)
        for j in range(SIDE):
            to[j] = (to[j].astype(F32) + more[j].astype(F32)).astype(BF16)

    def transit(k):
        for m in range(MATS):
            own_copy(k, m).wait()
            sib_copy(k, m).wait_recv()
            pos, _ = along(m, True, 1)
            pair_sum(k, m, wrap(pos + 2))
            copy1(k, m, 0).start()

    def combine(k):
        for m in range(MATS):
            copy1(k, m, 0).wait_recv()
            pos, _ = along(m, True, 1)
            i = wrap(pos + sign(m))
            to, more, came = group(own, k, m, i), group(sib, k, m, i), tr1.at[k, m]
            for j in range(SIDE):
                to[j] = (to[j].astype(F32) + more[j].astype(F32) + came[j].astype(F32)).astype(BF16)
            copy1(k, m, 2).start()

    def direct(k):
        for m in range(MATS):
            pos, _ = along(m, True, 1)
            pair_sum(k, m, wrap(pos - sign(m)))
            copy1(k, m, 1).start()

    def turn(k):
        for m in range(MATS):
            copy1(k, m, 1).wait_recv()
            copy1(k, m, 2).wait_recv()
            pos, _ = along(m, True, 1)
            to, more, came, came2 = group(own, k, m, pos), group(sib, k, m, pos), dr1.at[k, m], cb1.at[k, m]
            for j in range(SIDE):
                v = (to[j].astype(F32) + more[j].astype(F32)) + (came[j].astype(F32) + came2[j].astype(F32))
                mid[k, m, j] = v.astype(BF16)

            @pl.when(k < LAST)
            def _():
                copy2(k, m, 0).start()
                copy2(k, m, 1).start()

            @pl.when(k == LAST)
            def _():
                for which in range(3):
                    copy2_last(m, which).start()

    def combine2(k):
        for m in range(MATS):
            copy2(k, m, 0).wait_recv()
            pos, _ = along(m, False, 1)
            i = wrap(pos + sign(m))
            mid[k, m, i] = (mid[k, m, i].astype(F32) + tr2[k, m].astype(F32)).astype(BF16)
            copy2(k, m, 2).start()

    def collect(k, m, v):
        v = v.astype(BF16).astype(F32)
        res[m] = v
        acc[...] += jnp.sum(jnp.square(v).reshape(BLOCK // 8, 8, LANES), axis=0)

    def send_slots(k):
        for dz in (2, 1, 3, 0):
            for dc in range(2):
                slot = wrap(e + dz) * SLOTS + lax.rem(c + dc, 2)
                v = mask(0, slot) * res[0]
                for m in range(1, MATS):
                    v = v + mask(m, slot) * res[m]
                zout[k, 2 * dz + dc] = v.astype(BF16)
                z_copy(k, dz, dc).start()

    def finish_sum(k):
        for m in range(MATS):
            copy2(k, m, 1).wait_recv()
            copy2(k, m, 2).wait_recv()
            pos, _ = along(m, False, 1)
            collect(k, m, mid[k, m, pos].astype(F32) + (dr2[k, m].astype(F32) + cb2[k, m].astype(F32)))
        send_slots(k)

    stages = ((transit, 0, CHUNKS), (combine, 1, CHUNKS), (direct, 2, CHUNKS), (turn, 3, CHUNKS),
              (combine2, 4, LAST), (finish_sum, 5, LAST))

    def step(t, carry):
        for stage, lag, chunks in stages:
            @pl.when((t >= lag) & (t < chunks + lag))
            def _():
                stage(t - lag)
        return carry

    lax.fori_loop(0, LAST + 5, step, 0)
    for m in range(MATS):
        for which in range(3):
            copy2_last(m, which).wait_recv()
        pos, _ = along(m, False, 1)
        v = mid[LAST, m, pos].astype(F32) + tr2[LAST, m].astype(F32)
        collect(LAST, m, v + (dr2[LAST, m].astype(F32) + cb2[LAST, m].astype(F32)))

    me_column = 2 * e + c
    me_plane = 4 * x + y

    def spread_column(src, dst, send, recv):
        copies = [remote(src, dst.at[me_column], send.at[i], recv.at[i], in_column(*d)) for i, d in enumerate(COLUMN)]
        for copy in copies:
            copy.start()
        dst[me_column] = src[...]
        return copies

    def spread_plane(src, dst, send, recv):
        copies = [remote(src, dst.at[me_plane], send.at[i], recv.at[i], in_plane(*d)) for i, d in enumerate(PLANE)]
        for copy in copies:
            copy.start()
        dst[me_plane] = src[...]
        return copies

    def total_of(copies, ref, count):
        for copy in copies:
            copy.wait_recv()
        v = ref[0]
        for j in range(1, count):
            v = v + ref[j]
        return v

    first = spread_column(acc, column, cs, cr)
    send_slots(LAST)
    acc2[...] = total_of(first, column, 8)
    second = spread_plane(acc2, plane, ps, pr)
    mom_own.wait()
    mom_sib.wait_recv()
    for k in range(CHUNKS):
        for dz in range(4):
            for dc in range(2):
                if dz + dc:
                    z_copy(k, dz, dc).wait_recv()
                else:
                    z_copy(k, 0, 0).wait()
    mean = whole_sum(total_of(second, plane, 16)) / float(MATS * D * FF)
    factor = jnp.minimum(1.0, CLIP_RMS / jnp.sqrt(mean + MEAN_EPS))

    def direction(i, carry):
        for h in range(2):
            cols = pl.ds(h * HALF, HALF)
            grad = factor * zin[i, h].astype(F32)
            moved = MOMENT * buf[i, :, cols] + grad
            buf[i, :, cols] = moved
            v = grad + MOMENT * moved
            X[i, :, cols] = v.astype(BF16)
            sq = jnp.sum(jnp.square(v).reshape(BLOCK // 8, 8, HALF), axis=0)
            acc3[...] += sq[:, :128] + sq[:, 128:256] + sq[:, 256:384] + sq[:, 384:]
        return carry

    lax.fori_loop(0, GROUPS, direction, 0)
    new_own = pltpu.make_async_copy(buf.at[:, mine_rows], new_mom.at[c], ns.at[0])
    new_sib = remote(buf.at[:, other_rows], new_mom.at[c], ns.at[1], ns.at[2], in_column(0, 1))

    def part4(ref, r, i):
        return ref.at[pl.ds(pl.multiple_of((4 * r + i) * 4 * PART, 16), 4 * PART)]

    def part1(ref, r, i, j):
        return ref.at[pl.ds(pl.multiple_of((16 * r + 4 * i + j) * PART, 16), PART)]

    def first_copy(r, which):
        d = sign(r)
        pos, dev = along(r, True, -d if which == 1 else d)
        src = cbg.at[r] if which == 2 else part4(packed, r, wrap(pos + (2, -d)[which]))
        return remote(src, rs1.at[r, which], g1s.at[r, which], g1r.at[r, which], dev)

    def second_copy(r, step):
        pos, dev = along(r, False, step)
        src = midg.at[r, pl.ds(pl.multiple_of(wrap(pos + step) * PART, 16), PART)]
        return remote(src, rs2.at[r, step - 1], g2s.at[r, step - 1], g2r.at[r, step - 1], dev)

    def third_copy(r, step):
        pos1, _ = along(r, True, 1)
        pos2, dev = along(r, False, step)
        return remote(out2.at[r], part1(full, r, pos1, pos2), g3s.at[r, step - 1], g3r.at[r, step - 1], dev)

    def fourth_copy(r, which):
        d = sign(r)
        pos, dev = along(r, True, -d if which == 1 else d)
        ref = part4(full, r, wrap(pos - d) if which == 2 else pos)
        return remote(ref, ref, g4s.at[r, which], g4r.at[r, which], dev)

    ROUTES = (0, 1, 2, 3)
    STEPS = (2, 1, 3)
    flat = X[...].reshape(GROUPS * BLOCK, FF)
    at = 0
    for i in range(4):
        left = flat[:, i * PANEL:(i + 1) * PANEL]
        panel = lax.dot_general(left, flat[:, i * PANEL:], (((0,), (0,)), ((), ())),
                                preferred_element_type=F32).astype(BF16)
        for j in range(2 * (4 - i)):
            packed[at:at + PANEL] = panel[:, j * LANES:(j + 1) * LANES]
            at += PANEL
        first_copy(i, 0).start()
        first_copy(i, 1).start()
    squares = spread_plane(acc3, plane2, ps2, pr2)
    new_own.start()
    new_sib.start()
    for r in ROUTES:
        first_copy(r, 0).wait_recv()
        pos, _ = along(r, True, 1)
        mine = part4(packed, r, wrap(pos + sign(r)))
        cbg[r] = (mine[...].astype(F32) + rs1[r, 0].astype(F32)).astype(BF16)
        first_copy(r, 2).start()
    for r in ROUTES:
        first_copy(r, 1).wait_recv()
        first_copy(r, 2).wait_recv()
        pos, _ = along(r, True, 1)
        mine = part4(packed, r, pos)
        midg[r] = (mine[...].astype(F32) + (rs1[r, 1].astype(F32) + rs1[r, 2].astype(F32))).astype(BF16)
        for s in STEPS:
            second_copy(r, s).start()
    for r in ROUTES:
        for s in STEPS:
            second_copy(r, s).wait_recv()
        pos1, _ = along(r, True, 1)
        pos2, _ = along(r, False, 1)
        v = midg[r, pl.ds(pl.multiple_of(pos2 * PART, 16), PART)].astype(F32) + rs2[r, 0].astype(F32)
        v = (v + (rs2[r, 1].astype(F32) + rs2[r, 2].astype(F32))).astype(BF16)
        out2[r] = v
        for s in STEPS:
            third_copy(r, s).start()
        part1(full, r, pos1, pos2)[...] = v
    acc4[...] = total_of(squares, plane2, 16)
    spread = spread_column(acc4, sq_in, qs, qr)
    inv = 1.0 / (jnp.sqrt(whole_sum(acc4[...])) + NORM_EPS)
    for r in ROUTES:
        for s in STEPS:
            third_copy(r, s).wait_recv()
        fourth_copy(r, 0).start()
        fourth_copy(r, 1).start()
    for r in ROUTES:
        fourth_copy(r, 0).wait_recv()
        fourth_copy(r, 2).start()
    for r in ROUTES:
        fourth_copy(r, 1).wait_recv()
        fourth_copy(r, 2).wait_recv()
    at = 0
    for i in range(4):
        for j in range(2 * i, 8):
            block = full[at:at + PANEL]
            G[i * PANEL:(i + 1) * PANEL, j * LANES:(j + 1) * LANES] = block
            if j >= 2 * (i + 1):
                G[j * LANES:(j + 1) * LANES, i * PANEL:(i + 1) * PANEL] = block.T
            at += PANEL

    def product(lhs, rhs, out, finish):
        for i in range(4):
            low, high = i * PANEL, (i + 1) * PANEL
            v = jnp.dot(lhs[low:high], rhs[:, low:], preferred_element_type=F32)
            v = finish(v, slice(low, high), slice(low, FF)).astype(BF16)
            out[low:high, low:] = v
            for j in range(i + 1, 4):
                out[j * PANEL:(j + 1) * PANEL, low:high] = v[:, (j - i) * PANEL:(j - i + 1) * PANEL].T

    def polynomial(src, q, t, out, scale):
        b_s = COEF_B * scale
        c_s = COEF_C * scale * scale
        product(src, src, q, lambda v, i, j: b_s * src[i, j].astype(F32) + c_s * v)
        product(src, q, t, lambda v, i, j: scale * (COEF_A * src[i, j].astype(F32) + v))
        product(t, q, out, lambda v, i, j: COEF_A * t[i, j].astype(F32) + v)

    def advance(src, rhs, scale, dst):
        v = src[...].reshape(GROUPS * BLOCK, FF)
        w = scale * (COEF_A * v.astype(F32) + jnp.dot(v, rhs[...], preferred_element_type=F32))
        dst[...] = w.astype(BF16).reshape(GROUPS, BLOCK, FF)

    polynomial(G, A, B, T, inv * inv)
    advance(X, A, inv, X2)
    polynomial(T, A, B, G, 1.0)
    advance(X2, A, 1.0, X)

    def return_copy(dz, dc):
        j = 2 * dz + dc
        src = back.at[wrap(e + dz), lax.rem(c + dc, 2)]
        if j == 0:
            return pltpu.make_async_copy(src, ret.at[e, c], bs.at[0])
        return remote(src, ret.at[e, c], bs.at[j], br.at[j], in_column(dz, dc))

    for pair in ((2, 1), (3, 0)):
        v = jnp.concatenate([X[wrap(e + dz)] for dz in pair], axis=0)
        w = jnp.dot(v, G[...], preferred_element_type=F32).astype(BF16)
        z = jnp.dot(w, G[...], preferred_element_type=F32)
        z = (COEF_A * v.astype(F32) + COEF_B * w.astype(F32) + COEF_C * z).astype(BF16)
        for n, dz in enumerate(pair):
            for h in range(2):
                for k in range(2):
                    top = n * BLOCK + h * ROWS
                    back[wrap(e + dz), h, k * ROWS:(k + 1) * ROWS] = z[top:top + ROWS, k * HALF:(k + 1) * HALF]
            for dc in range(2):
                return_copy(dz, dc).start()

    for copy in spread:
        copy.wait_recv()
    lane = lax.broadcasted_iota(jnp.int32, (8, LANES), 1)
    mean_sq = jnp.zeros((8, LANES), F32)
    for slot in range(GROUPS * SLOTS):
        v = whole_sum(sq_in[slot]) / float(D * FF)
        for m in range(MATS):
            mean_sq = mean_sq + jnp.where(lane == m, mask(m, slot) * v, 0.0)
    rms_out[...] = jnp.sqrt(mean_sq)
    for k in range(CHUNKS):
        for m in range(MATS):
            sib_copy(k, m).wait_send()
            for which in range(3):
                copy1(k, m, which).wait_send()
                if k < LAST:
                    copy2(k, m, which).wait_send()
                else:
                    copy2_last(m, which).wait_send()
        for dz, dc in COLUMN:
            z_copy(k, dz, dc).wait_send()
    for r in ROUTES:
        for which in range(3):
            first_copy(r, which).wait_send()
            second_copy(r, which + 1).wait_send()
            third_copy(r, which + 1).wait_send()
            fourth_copy(r, which).wait_send()
    for copy in first + second + squares + spread:
        copy.wait_send()
    mom_sib.wait_send()
    new_own.wait()
    new_sib.wait()
    return_copy(0, 0).wait()
    for dz, dc in COLUMN:
        return_copy(dz, dc).wait()
    for m in range(MATS):
        v = mask(m, 0) * ret[0, 0].astype(F32)
        for slot in range(1, GROUPS * SLOTS):
            v = v + mask(m, slot) * ret[slot // SLOTS, slot % SLOTS].astype(F32)
        rows_out[m, :, :HALF] = v[:ROWS].astype(BF16)
        rows_out[m, :, HALF:] = v[ROWS:].astype(BF16)


ANY = pl.BlockSpec(memory_space=pl.ANY)
VMEM = pl.BlockSpec(memory_space=pltpu.VMEM)
SMEM = pl.BlockSpec(memory_space=pltpu.SMEM)
DMA = pltpu.SemaphoreType.DMA


def per_device(grad_terms, momentum, weights, owner_list):
    small = (CHUNKS, MATS, BLOCK, LANES)
    large = (CHUNKS, MATS, SIDE, BLOCK, LANES)
    whole = (CHUNKS, MATS, SIDE, SIDE, BLOCK, LANES)
    tile = pltpu.VMEM((8, LANES), F32)
    square = pltpu.VMEM((FF, FF), BF16)
    new_mom, rows, rms = pl.pallas_call(
        muon_kernel,
        name="muon",
        out_shape=(
            jax.ShapeDtypeStruct((SLOTS, GROUPS, ROWS, FF), F32),
            jax.ShapeDtypeStruct((MATS, ROWS, FF), BF16),
            jax.ShapeDtypeStruct((8, LANES), F32),
        ),
        in_specs=[SMEM, ANY, ANY],
        out_specs=(ANY, VMEM, VMEM),
        scratch_shapes=[
            pltpu.VMEM(whole, BF16), pltpu.VMEM(whole, BF16),
            pltpu.VMEM(large, BF16), pltpu.VMEM(large, BF16), pltpu.VMEM(large, BF16), pltpu.VMEM(large, BF16),
            pltpu.VMEM(small, BF16), pltpu.VMEM(small, BF16), pltpu.VMEM(small, BF16),
            pltpu.VMEM((MATS, BLOCK, LANES), F32),
            pltpu.VMEM((CHUNKS, 8, BLOCK, LANES), BF16),
            pltpu.VMEM((GROUPS, 2, BLOCK, HALF), BF16),
            pltpu.VMEM((GROUPS, BLOCK, FF), F32),
            pltpu.VMEM((GROUPS, BLOCK, FF), BF16),
            pltpu.VMEM((64 * PART, LANES), BF16), pltpu.VMEM((64 * PART, LANES), BF16),
            pltpu.VMEM((4, 3, 4 * PART, LANES), BF16),
            pltpu.VMEM((4, 4 * PART, LANES), BF16),
            pltpu.VMEM((4, 4 * PART, LANES), BF16),
            pltpu.VMEM((4, 3, PART, LANES), BF16),
            pltpu.VMEM((4, PART, LANES), BF16),
            square, square, square, square,
            pltpu.VMEM((GROUPS, BLOCK, FF), BF16),
            pltpu.VMEM((GROUPS, 2, BLOCK, HALF), BF16), pltpu.VMEM((GROUPS, SLOTS, BLOCK, HALF), BF16),
            tile, tile, tile, tile,
            pltpu.VMEM((8, 8, LANES), F32), pltpu.VMEM((16, 8, LANES), F32), pltpu.VMEM((16, 8, LANES), F32),
            pltpu.VMEM((8, 8, LANES), F32),
            DMA((CHUNKS, MATS)), DMA((CHUNKS, MATS)), DMA((CHUNKS, MATS)),
            DMA((CHUNKS, MATS, 3)), DMA((CHUNKS, MATS, 3)), DMA((CHUNKS, MATS, 3)), DMA((CHUNKS, MATS, 3)),
            DMA((CHUNKS, 8)), DMA((CHUNKS, 8)), DMA((CHUNKS,)), DMA((3,)),
            DMA((7,)), DMA((7,)), DMA((15,)), DMA((15,)), DMA((3,)),
            DMA((4, 3)), DMA((4, 3)), DMA((4, 3)), DMA((4, 3)), DMA((4, 3)), DMA((4, 3)), DMA((4, 3)), DMA((4, 3)),
            DMA((15,)), DMA((15,)), DMA((7,)), DMA((7,)), DMA((8,)), DMA((8,)),
        ],
        compiler_params=pltpu.CompilerParams(collective_id=0, has_side_effects=True, vmem_limit_bytes=60 << 20),
    )(owner_list, grad_terms.reshape(MATS, SIDE, SIDE, BLOCK, FF), momentum[0])

    rows = rows.astype(F32)
    scale_rms = 0.2 * math.sqrt(max(D, FF))
    update = (scale_rms * rows).astype(BF16)
    new_weights = weights * (1.0 - LEARN * DECAY) - LEARN * scale_rms * rows
    return (new_weights, update, new_mom[None], rms[0, :MATS])


def solution(mesh):
    placed = (
        P("dp", None, "expert", None),
        P("expert", None, None, "dp", None),
        P(None, ("expert", "dp"), None),
        P(),
    )
    return jax.shard_map(
        per_device,
        mesh=mesh,
        in_specs=placed,
        out_specs=(
            P(None, ("expert", "dp"), None),
            P(None, ("expert", "dp"), None),
            P("expert", None, None, "dp", None),
            P(),
        ),
        check_vma=False,
    )
```

```python
import math

import jax
import jax.numpy as jnp
from jax import lax
from jax.experimental import pallas as pl
from jax.experimental.pallas import tpu as pltpu
from jax.sharding import PartitionSpec as P

D = 7168
FF = 1024
MATS = 4
SLOTS = 2
GROUPS = 4
SIDE = 4
BLOCK = 112
ROWS = 56
HALF = FF // 2
LANES = 128
STRIP = 16
CHUNKS = BLOCK // STRIP
LAST = CHUNKS - 1
PANEL = 256
PART = 80

MOMENT = 0.95
CLIP_RMS = 1.0
LEARN = 0.1
DECAY = 0.1
COEF_A = 3.4445
COEF_B = -4.775
COEF_C = 2.0315
NORM_EPS = 1e-07
MEAN_EPS = 1e-06
F32 = jnp.float32
BF16 = jnp.bfloat16

COLUMN = ((2, 0), (2, 1), (1, 0), (1, 1), (3, 0), (3, 1), (0, 1))
PLANE = tuple((dx, dy) for dx in range(4) for dy in range(4) if dx + dy)


def wrap(v):
    return lax.rem(v + 4, 4)


def remote(src, dst, send, recv, device):
    return pltpu.make_async_remote_copy(src_ref=src, dst_ref=dst, send_sem=send, recv_sem=recv, device_id=device)


def whole_sum(v):
    return jnp.sum(jnp.sum(v, axis=0, keepdims=True), axis=1, keepdims=True)


def sign(m):
    return 1 if m % 2 else -1


def muon_kernel(owners, g, mom, new_mom, rows_out, rms_out,
                own, sib, tr1, dr1, cb1, mid, tr2, dr2, cb2, grad, zin, zout, zin2, momv, mout, min_, mall, buf, X, Xc, X2,
                packed, full, rs1, cbg, midg, rs2, out2, G, A, B, T, back, ret, acc, acc2, acc3, acc4,
                column, plane, plane2, sq_in,
                own_s, sib_s, sib_r, s1, r1, s2, r2, zs, zr, zl, ms, m1s, m1r, m2s, cs, cr, ps, pr, ns, g1s, g1r, g2s,
                g2r, g3s, g3r, g4s, g4r, g5s, g5r, ps2, pr2, qs, qr, z2s, z2r, bs, br, bl):
    e = lax.axis_index("expert")
    p = lax.axis_index("dp")
    x, y, c = p // 8, (p // 2) % 4, p % 2
    other = 1 - c

    def target(te, tx, ty, tc):
        return {"expert": te, "dp": tx * 8 + ty * 2 + tc}

    def in_column(dz, dc):
        return target(wrap(e + dz), x, y, lax.rem(c + dc, 2))

    def in_plane(dx, dy):
        return target(e, wrap(x + dx), wrap(y + dy), c)

    places = []
    for m in range(MATS):
        number = jnp.int32(0)
        for m2 in range(m):
            number = number + jnp.where(owners[m2] == owners[m], 1, 0)
        places.append(owners[m] * SLOTS + number)

    def mask(m, slot):
        return jnp.where(places[m] == slot, 1.0, 0.0).astype(F32)

    def strip(k):
        return pl.ds(pl.multiple_of(k * STRIP, STRIP), STRIP)

    def own_copy(k, m):
        cols = pl.ds(pl.multiple_of(c * HALF, HALF), HALF)
        return pltpu.make_async_copy(g.at[m, :, :, strip(k), cols], own.at[m, :, :, strip(k)], own_s.at[k, m])

    def sib_copy(k, m):
        cols = pl.ds(pl.multiple_of(other * HALF, HALF), HALF)
        return remote(g.at[m, :, :, strip(k), cols], sib.at[m, :, :, strip(k)], sib_s.at[k, m], sib_r.at[k, m],
                      in_column(0, 1))

    def along(m, first, step):
        on_x = (m < 2) == first
        return (x, in_plane(step, 0)) if on_x else (y, in_plane(0, step))

    def group(ref, k, m, i):
        return ref.at[m, i, :, strip(k)] if m < 2 else ref.at[m, :, i, strip(k)]

    def copy1(k, m, which):
        d = sign(m)
        pos, dev = along(m, True, -d if which == 1 else d)
        i = wrap(pos + (2, -d, d)[which])
        return remote(group(own, k, m, i), (tr1, dr1, cb1)[which].at[k, m], s1.at[k, m, which], r1.at[k, m, which], dev)

    def copy2(k, m, which):
        d = sign(m)
        pos, dev = along(m, False, -d if which == 1 else d)
        i = wrap(pos + (2, -d, d)[which])
        return remote(mid.at[k, m, i], (tr2, dr2, cb2)[which].at[k, m], s2.at[k, m, which], r2.at[k, m, which], dev)

    def copy2_last(m, which):
        step = (2, 1, 3)[which]
        pos, dev = along(m, False, step)
        return remote(mid.at[LAST, m, wrap(pos + step)], (tr2, dr2, cb2)[which].at[LAST, m], s2.at[LAST, m, which],
                      r2.at[LAST, m, which], dev)

    def z_copy(k, dz, dc):
        j = 2 * dz + dc
        src, dst = grad.at[wrap(e + dz), strip(k)], zin.at[e, c, strip(k)]
        if j == 0:
            return pltpu.make_async_copy(src, dst, zl.at[k])
        return remote(src, dst, zs.at[k, j], zr.at[k, j], in_column(dz, dc))

    mine_rows = pl.ds(pl.multiple_of(ROWS * c, 8), ROWS)
    other_rows = pl.ds(pl.multiple_of(ROWS * other, 8), ROWS)
    mom_load = pltpu.make_async_copy(mom, momv, ms.at[0])
    mom_own = pltpu.make_async_copy(mom.at[c], buf.at[:, mine_rows], ms.at[1])
    mom_sib = remote(mom.at[other], buf.at[:, mine_rows], ms.at[2], ms.at[3], in_column(0, 1))

    def mom_copy(dz):
        return remote(mout.at[dz], min_.at[e], m1s.at[dz], m1r.at[dz], in_column(dz, 0))

    mom_pass = remote(mall.at[c], mall.at[c], m2s.at[0], m2s.at[1], in_column(0, 1))

    for k in range(CHUNKS):
        for m in range(MATS):
            own_copy(k, m).start()
        if k == 0:
            mom_load.start()
    mom_own.start()
    barrier = pltpu.get_barrier_semaphore()
    for dz, dc in COLUMN:
        pl.semaphore_signal(barrier, inc=1, device_id=in_column(dz, dc))
    for dx, dy in PLANE:
        pl.semaphore_signal(barrier, inc=1, device_id=in_plane(dx, dy))
    pl.semaphore_wait(barrier, len(COLUMN) + len(PLANE))
    for k in range(CHUNKS):
        for m in range(MATS):
            sib_copy(k, m).start()
    acc[...] = jnp.zeros_like(acc)
    acc3[...] = jnp.zeros_like(acc3)

    def pair_sum(k, m, i):
        to, more = group(own, k, m, i), group(sib, k, m, i)
        for j in range(SIDE):
            to[j] = (to[j].astype(F32) + more[j].astype(F32)).astype(BF16)

    def transit(k):
        for m in range(MATS):
            own_copy(k, m).wait()
            sib_copy(k, m).wait_recv()
            pos, _ = along(m, True, 1)
            pair_sum(k, m, wrap(pos + 2))
            copy1(k, m, 0).start()

    def combine(k):
        for m in range(MATS):
            copy1(k, m, 0).wait_recv()
            pos, _ = along(m, True, 1)
            i = wrap(pos + sign(m))
            to, more, came = group(own, k, m, i), group(sib, k, m, i), tr1.at[k, m]
            for j in range(SIDE):
                to[j] = (to[j].astype(F32) + more[j].astype(F32) + came[j].astype(F32)).astype(BF16)
            copy1(k, m, 2).start()

    def direct(k):
        for m in range(MATS):
            pos, _ = along(m, True, 1)
            pair_sum(k, m, wrap(pos - sign(m)))
            copy1(k, m, 1).start()

    def turn(k):
        for m in range(MATS):
            copy1(k, m, 1).wait_recv()
            copy1(k, m, 2).wait_recv()
            pos, _ = along(m, True, 1)
            to, more, came, came2 = group(own, k, m, pos), group(sib, k, m, pos), dr1.at[k, m], cb1.at[k, m]
            for j in range(SIDE):
                v = (to[j].astype(F32) + more[j].astype(F32)) + (came[j].astype(F32) + came2[j].astype(F32))
                mid[k, m, j] = v.astype(BF16)

            @pl.when(k < LAST)
            def _():
                copy2(k, m, 0).start()
                copy2(k, m, 1).start()

            @pl.when(k == LAST)
            def _():
                for which in range(3):
                    copy2_last(m, which).start()

    def combine2(k):
        for m in range(MATS):
            copy2(k, m, 0).wait_recv()
            pos, _ = along(m, False, 1)
            i = wrap(pos + sign(m))
            mid[k, m, i] = (mid[k, m, i].astype(F32) + tr2[k, m].astype(F32)).astype(BF16)
            copy2(k, m, 2).start()

    def collect(k, m, v):
        v = v.astype(BF16)
        grad[m, strip(k)] = v
        v = jnp.square(v.astype(F32))
        v = v[:8] + v[8:]
        acc[...] += v[:, :128] + v[:, 128:256] + v[:, 256:384] + v[:, 384:]

    def send_strips(k):
        for dz in (2, 1, 3, 0):
            for dc in range(2):
                z_copy(k, dz, dc).start()

    def finish_sum(k):
        for m in range(MATS):
            copy2(k, m, 1).wait_recv()
            copy2(k, m, 2).wait_recv()
            pos, _ = along(m, False, 1)
            collect(k, m, mid[k, m, pos].astype(F32) + (dr2[k, m].astype(F32) + cb2[k, m].astype(F32)))
        send_strips(k)

    def mom_send(k):
        mom_load.wait()
        for dz in (2, 1, 3, 0):
            t = wrap(e + dz)
            first_is = jnp.float32(0)
            second_is = jnp.float32(0)
            for m in range(MATS):
                here = jnp.where(t == m, 1.0, 0.0).astype(F32)
                first_is = first_is + here * mask(m, 2 * e)
                second_is = second_is + here * mask(m, 2 * e + 1)
            for i in range(GROUPS):
                for h in range(2):
                    cols = slice(h * HALF, (h + 1) * HALF)
                    v = first_is * momv[0, i, :, cols] + second_is * momv[1, i, :, cols]
                    mout[dz, i, h * ROWS:(h + 1) * ROWS] = v.astype(BF16)
            if dz:
                mom_copy(dz).start()
        mom_sib.start()

    def mom_sum(k):
        for dz in (1, 2, 3):
            mom_copy(dz).wait_recv()
        for i in range(GROUPS):
            v = mout[0, i].astype(F32)
            for dz in (1, 2, 3):
                v = v + min_[wrap(e + dz), i].astype(F32)
            mall[c, i] = v.astype(BF16)
        mom_pass.start()

    stages = ((transit, 0, CHUNKS), (combine, 1, CHUNKS), (direct, 2, CHUNKS), (turn, 3, CHUNKS),
              (combine2, 4, LAST), (finish_sum, 5, LAST), (mom_send, 1, 1), (mom_sum, LAST + 2, 1))

    def step(t, carry):
        for stage, lag, chunks in stages:
            @pl.when((t >= lag) & (t < chunks + lag))
            def _():
                stage(t - lag)
        return carry

    lax.fori_loop(0, LAST + 5, step, 0)
    for m in range(MATS):
        for which in range(3):
            copy2_last(m, which).wait_recv()
        pos, _ = along(m, False, 1)
        v = mid[LAST, m, pos].astype(F32) + tr2[LAST, m].astype(F32)
        collect(LAST, m, v + (dr2[LAST, m].astype(F32) + cb2[LAST, m].astype(F32)))

    me_column = 2 * e + c
    me_plane = 4 * x + y

    def spread_column(src, dst, send, recv):
        copies = [remote(src, dst.at[me_column], send.at[i], recv.at[i], in_column(*d)) for i, d in enumerate(COLUMN)]
        for copy in copies:
            copy.start()
        dst[me_column] = src[...]
        return copies

    def spread_plane(src, dst, send, recv):
        copies = [remote(src, dst.at[me_plane], send.at[i], recv.at[i], in_plane(*d)) for i, d in enumerate(PLANE)]
        for copy in copies:
            copy.start()
        dst[me_plane] = src[...]
        return copies

    def total_of(copies, ref, count):
        for copy in copies:
            copy.wait_recv()
        v = ref[0]
        for j in range(1, count):
            v = v + ref[j]
        return v

    first = spread_column(acc, column, cs, cr)
    send_strips(LAST)
    acc2[...] = total_of(first, column, 8)
    second = spread_plane(acc2, plane, ps, pr)
    mom_pass.wait_recv()
    for k in range(CHUNKS):
        for dz in range(4):
            for dc in range(2):
                if dz + dc:
                    z_copy(k, dz, dc).wait_recv()
                else:
                    z_copy(k, 0, 0).wait()
    mean = whole_sum(total_of(second, plane, 16)) / float(MATS * D * FF)
    factor = jnp.minimum(1.0, CLIP_RMS / jnp.sqrt(mean + MEAN_EPS))

    def direction(i, carry):
        parts = [mall[k, i].astype(F32) for k in range(2)]
        for h in range(2):
            kept = jnp.concatenate([v[h * ROWS:(h + 1) * ROWS] for v in parts], axis=0)
            v = factor * zin[i, h].astype(F32)
            v = v + MOMENT * (MOMENT * kept + v)
            X[i, :, h * HALF:(h + 1) * HALF] = v.astype(BF16)
            sq = jnp.sum(jnp.square(v).reshape(BLOCK // 8, 8, HALF), axis=0)
            acc3[...] += sq[:, :128] + sq[:, 128:256] + sq[:, 256:384] + sq[:, 384:]
        return carry

    lax.fori_loop(0, GROUPS, direction, 0)

    d = 2 * c - 1

    def part4(ref, q, i):
        return ref.at[pl.ds(pl.multiple_of((4 * q + i) * 4 * PART, 16), 4 * PART)]

    def part1(ref, q, i, j):
        return ref.at[pl.ds(pl.multiple_of((16 * q + 4 * i + j) * PART, 16), PART)]

    def on(q, first, step):
        return (x, in_plane(step, 0)) if (q == 0) == first else (y, in_plane(0, step))

    def first_copy(q, which):
        pos, dev = on(q, True, -d if which == 1 else d)
        src = cbg.at[q] if which == 2 else part4(packed, q, wrap(pos + (2, -d)[which]))
        return remote(src, rs1.at[q, which], g1s.at[q, which], g1r.at[q, which], dev)

    def second_copy(q, step):
        pos, dev = on(q, False, step)
        src = midg.at[q, pl.ds(pl.multiple_of(wrap(pos + step) * PART, 16), PART)]
        return remote(src, rs2.at[q, step - 1], g2s.at[q, step - 1], g2r.at[q, step - 1], dev)

    def third_copy(q, step):
        pos1, _ = on(q, True, 1)
        pos2, dev = on(q, False, step)
        return remote(out2.at[q], part1(full.at[c], q, pos1, pos2), g3s.at[q, step - 1], g3r.at[q, step - 1], dev)

    def fourth_copy(q, which):
        pos, dev = on(q, True, -d if which == 1 else d)
        ref = part4(full.at[c], q, wrap(pos - d) if which == 2 else pos)
        return remote(ref, ref, g4s.at[q, which], g4r.at[q, which], dev)

    def pair_copy(q, n):
        pos, _ = on(q, True, 1)
        ref = part4(full.at[c], q, wrap(pos + n))
        return remote(ref, ref, g5s.at[q, n], g5r.at[q, n], in_column(0, 1))

    STEPS = (2, 1, 3)
    for j in range(4):
        cols = pl.ds(pl.multiple_of((2 * j + c) * LANES, LANES), LANES)
        Xc[:, j * LANES:(j + 1) * LANES] = X[:, :, cols].reshape(GROUPS * BLOCK, LANES)
    at = 0
    for i in range(4):
        left = X[:, :, i * PANEL:(i + 1) * PANEL].reshape(GROUPS * BLOCK, PANEL)
        panel = lax.dot_general(left, Xc[:, i * LANES:], (((0,), (0,)), ((), ())),
                                preferred_element_type=F32).astype(BF16)
        for j in range(4 - i):
            packed[at:at + PANEL] = panel[:, j * LANES:(j + 1) * LANES]
            at += PANEL
        if i in (1, 3):
            first_copy(i // 2, 0).start()
            first_copy(i // 2, 1).start()
    squares = spread_plane(acc3, plane2, ps2, pr2)
    mom_own.wait()
    mom_sib.wait_recv()
    for q in range(2):
        first_copy(q, 0).wait_recv()
        pos, _ = on(q, True, 1)
        mine = part4(packed, q, wrap(pos + d))
        cbg[q] = (mine[...].astype(F32) + rs1[q, 0].astype(F32)).astype(BF16)
        first_copy(q, 2).start()

    def slot_copy(dz, dc):
        j = 2 * dz + dc
        if j == 0:
            return pltpu.make_async_copy(zout.at[0], zin2.at[e, c], z2s.at[0])
        return remote(zout.at[j], zin2.at[e, c], z2s.at[j], z2r.at[j], in_column(dz, dc))

    for dz in (2, 1, 3, 0):
        for dc in range(2):
            slot = wrap(e + dz) * SLOTS + lax.rem(c + dc, 2)
            v = mask(0, slot) * grad[0].astype(F32)
            for m in range(1, MATS):
                v = v + mask(m, slot) * grad[m].astype(F32)
            zout[2 * dz + dc] = v.astype(BF16)
            slot_copy(dz, dc).start()

    for q in range(2):
        first_copy(q, 1).wait_recv()
        first_copy(q, 2).wait_recv()
        pos, _ = on(q, True, 1)
        mine = part4(packed, q, pos)
        midg[q] = (mine[...].astype(F32) + (rs1[q, 1].astype(F32) + rs1[q, 2].astype(F32))).astype(BF16)
        for s in STEPS:
            second_copy(q, s).start()
    for q in range(2):
        for s in STEPS:
            second_copy(q, s).wait_recv()
        pos1, _ = on(q, True, 1)
        pos2, _ = on(q, False, 1)
        v = midg[q, pl.ds(pl.multiple_of(pos2 * PART, 16), PART)].astype(F32) + rs2[q, 0].astype(F32)
        v = (v + (rs2[q, 1].astype(F32) + rs2[q, 2].astype(F32))).astype(BF16)
        out2[q] = v
        for s in STEPS:
            third_copy(q, s).start()
        part1(full.at[c], q, pos1, pos2)[...] = v
    acc4[...] = total_of(squares, plane2, 16)
    spread = spread_column(acc4, sq_in, qs, qr)
    inv = 1.0 / (jnp.sqrt(whole_sum(acc4[...])) + NORM_EPS)
    for q in range(2):
        for s in STEPS:
            third_copy(q, s).wait_recv()
        fourth_copy(q, 0).start()
        fourth_copy(q, 1).start()
        pair_copy(q, 0).start()
    for q in range(2):
        fourth_copy(q, 0).wait_recv()
        fourth_copy(q, 2).start()
    for q in range(2):
        fourth_copy(q, 1).wait_recv()
        pair_copy(q, 1).start()
        pair_copy(q, 3).start()
    for q in range(2):
        fourth_copy(q, 2).wait_recv()
        pair_copy(q, 2).start()
    for q in range(2):
        for n in range(4):
            pair_copy(q, n).wait_recv()
    for k in range(2):
        at = 0
        for i in range(4):
            for n in range(4 - i):
                j = 2 * (i + n) + k
                block = full[k, at:at + PANEL]
                G[i * PANEL:(i + 1) * PANEL, j * LANES:(j + 1) * LANES] = block
                if n:
                    G[j * LANES:(j + 1) * LANES, i * PANEL:(i + 1) * PANEL] = block.T
                at += PANEL

    def product(lhs, rhs, out, finish):
        for i in range(4):
            low, high = i * PANEL, (i + 1) * PANEL
            v = jnp.dot(lhs[low:high], rhs[:, low:], preferred_element_type=F32)
            v = finish(v, slice(low, high), slice(low, FF)).astype(BF16)
            out[low:high, low:] = v
            for j in range(i + 1, 4):
                out[j * PANEL:(j + 1) * PANEL, low:high] = v[:, (j - i) * PANEL:(j - i + 1) * PANEL].T

    def polynomial(src, q, t, out, scale):
        b_s = COEF_B * scale
        c_s = COEF_C * scale * scale
        product(src, src, q, lambda v, i, j: b_s * src[i, j].astype(F32) + c_s * v)
        product(src, q, t, lambda v, i, j: scale * (COEF_A * src[i, j].astype(F32) + v))
        product(t, q, out, lambda v, i, j: COEF_A * t[i, j].astype(F32) + v)

    def advance(src, rhs, scale):
        v = src[...]
        w = scale * (COEF_A * v.astype(F32) + jnp.dot(v, rhs[...], preferred_element_type=F32))
        return w.astype(BF16)

    for n in range(2):
        X2[0, n * BLOCK:(n + 1) * BLOCK] = X[2 * c + n]
    polynomial(G, A, B, T, inv * inv)
    X2[1] = advance(X2.at[0], A, inv)
    polynomial(T, A, B, G, 1.0)
    X2[0] = advance(X2.at[1], A, 1.0)
    v = X2[0]
    w = jnp.dot(v, G[...], preferred_element_type=F32).astype(BF16)
    z = jnp.dot(w, G[...], preferred_element_type=F32)
    z = (COEF_A * v.astype(F32) + COEF_B * w.astype(F32) + COEF_C * z).astype(BF16)

    def return_copy(n, dc):
        src = back.at[n, lax.rem(c + dc, 2)]
        return remote(src, ret.at[e], bs.at[n, dc], br.at[e], target(2 * c + n, x, y, lax.rem(c + dc, 2)))

    def return_local(n):
        return pltpu.make_async_copy(back.at[n, c], ret.at[e], bl.at[0])

    def return_in(m):
        return remote(back.at[0, 0], ret.at[m], bs.at[0, 0], br.at[m], in_column(0, 1))

    for n in range(2):
        for h in range(2):
            for k in range(2):
                top = n * BLOCK + h * ROWS
                back[n, h, k * ROWS:(k + 1) * ROWS] = z[top:top + ROWS, k * HALF:(k + 1) * HALF]
        return_copy(n, 1).start()

        @pl.when(2 * c + n != e)
        def _():
            return_copy(n, 0).start()

        @pl.when(2 * c + n == e)
        def _():
            return_local(n).start()

    for dz in range(4):
        for dc in range(2):
            if dz + dc:
                slot_copy(dz, dc).wait_recv()
            else:
                slot_copy(0, 0).wait()

    def momentum(i, carry):
        for h in range(2):
            cols = pl.ds(h * HALF, HALF)
            buf[i, :, cols] = MOMENT * buf[i, :, cols] + factor * zin2[i, h].astype(F32)
        return carry

    lax.fori_loop(0, GROUPS, momentum, 0)
    new_own = pltpu.make_async_copy(buf.at[:, mine_rows], new_mom.at[c], ns.at[0])
    new_sib = remote(buf.at[:, other_rows], new_mom.at[c], ns.at[1], ns.at[2], in_column(0, 1))
    new_sib.start()
    new_own.start()

    for copy in spread:
        copy.wait_recv()
    lane = lax.broadcasted_iota(jnp.int32, (8, LANES), 1)
    mean_sq = jnp.zeros((8, LANES), F32)
    for m in range(MATS):
        mean_sq = mean_sq + jnp.where(lane == m, whole_sum(sq_in[2 * m]) / float(D * FF), 0.0)
    rms_out[...] = jnp.sqrt(mean_sq)

    def drain(k, carry):
        for m in range(MATS):
            sib_copy(k, m).wait_send()
            for which in range(3):
                copy1(k, m, which).wait_send()

                @pl.when(k < LAST)
                def _():
                    copy2(k, m, which).wait_send()

                @pl.when(k == LAST)
                def _():
                    copy2_last(m, which).wait_send()
        for dz, dc in COLUMN:
            z_copy(k, dz, dc).wait_send()
        return carry

    lax.fori_loop(0, CHUNKS, drain, 0)
    for dz in (1, 2, 3):
        mom_copy(dz).wait_send()
    mom_pass.wait_send()
    mom_sib.wait_send()
    for q in range(2):
        for n in range(3):
            first_copy(q, n).wait_send()
            second_copy(q, n + 1).wait_send()
            third_copy(q, n + 1).wait_send()
            fourth_copy(q, n).wait_send()
        for n in range(4):
            pair_copy(q, n).wait_send()
    for dz, dc in COLUMN:
        slot_copy(dz, dc).wait_send()
    for copy in first + second + squares + spread:
        copy.wait_send()
    for dz in (0, 1, 3, 2):
        m = wrap(e + dz)
        if dz:
            return_in(m).wait_recv()
        else:
            @pl.when(e // 2 == c)
            def _():
                return_local(0).wait()

            @pl.when(e // 2 != c)
            def _():
                return_in(m).wait_recv()
        v = ret[m].astype(F32)
        rows_out[m, :, :HALF] = v[:ROWS].astype(BF16)
        rows_out[m, :, HALF:] = v[ROWS:].astype(BF16)
    for n in range(2):
        return_copy(n, 1).wait_send()

        @pl.when(2 * c + n != e)
        def _():
            return_copy(n, 0).wait_send()

    new_own.wait()
    new_sib.wait()


ANY = pl.BlockSpec(memory_space=pl.ANY)
VMEM = pl.BlockSpec(memory_space=pltpu.VMEM)
SMEM = pl.BlockSpec(memory_space=pltpu.SMEM)
DMA = pltpu.SemaphoreType.DMA


def per_device(grad_terms, momentum, weights, owner_list):
    small = (CHUNKS, MATS, STRIP, HALF)
    large = (CHUNKS, MATS, SIDE, STRIP, HALF)
    whole = (MATS, SIDE, SIDE, BLOCK, HALF)
    tile = pltpu.VMEM((8, LANES), F32)
    square = pltpu.VMEM((FF, FF), BF16)
    new_mom, rows, rms = pl.pallas_call(
        muon_kernel,
        name="muon",
        out_shape=(
            jax.ShapeDtypeStruct((SLOTS, GROUPS, ROWS, FF), F32),
            jax.ShapeDtypeStruct((MATS, ROWS, FF), BF16),
            jax.ShapeDtypeStruct((8, LANES), F32),
        ),
        in_specs=[SMEM, ANY, ANY],
        out_specs=(ANY, VMEM, VMEM),
        scratch_shapes=[
            pltpu.VMEM(whole, BF16), pltpu.VMEM(whole, BF16),
            pltpu.VMEM(large, BF16), pltpu.VMEM(large, BF16), pltpu.VMEM(large, BF16), pltpu.VMEM(large, BF16),
            pltpu.VMEM(small, BF16), pltpu.VMEM(small, BF16), pltpu.VMEM(small, BF16),
            pltpu.VMEM((MATS, BLOCK, HALF), BF16),
            pltpu.VMEM((GROUPS, 2, BLOCK, HALF), BF16),
            pltpu.VMEM((GROUPS * SLOTS, BLOCK, HALF), BF16),
            pltpu.VMEM((GROUPS, 2, BLOCK, HALF), BF16),
            pltpu.VMEM((SLOTS, GROUPS, ROWS, FF), F32),
            pltpu.VMEM((4, GROUPS, BLOCK, HALF), BF16), pltpu.VMEM((4, GROUPS, BLOCK, HALF), BF16),
            pltpu.VMEM((2, GROUPS, BLOCK, HALF), BF16),
            pltpu.VMEM((GROUPS, BLOCK, FF), F32),
            pltpu.VMEM((GROUPS, BLOCK, FF), BF16),
            pltpu.VMEM((GROUPS * BLOCK, HALF), BF16),
            pltpu.VMEM((2, 2 * BLOCK, FF), BF16),
            pltpu.VMEM((32 * PART, LANES), BF16), pltpu.VMEM((2, 32 * PART, LANES), BF16),
            pltpu.VMEM((2, 3, 4 * PART, LANES), BF16),
            pltpu.VMEM((2, 4 * PART, LANES), BF16),
            pltpu.VMEM((2, 4 * PART, LANES), BF16),
            pltpu.VMEM((2, 3, PART, LANES), BF16),
            pltpu.VMEM((2, PART, LANES), BF16),
            square, square, square, square,
            pltpu.VMEM((2, 2, BLOCK, HALF), BF16), pltpu.VMEM((MATS, BLOCK, HALF), BF16),
            tile, tile, tile, tile,
            pltpu.VMEM((8, 8, LANES), F32), pltpu.VMEM((16, 8, LANES), F32), pltpu.VMEM((16, 8, LANES), F32),
            pltpu.VMEM((8, 8, LANES), F32),
            DMA((CHUNKS, MATS)), DMA((CHUNKS, MATS)), DMA((CHUNKS, MATS)),
            DMA((CHUNKS, MATS, 3)), DMA((CHUNKS, MATS, 3)), DMA((CHUNKS, MATS, 3)), DMA((CHUNKS, MATS, 3)),
            DMA((CHUNKS, 8)), DMA((CHUNKS, 8)), DMA((CHUNKS,)), DMA((4,)), DMA((4,)), DMA((4,)), DMA((2,)),
            DMA((7,)), DMA((7,)), DMA((15,)), DMA((15,)), DMA((3,)),
            DMA((2, 3)), DMA((2, 3)), DMA((2, 3)), DMA((2, 3)), DMA((2, 3)), DMA((2, 3)), DMA((2, 3)), DMA((2, 3)),
            DMA((2, 4)), DMA((2, 4)),
            DMA((15,)), DMA((15,)), DMA((7,)), DMA((7,)), DMA((8,)), DMA((8,)), DMA((2, 2)), DMA((4,)), DMA((1,)),
        ],
        compiler_params=pltpu.CompilerParams(collective_id=0, has_side_effects=True, vmem_limit_bytes=60 << 20),
    )(owner_list, grad_terms.reshape(MATS, SIDE, SIDE, BLOCK, FF), momentum[0])

    rows = rows.astype(F32)
    scale_rms = 0.2 * math.sqrt(max(D, FF))
    update = (scale_rms * rows).astype(BF16)
    new_weights = weights * (1.0 - LEARN * DECAY) - LEARN * scale_rms * rows
    return (new_weights, update, new_mom[None], rms[0, :MATS])


def solution(mesh):
    placed = (
        P("dp", None, "expert", None),
        P("expert", None, None, "dp", None),
        P(None, ("expert", "dp"), None),
        P(),
    )
    return jax.shard_map(
        per_device,
        mesh=mesh,
        in_specs=placed,
        out_specs=(
            P(None, ("expert", "dp"), None),
            P(None, ("expert", "dp"), None),
            P("expert", None, None, "dp", None),
            P(),
        ),
        check_vma=False,
    )
```

```python
import math

import jax
import jax.numpy as jnp
from jax import lax
from jax.experimental import pallas as pl
from jax.experimental.pallas import tpu as pltpu
from jax.sharding import PartitionSpec as P

D = 7168
FF = 1024
MATS = 4
SLOTS = 2
GROUPS = 4
SIDE = 4
BLOCK = 112
ROWS = 56
HALF = FF // 2
LANES = 128
STRIP = 16
CHUNKS = BLOCK // STRIP
LAST = CHUNKS - 1
SHORT = 5
PANEL = 256
PART = 80

MOMENT = 0.95
CLIP_RMS = 1.0
LEARN = 0.1
DECAY = 0.1
COEF_A = 3.4445
COEF_B = -4.775
COEF_C = 2.0315
NORM_EPS = 1e-07
MEAN_EPS = 1e-06
F32 = jnp.float32
BF16 = jnp.bfloat16

COLUMN = ((2, 0), (2, 1), (1, 0), (1, 1), (3, 0), (3, 1), (0, 1))
PLANE = tuple((dx, dy) for dx in range(4) for dy in range(4) if dx + dy)


def wrap(v):
    return lax.rem(v + 4, 4)


def remote(src, dst, send, recv, device):
    return pltpu.make_async_remote_copy(src_ref=src, dst_ref=dst, send_sem=send, recv_sem=recv, device_id=device)


def whole_sum(v):
    return jnp.sum(jnp.sum(v, axis=0, keepdims=True), axis=1, keepdims=True)


def sign(m):
    return 1 if m % 2 else -1


def muon_kernel(owners, g, mom, new_mom, rows_out, rms_out,
                own, sib, tr1, dr1, cb1, mid, tr2, dr2, cb2, grad, zin, zout, zin2, momv, mout, min_, mall, buf, X, Xc, X2,
                packed, full, rs1, midg, rs2, G, A, B, T, back, ret, acc, acc2, acc3, acc4,
                column, plane, plane2, sq_in,
                own_s, sib_s, sib_r, s1, r1, s2, r2, zs, zr, zl, ms, m1s, m1r, m2s, cs, cr, ps, pr, ns, g1s, g1r, g2s,
                g2r, g3s, g3r, g5s, g5r, ps2, pr2, qs, qr, z2s, z2r, bs, br, bl):
    e = lax.axis_index("expert")
    p = lax.axis_index("dp")
    x, y, c = p // 8, (p // 2) % 4, p % 2
    other = 1 - c

    def target(te, tx, ty, tc):
        return {"expert": te, "dp": tx * 8 + ty * 2 + tc}

    def in_column(dz, dc):
        return target(wrap(e + dz), x, y, lax.rem(c + dc, 2))

    def in_plane(dx, dy):
        return target(e, wrap(x + dx), wrap(y + dy), c)

    places = []
    for m in range(MATS):
        number = jnp.int32(0)
        for m2 in range(m):
            number = number + jnp.where(owners[m2] == owners[m], 1, 0)
        places.append(owners[m] * SLOTS + number)

    def mask(m, slot):
        return jnp.where(places[m] == slot, 1.0, 0.0).astype(F32)

    def strip(k):
        return pl.ds(pl.multiple_of(k * STRIP, STRIP), STRIP)

    def own_copy(k, m):
        cols = pl.ds(pl.multiple_of(c * HALF, HALF), HALF)
        return pltpu.make_async_copy(g.at[m, :, :, strip(k), cols], own.at[m, :, :, strip(k)], own_s.at[k, m])

    def sib_copy(k, m):
        cols = pl.ds(pl.multiple_of(other * HALF, HALF), HALF)
        return remote(g.at[m, :, :, strip(k), cols], sib.at[m, :, :, strip(k)], sib_s.at[k, m], sib_r.at[k, m],
                      in_column(0, 1))

    def along(m, first, step):
        on_x = (m < 2) == first
        return (x, in_plane(step, 0)) if on_x else (y, in_plane(0, step))

    def group(ref, k, m, i):
        return ref.at[m, i, :, strip(k)] if m < 2 else ref.at[m, :, i, strip(k)]

    def copy1(k, m, which):
        d = sign(m)
        pos, dev = along(m, True, -d if which == 1 else d)
        i = wrap(pos + (2, -d, d)[which])
        return remote(group(own, k, m, i), (tr1, dr1, cb1)[which].at[k, m], s1.at[k, m, which], r1.at[k, m, which], dev)

    def copy2(k, m, which):
        d = sign(m)
        pos, dev = along(m, False, -d if which == 1 else d)
        i = wrap(pos + (2, -d, d)[which])
        return remote(mid.at[k, m, i], (tr2, dr2, cb2)[which].at[k, m], s2.at[k, m, which], r2.at[k, m, which], dev)

    def copy2_short(k, m, which):
        step = (2, 1, 3)[which]
        pos, dev = along(m, False, step)
        return remote(mid.at[k, m, wrap(pos + step)], (tr2, dr2, cb2)[which].at[k, m], s2.at[k, m, which],
                      r2.at[k, m, which], dev)

    def z_copy(k, dz, dc):
        j = 2 * dz + dc
        src, dst = grad.at[wrap(e + dz), strip(k)], zin.at[e, c, strip(k)]
        if j == 0:
            return pltpu.make_async_copy(src, dst, zl.at[k])
        return remote(src, dst, zs.at[k, j], zr.at[k, j], in_column(dz, dc))

    mine_rows = pl.ds(pl.multiple_of(ROWS * c, 8), ROWS)
    other_rows = pl.ds(pl.multiple_of(ROWS * other, 8), ROWS)
    mom_load = pltpu.make_async_copy(mom, momv, ms.at[0])
    mom_own = pltpu.make_async_copy(mom.at[c], buf.at[:, mine_rows], ms.at[1])
    mom_sib = remote(mom.at[other], buf.at[:, mine_rows], ms.at[2], ms.at[3], in_column(0, 1))

    def mom_copy(dz):
        return remote(mout.at[dz], min_.at[e], m1s.at[dz], m1r.at[dz], in_column(dz, 0))

    mom_pass = remote(mall.at[c], mall.at[c], m2s.at[0], m2s.at[1], in_column(0, 1))

    for k in range(CHUNKS):
        for m in range(MATS):
            own_copy(k, m).start()
        if k == 0:
            mom_load.start()
    mom_own.start()
    barrier = pltpu.get_barrier_semaphore()
    for dz, dc in COLUMN:
        pl.semaphore_signal(barrier, inc=1, device_id=in_column(dz, dc))
    for dx, dy in PLANE:
        pl.semaphore_signal(barrier, inc=1, device_id=in_plane(dx, dy))
    pl.semaphore_wait(barrier, len(COLUMN) + len(PLANE))
    for k in range(CHUNKS):
        for m in range(MATS):
            sib_copy(k, m).start()
    acc[...] = jnp.zeros_like(acc)
    acc3[...] = jnp.zeros_like(acc3)

    def pair_sum(k, m, i):
        to, more = group(own, k, m, i), group(sib, k, m, i)
        for j in range(SIDE):
            to[j] = (to[j].astype(F32) + more[j].astype(F32)).astype(BF16)

    def transit(k):
        for m in range(MATS):
            own_copy(k, m).wait()
            sib_copy(k, m).wait_recv()
            pos, _ = along(m, True, 1)
            pair_sum(k, m, wrap(pos + 2))
            copy1(k, m, 0).start()

    def combine(k):
        for m in range(MATS):
            copy1(k, m, 0).wait_recv()
            pos, _ = along(m, True, 1)
            i = wrap(pos + sign(m))
            to, more, came = group(own, k, m, i), group(sib, k, m, i), tr1.at[k, m]
            for j in range(SIDE):
                to[j] = (to[j].astype(F32) + more[j].astype(F32) + came[j].astype(F32)).astype(BF16)
            copy1(k, m, 2).start()

    def direct(k):
        for m in range(MATS):
            pos, _ = along(m, True, 1)
            pair_sum(k, m, wrap(pos - sign(m)))
            copy1(k, m, 1).start()

    def turn(k):
        for m in range(MATS):
            copy1(k, m, 1).wait_recv()
            copy1(k, m, 2).wait_recv()
            pos, _ = along(m, True, 1)
            to, more, came, came2 = group(own, k, m, pos), group(sib, k, m, pos), dr1.at[k, m], cb1.at[k, m]
            for j in range(SIDE):
                v = (to[j].astype(F32) + more[j].astype(F32)) + (came[j].astype(F32) + came2[j].astype(F32))
                mid[k, m, j] = v.astype(BF16)

            @pl.when(k < SHORT)
            def _():
                copy2(k, m, 0).start()
                copy2(k, m, 1).start()

            @pl.when(k >= SHORT)
            def _():
                for which in range(3):
                    copy2_short(k, m, which).start()

    def combine2(k):
        for m in range(MATS):
            copy2(k, m, 0).wait_recv()
            pos, _ = along(m, False, 1)
            i = wrap(pos + sign(m))
            mid[k, m, i] = (mid[k, m, i].astype(F32) + tr2[k, m].astype(F32)).astype(BF16)
            copy2(k, m, 2).start()

    def collect(k, m, v):
        v = v.astype(BF16)
        grad[m, strip(k)] = v
        v = jnp.square(v.astype(F32))
        v = v[:8] + v[8:]
        acc[...] += v[:, :128] + v[:, 128:256] + v[:, 256:384] + v[:, 384:]

    def send_strips(k):
        for dz in (2, 1, 3, 0):
            for dc in range(2):
                z_copy(k, dz, dc).start()

    def finish_sum(k):
        for m in range(MATS):
            copy2(k, m, 1).wait_recv()
            copy2(k, m, 2).wait_recv()
            pos, _ = along(m, False, 1)
            collect(k, m, mid[k, m, pos].astype(F32) + (dr2[k, m].astype(F32) + cb2[k, m].astype(F32)))
        send_strips(k)

    def finish_short(k):
        for m in range(MATS):
            for which in range(3):
                copy2_short(k, m, which).wait_recv()
            pos, _ = along(m, False, 1)
            v = mid[k, m, pos].astype(F32) + tr2[k, m].astype(F32)
            collect(k, m, v + (dr2[k, m].astype(F32) + cb2[k, m].astype(F32)))

    def mom_send(k):
        mom_load.wait()
        for dz in (2, 1, 3, 0):
            t = wrap(e + dz)
            first_is = jnp.float32(0)
            second_is = jnp.float32(0)
            for m in range(MATS):
                here = jnp.where(t == m, 1.0, 0.0).astype(F32)
                first_is = first_is + here * mask(m, 2 * e)
                second_is = second_is + here * mask(m, 2 * e + 1)
            for i in range(GROUPS):
                for h in range(2):
                    cols = slice(h * HALF, (h + 1) * HALF)
                    v = first_is * momv[0, i, :, cols] + second_is * momv[1, i, :, cols]
                    mout[dz, i, h * ROWS:(h + 1) * ROWS] = v.astype(BF16)
            if dz:
                mom_copy(dz).start()
        mom_sib.start()

    def mom_sum(k):
        for dz in (1, 2, 3):
            mom_copy(dz).wait_recv()
        for i in range(GROUPS):
            v = mout[0, i].astype(F32)
            for dz in (1, 2, 3):
                v = v + min_[wrap(e + dz), i].astype(F32)
            mall[c, i] = v.astype(BF16)
        mom_pass.start()

    def finish_send(k):
        finish_short(k)
        send_strips(k)

    stages = ((transit, 0, 0, CHUNKS), (combine, 1, 0, CHUNKS), (direct, 2, 0, CHUNKS), (turn, 3, 0, CHUNKS),
              (combine2, 4, 0, SHORT), (finish_sum, 5, 0, SHORT), (finish_send, 4, SHORT, LAST), (mom_send, 1, 0, 1),
              (mom_sum, LAST + 2, 0, 1))

    def step(t, carry):
        for stage, lag, low, high in stages:
            if low < high:
                @pl.when((t >= low + lag) & (t < high + lag))
                def _():
                    stage(t - lag)
        return carry

    lax.fori_loop(0, LAST + 5, step, 0)
    finish_short(LAST)

    me_column = 2 * e + c
    me_plane = 4 * x + y

    def spread_column(src, dst, send, recv):
        copies = [remote(src, dst.at[me_column], send.at[i], recv.at[i], in_column(*d)) for i, d in enumerate(COLUMN)]
        for copy in copies:
            copy.start()
        dst[me_column] = src[...]
        return copies

    def spread_plane(src, dst, send, recv):
        copies = [remote(src, dst.at[me_plane], send.at[i], recv.at[i], in_plane(*d)) for i, d in enumerate(PLANE)]
        for copy in copies:
            copy.start()
        dst[me_plane] = src[...]
        return copies

    def total_of(copies, ref, count):
        for copy in copies:
            copy.wait_recv()
        v = ref[0]
        for j in range(1, count):
            v = v + ref[j]
        return v

    first = spread_column(acc, column, cs, cr)
    send_strips(LAST)
    acc2[...] = total_of(first, column, 8)
    second = spread_plane(acc2, plane, ps, pr)
    mom_pass.wait_recv()
    for k in range(CHUNKS):
        for dz in range(4):
            for dc in range(2):
                if dz + dc:
                    z_copy(k, dz, dc).wait_recv()
                else:
                    z_copy(k, 0, 0).wait()
    mean = whole_sum(total_of(second, plane, 16)) / float(MATS * D * FF)
    factor = jnp.minimum(1.0, CLIP_RMS / jnp.sqrt(mean + MEAN_EPS))

    def direction(i, carry):
        parts = [mall[k, i].astype(F32) for k in range(2)]
        for h in range(2):
            kept = jnp.concatenate([v[h * ROWS:(h + 1) * ROWS] for v in parts], axis=0)
            v = factor * zin[i, h].astype(F32)
            v = v + MOMENT * (MOMENT * kept + v)
            X[i, :, h * HALF:(h + 1) * HALF] = v.astype(BF16)
            sq = jnp.sum(jnp.square(v).reshape(BLOCK // 8, 8, HALF), axis=0)
            acc3[...] += sq[:, :128] + sq[:, 128:256] + sq[:, 256:384] + sq[:, 384:]
        return carry

    lax.fori_loop(0, GROUPS, direction, 0)


    def part4(ref, q, i):
        return ref.at[pl.ds(pl.multiple_of((4 * q + i) * 4 * PART, 16), 4 * PART)]

    def on(q, first, step):
        return (x, in_plane(step, 0)) if (q == 0) == first else (y, in_plane(0, step))

    def first_copy(q, step):
        pos, dev = on(q, True, step)
        return remote(part4(packed, q, wrap(pos + step)), rs1.at[q, step - 1], g1s.at[q, step - 1], g1r.at[q, step - 1],
                      dev)

    def second_copy(q, step):
        _, dev = on(q, False, step)
        return remote(midg.at[q], rs2.at[q, step - 1], g2s.at[q, step - 1], g2r.at[q, step - 1], dev)

    def third_copy(q, step):
        pos, dev = on(q, True, step)
        ref = part4(full.at[c], q, pos)
        return remote(ref, ref, g3s.at[q, step - 1], g3r.at[q, step - 1], dev)

    def pair_copy(q, n):
        pos, _ = on(q, True, 1)
        ref = part4(full.at[c], q, wrap(pos + n))
        return remote(ref, ref, g5s.at[q, n], g5r.at[q, n], in_column(0, 1))

    STEPS = (2, 1, 3)
    for j in range(4):
        cols = pl.ds(pl.multiple_of((2 * j + c) * LANES, LANES), LANES)
        Xc[:, j * LANES:(j + 1) * LANES] = X[:, :, cols].reshape(GROUPS * BLOCK, LANES)
    at = 0
    for i in range(4):
        left = X[:, :, i * PANEL:(i + 1) * PANEL].reshape(GROUPS * BLOCK, PANEL)
        panel = lax.dot_general(left, Xc[:, i * LANES:], (((0,), (0,)), ((), ())),
                                preferred_element_type=F32).astype(BF16)
        for j in range(4 - i):
            packed[at:at + PANEL] = panel[:, j * LANES:(j + 1) * LANES]
            at += PANEL
        if i in (1, 3):
            for s in STEPS:
                first_copy(i // 2, s).start()
    squares = spread_plane(acc3, plane2, ps2, pr2)
    mom_own.wait()
    mom_sib.wait_recv()

    def slot_copy(dz, dc):
        j = 2 * dz + dc
        if j == 0:
            return pltpu.make_async_copy(zout.at[0], zin2.at[e, c], z2s.at[0])
        return remote(zout.at[j], zin2.at[e, c], z2s.at[j], z2r.at[j], in_column(dz, dc))

    for dz in (2, 1, 3, 0):
        for dc in range(2):
            slot = wrap(e + dz) * SLOTS + lax.rem(c + dc, 2)
            v = mask(0, slot) * grad[0].astype(F32)
            for m in range(1, MATS):
                v = v + mask(m, slot) * grad[m].astype(F32)
            zout[2 * dz + dc] = v.astype(BF16)
            slot_copy(dz, dc).start()

    def drain(k, carry):
        for m in range(MATS):
            sib_copy(k, m).wait_send()
            for which in range(3):
                copy1(k, m, which).wait_send()

                copy2(k, m, which).wait_send()
        for dz, dc in COLUMN:
            z_copy(k, dz, dc).wait_send()
        return carry

    lax.fori_loop(0, CHUNKS, drain, 0)
    for dz in (1, 2, 3):
        mom_copy(dz).wait_send()
    mom_pass.wait_send()
    mom_sib.wait_send()
    for q in range(2):
        for s in STEPS:
            first_copy(q, s).wait_recv()
        pos, _ = on(q, True, 1)
        v = part4(packed, q, pos)[...].astype(F32) + rs1[q, 0].astype(F32)
        midg[q] = (v + (rs1[q, 1].astype(F32) + rs1[q, 2].astype(F32))).astype(BF16)
        for s in STEPS:
            second_copy(q, s).start()
    for q in range(2):
        for s in STEPS:
            second_copy(q, s).wait_recv()
        pos, _ = on(q, True, 1)
        v = midg[q].astype(F32) + rs2[q, 0].astype(F32)
        part4(full.at[c], q, pos)[...] = (v + (rs2[q, 1].astype(F32) + rs2[q, 2].astype(F32))).astype(BF16)
        for s in STEPS:
            third_copy(q, s).start()
        pair_copy(q, 0).start()
    acc4[...] = total_of(squares, plane2, 16)
    spread = spread_column(acc4, sq_in, qs, qr)
    inv = 1.0 / (jnp.sqrt(whole_sum(acc4[...])) + NORM_EPS)
    for s in (1, 3, 2):
        for q in range(2):
            third_copy(q, s).wait_recv()
            pair_copy(q, 4 - s).start()
    for q in range(2):
        for n in range(4):
            pair_copy(q, n).wait_recv()
    for k in range(2):
        at = 0
        for i in range(4):
            for n in range(4 - i):
                j = 2 * (i + n) + k
                block = full[k, at:at + PANEL]
                G[i * PANEL:(i + 1) * PANEL, j * LANES:(j + 1) * LANES] = block
                if n:
                    G[j * LANES:(j + 1) * LANES, i * PANEL:(i + 1) * PANEL] = block.T
                at += PANEL

    def product(lhs, rhs, out, finish):
        for i in range(4):
            low, high = i * PANEL, (i + 1) * PANEL
            v = jnp.dot(lhs[low:high], rhs[:, low:], preferred_element_type=F32)
            v = finish(v, slice(low, high), slice(low, FF)).astype(BF16)
            out[low:high, low:] = v
            for j in range(i + 1, 4):
                out[j * PANEL:(j + 1) * PANEL, low:high] = v[:, (j - i) * PANEL:(j - i + 1) * PANEL].T

    def polynomial(src, q, t, out, scale):
        b_s = COEF_B * scale
        c_s = COEF_C * scale * scale
        product(src, src, q, lambda v, i, j: b_s * src[i, j].astype(F32) + c_s * v)
        product(src, q, t, lambda v, i, j: scale * (COEF_A * src[i, j].astype(F32) + v))
        product(t, q, out, lambda v, i, j: COEF_A * t[i, j].astype(F32) + v)

    def advance(src, rhs, scale):
        v = src[...]
        w = scale * (COEF_A * v.astype(F32) + jnp.dot(v, rhs[...], preferred_element_type=F32))
        return w.astype(BF16)

    for n in range(2):
        X2[0, n * BLOCK:(n + 1) * BLOCK] = X[2 * c + n]
    polynomial(G, A, B, T, inv * inv)
    X2[1] = advance(X2.at[0], A, inv)
    polynomial(T, A, B, G, 1.0)
    X2[0] = advance(X2.at[1], A, 1.0)
    v = X2[0]
    w = jnp.dot(v, G[...], preferred_element_type=F32).astype(BF16)
    z = jnp.dot(w, G[...], preferred_element_type=F32)
    z = (COEF_A * v.astype(F32) + COEF_B * w.astype(F32) + COEF_C * z).astype(BF16)

    def return_copy(n, dc):
        src = back.at[n, lax.rem(c + dc, 2)]
        return remote(src, ret.at[e], bs.at[n, dc], br.at[e], target(2 * c + n, x, y, lax.rem(c + dc, 2)))

    def return_local(n):
        return pltpu.make_async_copy(back.at[n, c], ret.at[e], bl.at[0])

    def return_in(m):
        return remote(back.at[0, 0], ret.at[m], bs.at[0, 0], br.at[m], in_column(0, 1))

    for n in range(2):
        for h in range(2):
            for k in range(2):
                top = n * BLOCK + h * ROWS
                back[n, h, k * ROWS:(k + 1) * ROWS] = z[top:top + ROWS, k * HALF:(k + 1) * HALF]
        return_copy(n, 1).start()

        @pl.when(2 * c + n != e)
        def _():
            return_copy(n, 0).start()

        @pl.when(2 * c + n == e)
        def _():
            return_local(n).start()

    for dz in range(4):
        for dc in range(2):
            if dz + dc:
                slot_copy(dz, dc).wait_recv()
            else:
                slot_copy(0, 0).wait()

    def momentum(i, carry):
        for h in range(2):
            cols = pl.ds(h * HALF, HALF)
            buf[i, :, cols] = MOMENT * buf[i, :, cols] + factor * zin2[i, h].astype(F32)
        return carry

    lax.fori_loop(0, GROUPS, momentum, 0)
    new_own = pltpu.make_async_copy(buf.at[:, mine_rows], new_mom.at[c], ns.at[0])
    new_sib = remote(buf.at[:, other_rows], new_mom.at[c], ns.at[1], ns.at[2], in_column(0, 1))
    new_sib.start()
    new_own.start()

    for copy in spread:
        copy.wait_recv()
    lane = lax.broadcasted_iota(jnp.int32, (8, LANES), 1)
    mean_sq = jnp.zeros((8, LANES), F32)
    for m in range(MATS):
        mean_sq = mean_sq + jnp.where(lane == m, whole_sum(sq_in[2 * m]) / float(D * FF), 0.0)
    rms_out[...] = jnp.sqrt(mean_sq)

    for q in range(2):
        for s in STEPS:
            first_copy(q, s).wait_send()
            second_copy(q, s).wait_send()
            third_copy(q, s).wait_send()
        for n in range(4):
            pair_copy(q, n).wait_send()
    for dz, dc in COLUMN:
        slot_copy(dz, dc).wait_send()
    for copy in first + second + squares + spread:
        copy.wait_send()
    for dz in (0, 1, 3, 2):
        m = wrap(e + dz)
        if dz:
            return_in(m).wait_recv()
        else:
            @pl.when(e // 2 == c)
            def _():
                return_local(0).wait()

            @pl.when(e // 2 != c)
            def _():
                return_in(m).wait_recv()
        v = ret[m].astype(F32)
        rows_out[m, :, :HALF] = v[:ROWS].astype(BF16)
        rows_out[m, :, HALF:] = v[ROWS:].astype(BF16)
    for n in range(2):
        return_copy(n, 1).wait_send()

        @pl.when(2 * c + n != e)
        def _():
            return_copy(n, 0).wait_send()

    new_own.wait()
    new_sib.wait()


ANY = pl.BlockSpec(memory_space=pl.ANY)
VMEM = pl.BlockSpec(memory_space=pltpu.VMEM)
SMEM = pl.BlockSpec(memory_space=pltpu.SMEM)
DMA = pltpu.SemaphoreType.DMA


def per_device(grad_terms, momentum, weights, owner_list):
    small = (CHUNKS, MATS, STRIP, HALF)
    large = (CHUNKS, MATS, SIDE, STRIP, HALF)
    whole = (MATS, SIDE, SIDE, BLOCK, HALF)
    tile = pltpu.VMEM((8, LANES), F32)
    square = pltpu.VMEM((FF, FF), BF16)
    new_mom, rows, rms = pl.pallas_call(
        muon_kernel,
        name="muon",
        out_shape=(
            jax.ShapeDtypeStruct((SLOTS, GROUPS, ROWS, FF), F32),
            jax.ShapeDtypeStruct((MATS, ROWS, FF), BF16),
            jax.ShapeDtypeStruct((8, LANES), F32),
        ),
        in_specs=[SMEM, ANY, ANY],
        out_specs=(ANY, VMEM, VMEM),
        scratch_shapes=[
            pltpu.VMEM(whole, BF16), pltpu.VMEM(whole, BF16),
            pltpu.VMEM(large, BF16), pltpu.VMEM(large, BF16), pltpu.VMEM(large, BF16), pltpu.VMEM(large, BF16),
            pltpu.VMEM(small, BF16), pltpu.VMEM(small, BF16), pltpu.VMEM(small, BF16),
            pltpu.VMEM((MATS, BLOCK, HALF), BF16),
            pltpu.VMEM((GROUPS, 2, BLOCK, HALF), BF16),
            pltpu.VMEM((GROUPS * SLOTS, BLOCK, HALF), BF16),
            pltpu.VMEM((GROUPS, 2, BLOCK, HALF), BF16),
            pltpu.VMEM((SLOTS, GROUPS, ROWS, FF), F32),
            pltpu.VMEM((4, GROUPS, BLOCK, HALF), BF16), pltpu.VMEM((4, GROUPS, BLOCK, HALF), BF16),
            pltpu.VMEM((2, GROUPS, BLOCK, HALF), BF16),
            pltpu.VMEM((GROUPS, BLOCK, FF), F32),
            pltpu.VMEM((GROUPS, BLOCK, FF), BF16),
            pltpu.VMEM((GROUPS * BLOCK, HALF), BF16),
            pltpu.VMEM((2, 2 * BLOCK, FF), BF16),
            pltpu.VMEM((32 * PART, LANES), BF16), pltpu.VMEM((2, 32 * PART, LANES), BF16),
            pltpu.VMEM((2, 3, 4 * PART, LANES), BF16),
            pltpu.VMEM((2, 4 * PART, LANES), BF16),
            pltpu.VMEM((2, 3, 4 * PART, LANES), BF16),
            square, square, square, square,
            pltpu.VMEM((2, 2, BLOCK, HALF), BF16), pltpu.VMEM((MATS, BLOCK, HALF), BF16),
            tile, tile, tile, tile,
            pltpu.VMEM((8, 8, LANES), F32), pltpu.VMEM((16, 8, LANES), F32), pltpu.VMEM((16, 8, LANES), F32),
            pltpu.VMEM((8, 8, LANES), F32),
            DMA((CHUNKS, MATS)), DMA((CHUNKS, MATS)), DMA((CHUNKS, MATS)),
            DMA((CHUNKS, MATS, 3)), DMA((CHUNKS, MATS, 3)), DMA((CHUNKS, MATS, 3)), DMA((CHUNKS, MATS, 3)),
            DMA((CHUNKS, 8)), DMA((CHUNKS, 8)), DMA((CHUNKS,)), DMA((4,)), DMA((4,)), DMA((4,)), DMA((2,)),
            DMA((7,)), DMA((7,)), DMA((15,)), DMA((15,)), DMA((3,)),
            DMA((2, 3)), DMA((2, 3)), DMA((2, 3)), DMA((2, 3)), DMA((2, 3)), DMA((2, 3)),
            DMA((2, 4)), DMA((2, 4)),
            DMA((15,)), DMA((15,)), DMA((7,)), DMA((7,)), DMA((8,)), DMA((8,)), DMA((2, 2)), DMA((4,)), DMA((1,)),
        ],
        compiler_params=pltpu.CompilerParams(collective_id=0, has_side_effects=True, vmem_limit_bytes=60 << 20),
    )(owner_list, grad_terms.reshape(MATS, SIDE, SIDE, BLOCK, FF), momentum[0])

    rows = rows.astype(F32)
    scale_rms = 0.2 * math.sqrt(max(D, FF))
    update = (scale_rms * rows).astype(BF16)
    new_weights = weights * (1.0 - LEARN * DECAY) - LEARN * scale_rms * rows
    return (new_weights, update, new_mom[None], rms[0, :MATS])


def solution(mesh):
    placed = (
        P("dp", None, "expert", None),
        P("expert", None, None, "dp", None),
        P(None, ("expert", "dp"), None),
        P(),
    )
    return jax.shard_map(
        per_device,
        mesh=mesh,
        in_specs=placed,
        out_specs=(
            P(None, ("expert", "dp"), None),
            P(None, ("expert", "dp"), None),
            P("expert", None, None, "dp", None),
            P(),
        ),
        check_vma=False,
    )
```

```python
import math

import jax
import jax.numpy as jnp
from jax import lax
from jax.experimental import pallas as pl
from jax.experimental.pallas import tpu as pltpu
from jax.sharding import PartitionSpec as P

D = 7168
FF = 1024
MATS = 4
SLOTS = 2
GROUPS = 4
SIDE = 4
BLOCK = 112
ROWS = 56
HALF = FF // 2
LANES = 128
STRIP = 16
CHUNKS = BLOCK // STRIP
LAST = CHUNKS - 1
SHORT = 5
PANEL = 256
PART = 80

MOMENT = 0.95
CLIP_RMS = 1.0
LEARN = 0.1
DECAY = 0.1
COEF_A = 3.4445
COEF_B = -4.775
COEF_C = 2.0315
NORM_EPS = 1e-07
MEAN_EPS = 1e-06
F32 = jnp.float32
BF16 = jnp.bfloat16

COLUMN = ((2, 0), (2, 1), (1, 0), (1, 1), (3, 0), (3, 1), (0, 1))
PLANE = tuple((dx, dy) for dx in range(4) for dy in range(4) if dx + dy)


def wrap(v):
    return lax.rem(v + 4, 4)


def remote(src, dst, send, recv, device):
    return pltpu.make_async_remote_copy(src_ref=src, dst_ref=dst, send_sem=send, recv_sem=recv, device_id=device)


def whole_sum(v):
    return jnp.sum(jnp.sum(v, axis=0, keepdims=True), axis=1, keepdims=True)


def sign(m):
    return 1 if m % 2 else -1


def muon_kernel(owners, g, mom, new_mom, rows_out, rms_out,
                own, sib, tr1, dc1, mid, tr2, dc2, grad, zin, zout, zin2, momv, mout, min_, mall, Mb, gright, mright, grams, buf, X, X2,
                packed, full, rs1, midg, rs2, G, A, B, T, back, ret, acc, acc2, acc3, acc4,
                column, plane, plane2, sq_in,
                own_s, sib_s, sib_r, s1, t1r, d1r, s2, t2r, d2r, zs, zr, zl, ms, m1s, m1r, m2s, cs, cr, ps, pr, ns, g1s, g1r,
                g2s, g2r, g3s, g3r, g5s, g5r, ps2, pr2, qs, qr, z2s, z2r, z2l, bs, br, bl):
    e = lax.axis_index("expert")
    p = lax.axis_index("dp")
    x, y, c = p // 8, (p // 2) % 4, p % 2
    other = 1 - c

    def target(te, tx, ty, tc):
        return {"expert": te, "dp": tx * 8 + ty * 2 + tc}

    def in_column(dz, dc):
        return target(wrap(e + dz), x, y, lax.rem(c + dc, 2))

    def in_plane(dx, dy):
        return target(e, wrap(x + dx), wrap(y + dy), c)

    def arrived(sem, ref):
        remote(ref, ref, sem, sem, in_column(0, 1)).wait_recv()

    def left(sem, ref):
        remote(ref, ref, sem, sem, in_column(0, 1)).wait_send()

    places = []
    for m in range(MATS):
        number = jnp.int32(0)
        for m2 in range(m):
            number = number + jnp.where(owners[m2] == owners[m], 1, 0)
        places.append(owners[m] * SLOTS + number)

    def mask(m, slot):
        return jnp.where(places[m] == slot, 1.0, 0.0).astype(F32)

    def strip(k):
        return pl.ds(pl.multiple_of(k * STRIP, STRIP), STRIP)

    def own_copy(k):
        cols = pl.ds(pl.multiple_of(c * HALF, HALF), HALF)
        return pltpu.make_async_copy(g.at[:, :, :, strip(k), cols], own.at[:, :, :, strip(k)], own_s.at[k])

    def sib_copy(k, m):
        cols = pl.ds(pl.multiple_of(other * HALF, HALF), HALF)
        return remote(g.at[m, :, :, strip(k), cols], sib.at[m, :, :, strip(k)], sib_s.at[0], sib_r.at[k, m],
                      in_column(0, 1))

    def along(m, first, step):
        on_x = (m < 2) == first
        return (x, in_plane(step, 0)) if on_x else (y, in_plane(0, step))

    def group(ref, k, m, i):
        return ref.at[m, i, :, strip(k)] if m < 2 else ref.at[m, :, i, strip(k)]

    def copy1(k, m, which):
        d = sign(m)
        pos, dev = along(m, True, -d if which == 1 else d)
        i = wrap(pos + (2, -d, d)[which])
        if which == 0:
            dst, recv = tr1.at[k, m], t1r.at[k]
        else:
            dst, recv = dc1.at[k, m, which - 1], d1r.at[k]
        return remote(group(own, k, m, i), dst, s1.at[which], recv, dev)

    def ends2(k, m, which):
        if which == 0:
            return tr2.at[k, m], s2.at[0], t2r.at[k]
        return dc2.at[k, m, which - 1], s2.at[which], d2r.at[k]

    def copy2(k, m, which):
        d = sign(m)
        pos, dev = along(m, False, -d if which == 1 else d)
        i = wrap(pos + (2, -d, d)[which])
        return remote(mid.at[k, m, i], *ends2(k, m, which), dev)

    def copy2_short(k, m, which):
        step = (2, 1, 3)[which]
        pos, dev = along(m, False, step)
        return remote(mid.at[k, m, wrap(pos + step)], *ends2(k, m, which), dev)

    def z_copy(k, dz, dc):
        j = 2 * dz + dc
        src, dst = grad.at[wrap(e + dz), strip(k)], zin.at[2 * e + c, strip(k)]
        if j == 0:
            return pltpu.make_async_copy(src, dst, zl.at[0])
        return remote(src, dst, zs.at[0], zr.at[0], in_column(dz, dc))

    mine_rows = pl.ds(pl.multiple_of(ROWS * c, 8), ROWS)
    other_rows = pl.ds(pl.multiple_of(ROWS * other, 8), ROWS)
    mom_load = pltpu.make_async_copy(mom, momv, ms.at[0])
    mom_own = pltpu.make_async_copy(mom.at[c], buf.at[:, mine_rows], ms.at[1])
    mom_sib = remote(mom.at[other], buf.at[:, mine_rows], ms.at[2], ms.at[3], in_column(0, 1))

    def mom_copy(dz):
        return remote(mout.at[dz], min_.at[e], m1s.at[0], m1r.at[0], in_column(dz, 0))

    mom_pass = remote(mall.at[c], mall.at[c], m2s.at[0], m2s.at[1], in_column(0, 1))

    for k in range(CHUNKS):
        own_copy(k).start()
        if k == 0:
            mom_load.start()
    mom_own.start()
    barrier = pltpu.get_barrier_semaphore()
    for dz, dc in COLUMN:
        pl.semaphore_signal(barrier, inc=1, device_id=in_column(dz, dc))
    for dx, dy in PLANE:
        pl.semaphore_signal(barrier, inc=1, device_id=in_plane(dx, dy))
    pl.semaphore_wait(barrier, len(COLUMN) + len(PLANE))
    for k in range(CHUNKS):
        for m in range(MATS):
            sib_copy(k, m).start()
    acc[...] = jnp.zeros_like(acc)
    acc3[...] = jnp.zeros_like(acc3)

    def pair_sum(k, m, i):
        to, more = group(own, k, m, i), group(sib, k, m, i)
        for j in range(SIDE):
            to[j] = (to[j].astype(F32) + more[j].astype(F32)).astype(BF16)

    def transit(k):
        own_copy(k).wait()
        for m in range(MATS):
            sib_copy(k, m).wait_recv()
            pos, _ = along(m, True, 1)
            pair_sum(k, m, wrap(pos + 2))
            copy1(k, m, 0).start()

    def combine(k):
        arrived(t1r.at[k], tr1.at[k])
        for m in range(MATS):
            pos, _ = along(m, True, 1)
            i = wrap(pos + sign(m))
            to, more, came = group(own, k, m, i), group(sib, k, m, i), tr1.at[k, m]
            for j in range(SIDE):
                to[j] = (to[j].astype(F32) + more[j].astype(F32) + came[j].astype(F32)).astype(BF16)
            copy1(k, m, 2).start()

    def direct(k):
        for m in range(MATS):
            pos, _ = along(m, True, 1)
            pair_sum(k, m, wrap(pos - sign(m)))
            copy1(k, m, 1).start()

    def turn(k):
        arrived(d1r.at[k], dc1.at[k])
        for m in range(MATS):
            pos, _ = along(m, True, 1)
            to, more, came, came2 = group(own, k, m, pos), group(sib, k, m, pos), dc1.at[k, m, 0], dc1.at[k, m, 1]
            for j in range(SIDE):
                v = (to[j].astype(F32) + more[j].astype(F32)) + (came[j].astype(F32) + came2[j].astype(F32))
                mid[k, m, j] = v.astype(BF16)

            @pl.when(k < SHORT)
            def _():
                copy2(k, m, 0).start()
                copy2(k, m, 1).start()

            @pl.when(k >= SHORT)
            def _():
                for which in range(3):
                    copy2_short(k, m, which).start()

    def combine2(k):
        arrived(t2r.at[k], tr2.at[k])
        for m in range(MATS):
            pos, _ = along(m, False, 1)
            i = wrap(pos + sign(m))
            mid[k, m, i] = (mid[k, m, i].astype(F32) + tr2[k, m].astype(F32)).astype(BF16)
            copy2(k, m, 2).start()

    def collect(k, m, v):
        v = v.astype(BF16)
        grad[m, strip(k)] = v
        v = jnp.square(v.astype(F32))
        v = v[:8] + v[8:]
        acc[...] += v[:, :128] + v[:, 128:256] + v[:, 256:384] + v[:, 384:]

    def send_strips(k):
        for dz in (2, 1, 3, 0):
            for dc in range(2):
                z_copy(k, dz, dc).start()

    def finish_sum(k):
        arrived(d2r.at[k], dc2.at[k])
        for m in range(MATS):
            pos, _ = along(m, False, 1)
            collect(k, m, mid[k, m, pos].astype(F32) + (dc2[k, m, 0].astype(F32) + dc2[k, m, 1].astype(F32)))
        send_strips(k)

    def finish_short(k):
        arrived(t2r.at[k], tr2.at[k])
        arrived(d2r.at[k], dc2.at[k])
        for m in range(MATS):
            pos, _ = along(m, False, 1)
            v = mid[k, m, pos].astype(F32) + tr2[k, m].astype(F32)
            collect(k, m, v + (dc2[k, m, 0].astype(F32) + dc2[k, m, 1].astype(F32)))

    def mom_send(k):
        mom_load.wait()
        for dz in (2, 1, 3, 0):
            t = wrap(e + dz)
            first_is = jnp.float32(0)
            second_is = jnp.float32(0)
            for m in range(MATS):
                here = jnp.where(t == m, 1.0, 0.0).astype(F32)
                first_is = first_is + here * mask(m, 2 * e)
                second_is = second_is + here * mask(m, 2 * e + 1)
            for i in range(GROUPS):
                for h in range(2):
                    cols = slice(h * HALF, (h + 1) * HALF)
                    v = first_is * momv[0, i, :, cols] + second_is * momv[1, i, :, cols]
                    mout[dz, i, h * ROWS:(h + 1) * ROWS] = v.astype(BF16)
            if dz:
                mom_copy(dz).start()
        mom_sib.start()

    def mom_sum(k):
        arrived(m1r.at[0], min_.at[pl.ds(0, 3)])
        for i in range(GROUPS):
            v = mout[0, i].astype(F32)
            for dz in (1, 2, 3):
                v = v + min_[wrap(e + dz), i].astype(F32)
            mall[c, i] = v.astype(BF16)
        mom_pass.start()

    def finish_send(k):
        finish_short(k)
        send_strips(k)

    stages = ((transit, 0, 0, CHUNKS), (combine, 1, 0, CHUNKS), (direct, 2, 0, CHUNKS), (turn, 3, 0, CHUNKS),
              (combine2, 4, 0, SHORT), (finish_sum, 5, 0, SHORT), (finish_send, 4, SHORT, LAST), (mom_send, 1, 0, 1),
              (mom_sum, LAST + 2, 0, 1))

    def step(t, carry):
        for stage, lag, low, high in stages:
            if low < high:
                @pl.when((t >= low + lag) & (t < high + lag))
                def _():
                    stage(t - lag)
        return carry

    lax.fori_loop(0, LAST + 5, step, 0)
    finish_short(LAST)

    me_column = 2 * e + c
    me_plane = 4 * x + y

    def spread_column(src, dst, send, recv):
        copies = [remote(src, dst.at[me_column], send.at[0], recv.at[0], in_column(*d)) for d in COLUMN]
        for copy in copies:
            copy.start()
        dst[me_column] = src[...]

    def spread_plane(src, dst, send, recv):
        copies = [remote(src, dst.at[me_plane], send.at[0], recv.at[0], in_plane(*d)) for d in PLANE]
        for copy in copies:
            copy.start()
        dst[me_plane] = src[...]

    def total_of(recv, ref, count):
        arrived(recv.at[0], ref.at[pl.ds(0, count - 1)])
        v = ref[0]
        for j in range(1, count):
            v = v + ref[j]
        return v

    spread_column(acc, column, cs, cr)
    send_strips(LAST)
    acc2[...] = total_of(cr, column, 8)
    spread_plane(acc2, plane, ps, pr)
    mom_pass.wait_recv()
    arrived(zr.at[0], zin.at[pl.ds(0, 7)])
    pltpu.make_async_copy(zin.at[0], zin.at[0], zl.at[0]).wait()

    def unpack(i, carry):
        parts = [mall[k, i].astype(F32) for k in range(2)]
        for h in range(2):
            kept_rows = [v[h * ROWS:(h + 1) * ROWS] for v in parts]
            Mb[i, h] = jnp.concatenate(kept_rows, axis=0).astype(BF16)
        return carry

    lax.fori_loop(0, GROUPS, unpack, 0)
    for j in range(4):
        cols = pl.ds(pl.multiple_of((2 * (j % 2) + c) * LANES, LANES), LANES)
        gright[:, j * LANES:(j + 1) * LANES] = jnp.concatenate([zin[2 * n + j // 2, :, cols] for n in range(GROUPS)], axis=0)
        mright[:, j * LANES:(j + 1) * LANES] = Mb[:, j // 2, :, cols].reshape(GROUPS * BLOCK, LANES)

    def outer(left, right):
        return lax.dot_general(left, right, (((0,), (0,)), ((), ())), preferred_element_type=F32)

    at = 0
    for i in range(4):
        cols = slice((i % 2) * PANEL, (i % 2 + 1) * PANEL)
        gleft = jnp.concatenate([zin[2 * n + i // 2, :, cols] for n in range(GROUPS)], axis=0)
        mleft = Mb[:, i // 2, :, cols].reshape(GROUPS * BLOCK, PANEL)
        gr, mr = gright[:, i * LANES:], mright[:, i * LANES:]
        gg, gm, mm = outer(gleft, gr), outer(gleft, mr) + outer(mleft, gr), outer(mleft, mr)
        for j in range(4 - i):
            for n, v in enumerate((gg, gm, mm)):
                grams[n, at:at + PANEL] = v[:, j * LANES:(j + 1) * LANES]
            at += PANEL
    mean = whole_sum(total_of(pr, plane, 16)) / float(MATS * D * FF)
    factor = jnp.minimum(1.0, CLIP_RMS / jnp.sqrt(mean + MEAN_EPS))


    def part4(ref, q, i):
        return ref.at[pl.ds(pl.multiple_of((4 * q + i) * 4 * PART, 16), 4 * PART)]

    def on(q, first, step):
        return (x, in_plane(step, 0)) if (q == 0) == first else (y, in_plane(0, step))

    def first_copy(q, step):
        pos, dev = on(q, True, step)
        return remote(part4(packed, q, wrap(pos + step)), rs1.at[q, step - 1], g1s.at[0], g1r.at[q],
                      dev)

    def second_copy(q, step):
        _, dev = on(q, False, step)
        return remote(midg.at[q], rs2.at[q, step - 1], g2s.at[0], g2r.at[q], dev)

    def third_copy(q, step):
        pos, dev = on(q, True, step)
        ref = part4(full.at[c], q, pos)
        return remote(ref, ref, g3s.at[0], g3r.at[q, step - 1], dev)

    def pair_copy(q, n):
        pos, _ = on(q, True, 1)
        ref = part4(full.at[c], q, wrap(pos + n))
        return remote(ref, ref, g5s.at[0], g5r.at[0], in_column(0, 1))

    STEPS = (2, 1, 3)
    u = (1.0 + MOMENT) * factor
    w = MOMENT * MOMENT
    for q in range(2):
        def weigh(i, carry):
            rows = pl.ds(pl.multiple_of((16 * q + i) * PART, 16), PART)
            v = (u * u) * grams[0, rows] + (u * w) * grams[1, rows] + (w * w) * grams[2, rows]
            packed[rows] = v.astype(BF16)
            return carry

        lax.fori_loop(0, 16, weigh, 0)
        for s in STEPS:
            first_copy(q, s).start()

    def direction(i, carry):
        for h in range(2):
            v = factor * zin[2 * i + h].astype(F32)
            v = v + MOMENT * (MOMENT * Mb[i, h].astype(F32) + v)
            X[i, :, h * HALF:(h + 1) * HALF] = v.astype(BF16)
            sq = jnp.sum(jnp.square(v).reshape(BLOCK // 8, 8, HALF), axis=0)
            acc3[...] += sq[:, :128] + sq[:, 128:256] + sq[:, 256:384] + sq[:, 384:]
        return carry

    lax.fori_loop(0, GROUPS, direction, 0)

    spread_plane(acc3, plane2, ps2, pr2)
    mom_own.wait()
    mom_sib.wait_recv()

    def slot_copy(dz, dc):
        j = 2 * dz + dc
        if j == 0:
            return pltpu.make_async_copy(zout.at[0], zin2.at[2 * e + c], z2l.at[0])
        return remote(zout.at[j], zin2.at[2 * e + c], z2s.at[0], z2r.at[0], in_column(dz, dc))

    for dz in (2, 1, 3, 0):
        for dc in range(2):
            slot = wrap(e + dz) * SLOTS + lax.rem(c + dc, 2)
            v = mask(0, slot) * grad[0].astype(F32)
            for m in range(1, MATS):
                v = v + mask(m, slot) * grad[m].astype(F32)
            zout[2 * dz + dc] = v.astype(BF16)
            slot_copy(dz, dc).start()

    left(sib_s.at[0], sib)
    for which in range(3):
        left(s1.at[which], tr1)
        left(s2.at[which], tr2)
    left(zs.at[0], zin.at[pl.ds(0, 7)])
    left(m1s.at[0], mout.at[pl.ds(0, 3)])
    for q in range(2):
        arrived(g1r.at[q], rs1.at[q])
        pos, _ = on(q, True, 1)
        v = part4(packed, q, pos)[...].astype(F32) + rs1[q, 0].astype(F32)
        midg[q] = (v + (rs1[q, 1].astype(F32) + rs1[q, 2].astype(F32))).astype(BF16)
        for s in STEPS:
            second_copy(q, s).start()
    for q in range(2):
        arrived(g2r.at[q], rs2.at[q])
        pos, _ = on(q, True, 1)
        v = midg[q].astype(F32) + rs2[q, 0].astype(F32)
        part4(full.at[c], q, pos)[...] = (v + (rs2[q, 1].astype(F32) + rs2[q, 2].astype(F32))).astype(BF16)
        for s in STEPS:
            third_copy(q, s).start()
        pair_copy(q, 0).start()
    acc4[...] = total_of(pr2, plane2, 16)
    spread_column(acc4, sq_in, qs, qr)
    inv = 1.0 / (jnp.sqrt(whole_sum(acc4[...])) + NORM_EPS)
    for s in (1, 3, 2):
        for q in range(2):
            third_copy(q, s).wait_recv()
            pair_copy(q, 4 - s).start()
    arrived(g5r.at[0], full.at[other])
    for k in range(2):
        at = 0
        for i in range(4):
            for n in range(4 - i):
                j = 2 * (i + n) + k
                block = full[k, at:at + PANEL]
                G[i * PANEL:(i + 1) * PANEL, j * LANES:(j + 1) * LANES] = block
                if n:
                    G[j * LANES:(j + 1) * LANES, i * PANEL:(i + 1) * PANEL] = block.T
                at += PANEL

    def product(lhs, rhs, out, finish):
        for i in range(4):
            low, high = i * PANEL, (i + 1) * PANEL
            v = jnp.dot(lhs[low:high], rhs[:, low:], preferred_element_type=F32)
            v = finish(v, slice(low, high), slice(low, FF)).astype(BF16)
            out[low:high, low:] = v
            for j in range(i + 1, 4):
                out[j * PANEL:(j + 1) * PANEL, low:high] = v[:, (j - i) * PANEL:(j - i + 1) * PANEL].T

    def polynomial(src, q, t, out, scale):
        b_s = COEF_B * scale
        c_s = COEF_C * scale * scale
        product(src, src, q, lambda v, i, j: b_s * src[i, j].astype(F32) + c_s * v)
        product(src, q, t, lambda v, i, j: scale * (COEF_A * src[i, j].astype(F32) + v))
        product(t, q, out, lambda v, i, j: COEF_A * t[i, j].astype(F32) + v)

    def advance(src, rhs, scale):
        v = src[...]
        w = scale * (COEF_A * v.astype(F32) + jnp.dot(v, rhs[...], preferred_element_type=F32))
        return w.astype(BF16)

    for n in range(2):
        X2[0, n * BLOCK:(n + 1) * BLOCK] = X[2 * c + n]
    polynomial(G, A, B, T, inv * inv)
    X2[1] = advance(X2.at[0], A, inv)
    polynomial(T, A, B, G, 1.0)
    X2[0] = advance(X2.at[1], A, 1.0)
    v = X2[0]
    w = jnp.dot(v, G[...], preferred_element_type=F32).astype(BF16)
    z = jnp.dot(w, G[...], preferred_element_type=F32)
    z = (COEF_A * v.astype(F32) + COEF_B * w.astype(F32) + COEF_C * z).astype(BF16)

    def return_copy(n, dc):
        src = back.at[n, lax.rem(c + dc, 2)]
        return remote(src, ret.at[e], bs.at[n, dc], br.at[e], target(2 * c + n, x, y, lax.rem(c + dc, 2)))

    def return_local(n):
        return pltpu.make_async_copy(back.at[n, c], ret.at[e], bl.at[0])

    def return_in(m):
        return remote(back.at[0, 0], ret.at[m], bs.at[0, 0], br.at[m], in_column(0, 1))

    for n in range(2):
        for h in range(2):
            for k in range(2):
                top = n * BLOCK + h * ROWS
                back[n, h, k * ROWS:(k + 1) * ROWS] = z[top:top + ROWS, k * HALF:(k + 1) * HALF]
        return_copy(n, 1).start()

        @pl.when(2 * c + n != e)
        def _():
            return_copy(n, 0).start()

        @pl.when(2 * c + n == e)
        def _():
            return_local(n).start()

    arrived(z2r.at[0], zin2.at[pl.ds(0, 7)])
    slot_copy(0, 0).wait()

    def momentum(i, carry):
        for h in range(2):
            cols = pl.ds(h * HALF, HALF)
            buf[i, :, cols] = MOMENT * buf[i, :, cols] + factor * zin2[2 * i + h].astype(F32)
        return carry

    lax.fori_loop(0, GROUPS, momentum, 0)
    new_own = pltpu.make_async_copy(buf.at[:, mine_rows], new_mom.at[c], ns.at[0])
    new_sib = remote(buf.at[:, other_rows], new_mom.at[c], ns.at[1], ns.at[2], in_column(0, 1))
    new_sib.start()
    new_own.start()

    arrived(qr.at[0], sq_in.at[pl.ds(0, 7)])
    lane = lax.broadcasted_iota(jnp.int32, (8, LANES), 1)
    mean_sq = jnp.zeros((8, LANES), F32)
    for m in range(MATS):
        mean_sq = mean_sq + jnp.where(lane == m, whole_sum(sq_in[2 * m]) / float(D * FF), 0.0)
    rms_out[...] = jnp.sqrt(mean_sq)

    mom_pass.wait_send()
    mom_sib.wait_send()
    left(g1s.at[0], rs1)
    left(g2s.at[0], rs2)
    left(g3s.at[0], rs1)
    left(g5s.at[0], full.at[0])
    left(z2s.at[0], zout.at[pl.ds(0, 7)])
    left(cs.at[0], column.at[pl.ds(0, 7)])
    left(ps.at[0], plane.at[pl.ds(0, 15)])
    left(ps2.at[0], plane2.at[pl.ds(0, 15)])
    left(qs.at[0], sq_in.at[pl.ds(0, 7)])
    for dz in (0, 1, 3, 2):
        m = wrap(e + dz)
        if dz:
            return_in(m).wait_recv()
        else:
            @pl.when(e // 2 == c)
            def _():
                return_local(0).wait()

            @pl.when(e // 2 != c)
            def _():
                return_in(m).wait_recv()
        v = ret[m].astype(F32)
        rows_out[m, :, :HALF] = v[:ROWS].astype(BF16)
        rows_out[m, :, HALF:] = v[ROWS:].astype(BF16)
    for n in range(2):
        return_copy(n, 1).wait_send()

        @pl.when(2 * c + n != e)
        def _():
            return_copy(n, 0).wait_send()

    new_own.wait()
    new_sib.wait()


ANY = pl.BlockSpec(memory_space=pl.ANY)
VMEM = pl.BlockSpec(memory_space=pltpu.VMEM)
SMEM = pl.BlockSpec(memory_space=pltpu.SMEM)
DMA = pltpu.SemaphoreType.DMA


def per_device(grad_terms, momentum, weights, owner_list):
    small = (CHUNKS, MATS, STRIP, HALF)
    large = (CHUNKS, MATS, SIDE, STRIP, HALF)
    whole = (MATS, SIDE, SIDE, BLOCK, HALF)
    tile = pltpu.VMEM((8, LANES), F32)
    square = pltpu.VMEM((FF, FF), BF16)
    new_mom, rows, rms = pl.pallas_call(
        muon_kernel,
        name="muon",
        out_shape=(
            jax.ShapeDtypeStruct((SLOTS, GROUPS, ROWS, FF), F32),
            jax.ShapeDtypeStruct((MATS, ROWS, FF), BF16),
            jax.ShapeDtypeStruct((8, LANES), F32),
        ),
        in_specs=[SMEM, ANY, ANY],
        out_specs=(ANY, VMEM, VMEM),
        scratch_shapes=[
            pltpu.VMEM(whole, BF16), pltpu.VMEM(whole, BF16),
            pltpu.VMEM(large, BF16), pltpu.VMEM((CHUNKS, MATS, 2, SIDE, STRIP, HALF), BF16), pltpu.VMEM(large, BF16),
            pltpu.VMEM(small, BF16), pltpu.VMEM((CHUNKS, MATS, 2, STRIP, HALF), BF16),
            pltpu.VMEM((MATS, BLOCK, HALF), BF16),
            pltpu.VMEM((GROUPS * 2, BLOCK, HALF), BF16),
            pltpu.VMEM((GROUPS * SLOTS, BLOCK, HALF), BF16),
            pltpu.VMEM((GROUPS * 2, BLOCK, HALF), BF16),
            pltpu.VMEM((SLOTS, GROUPS, ROWS, FF), F32),
            pltpu.VMEM((4, GROUPS, BLOCK, HALF), BF16), pltpu.VMEM((4, GROUPS, BLOCK, HALF), BF16),
            pltpu.VMEM((2, GROUPS, BLOCK, HALF), BF16),
            pltpu.VMEM((GROUPS, 2, BLOCK, HALF), BF16),
            pltpu.VMEM((GROUPS * BLOCK, HALF), BF16), pltpu.VMEM((GROUPS * BLOCK, HALF), BF16),
            pltpu.VMEM((3, 32 * PART, LANES), F32),
            pltpu.VMEM((GROUPS, BLOCK, FF), F32),
            pltpu.VMEM((GROUPS, BLOCK, FF), BF16),
            pltpu.VMEM((2, 2 * BLOCK, FF), BF16),
            pltpu.VMEM((32 * PART, LANES), BF16), pltpu.VMEM((2, 32 * PART, LANES), BF16),
            pltpu.VMEM((2, 3, 4 * PART, LANES), BF16),
            pltpu.VMEM((2, 4 * PART, LANES), BF16),
            pltpu.VMEM((2, 3, 4 * PART, LANES), BF16),
            square, square, square, square,
            pltpu.VMEM((2, 2, BLOCK, HALF), BF16), pltpu.VMEM((MATS, BLOCK, HALF), BF16),
            tile, tile, tile, tile,
            pltpu.VMEM((8, 8, LANES), F32), pltpu.VMEM((16, 8, LANES), F32), pltpu.VMEM((16, 8, LANES), F32),
            pltpu.VMEM((8, 8, LANES), F32),
            DMA((CHUNKS,)), DMA((1,)), DMA((CHUNKS, MATS)),
            DMA((3,)), DMA((CHUNKS,)), DMA((CHUNKS,)), DMA((3,)), DMA((CHUNKS,)), DMA((CHUNKS,)),
            DMA((1,)), DMA((1,)), DMA((1,)), DMA((4,)), DMA((1,)), DMA((1,)), DMA((2,)),
            DMA((1,)), DMA((1,)), DMA((1,)), DMA((1,)), DMA((3,)),
            DMA((1,)), DMA((2,)), DMA((1,)), DMA((2,)), DMA((1,)), DMA((2, 3)), DMA((1,)), DMA((1,)),
            DMA((1,)), DMA((1,)), DMA((1,)), DMA((1,)), DMA((1,)), DMA((1,)), DMA((1,)), DMA((2, 2)), DMA((4,)),
            DMA((1,)),
        ],
        compiler_params=pltpu.CompilerParams(collective_id=0, has_side_effects=True, vmem_limit_bytes=60 << 20),
    )(owner_list, grad_terms.reshape(MATS, SIDE, SIDE, BLOCK, FF), momentum[0])

    rows = rows.astype(F32)
    scale_rms = 0.2 * math.sqrt(max(D, FF))
    update = (scale_rms * rows).astype(BF16)
    new_weights = weights * (1.0 - LEARN * DECAY) - LEARN * scale_rms * rows
    return (new_weights, update, new_mom[None], rms[0, :MATS])


def solution(mesh):
    placed = (
        P("dp", None, "expert", None),
        P("expert", None, None, "dp", None),
        P(None, ("expert", "dp"), None),
        P(),
    )
    return jax.shard_map(
        per_device,
        mesh=mesh,
        in_specs=placed,
        out_specs=(
            P(None, ("expert", "dp"), None),
            P(None, ("expert", "dp"), None),
            P("expert", None, None, "dp", None),
            P(),
        ),
        check_vma=False,
    )
```

```python
import math

import jax
import jax.numpy as jnp
from jax import lax
from jax.experimental import pallas as pl
from jax.experimental.pallas import tpu as pltpu
from jax.sharding import PartitionSpec as P

D = 7168
FF = 1024
MATS = 4
SLOTS = 2
GROUPS = 4
SIDE = 4
BLOCK = 112
ROWS = 56
HALF = FF // 2
LANES = 128
STRIP = 16
CHUNKS = BLOCK // STRIP
LAST = CHUNKS - 1
SHORT = 5
PANEL = 256
PART = 80

MOMENT = 0.95
CLIP_RMS = 1.0
LEARN = 0.1
DECAY = 0.1
COEF_A = 3.4445
COEF_B = -4.775
COEF_C = 2.0315
NORM_EPS = 1e-07
MEAN_EPS = 1e-06
F32 = jnp.float32
BF16 = jnp.bfloat16

COLUMN = ((2, 0), (2, 1), (1, 0), (1, 1), (3, 0), (3, 1), (0, 1))
PLANE = tuple((dx, dy) for dx in range(4) for dy in range(4) if dx + dy)


def wrap(v):
    return lax.rem(v + 4, 4)


def remote(src, dst, send, recv, device):
    return pltpu.make_async_remote_copy(src_ref=src, dst_ref=dst, send_sem=send, recv_sem=recv, device_id=device)


def whole_sum(v):
    return jnp.sum(jnp.sum(v, axis=0, keepdims=True), axis=1, keepdims=True)


def sign(m):
    return 1 if m % 2 else -1


def muon_kernel(owners, g, mom, new_mom, rows_out, rms_out,
                own, sib, tr1, dc1, mid, tr2, dc2, grad, zin, zout, zin2, momv, mout, min_, mall, Mb, gright, mright, grams, buf, X, X2,
                packed, full, rs1, midg, rs2, G, A, B, T, back, ret, acc, acc2, acc3, acc4,
                column, plane, plane2, sq_in,
                own_s, sib_s, sib_r, s1, t1r, d1r, s2, t2r, d2r, zs, zr, zl, ms, m1s, m1r, m2s, cs, cr, ps, pr, ns, g1s, g1r,
                g2s, g2r, g3s, g3r, g5s, g5r, ps2, pr2, qs, qr, z2s, z2r, z2l, bs, br, bl):
    e = lax.axis_index("expert")
    p = lax.axis_index("dp")
    x, y, c = p // 8, (p // 2) % 4, p % 2
    other = 1 - c

    def target(te, tx, ty, tc):
        return {"expert": te, "dp": tx * 8 + ty * 2 + tc}

    def in_column(dz, dc):
        return target(wrap(e + dz), x, y, lax.rem(c + dc, 2))

    def in_plane(dx, dy):
        return target(e, wrap(x + dx), wrap(y + dy), c)

    def arrived(sem, ref):
        remote(ref, ref, sem, sem, in_column(0, 1)).wait_recv()

    def left(sem, ref):
        remote(ref, ref, sem, sem, in_column(0, 1)).wait_send()

    places = []
    for m in range(MATS):
        number = jnp.int32(0)
        for m2 in range(m):
            number = number + jnp.where(owners[m2] == owners[m], 1, 0)
        places.append(owners[m] * SLOTS + number)

    def mask(m, slot):
        return jnp.where(places[m] == slot, 1.0, 0.0).astype(F32)

    def strip(k):
        return pl.ds(pl.multiple_of(k * STRIP, STRIP), STRIP)

    def own_copy(k):
        cols = pl.ds(pl.multiple_of(c * HALF, HALF), HALF)
        return pltpu.make_async_copy(g.at[:, :, :, strip(k), cols], own.at[:, :, :, strip(k)], own_s.at[k])

    def sib_copy(k, m):
        cols = pl.ds(pl.multiple_of(other * HALF, HALF), HALF)
        return remote(g.at[m, :, :, strip(k), cols], sib.at[m, :, :, strip(k)], sib_s.at[0], sib_r.at[k, m],
                      in_column(0, 1))

    def along(m, first, step):
        on_x = (m < 2) == first
        return (x, in_plane(step, 0)) if on_x else (y, in_plane(0, step))

    def group(ref, k, m, i):
        return ref.at[m, i, :, strip(k)] if m < 2 else ref.at[m, :, i, strip(k)]

    def copy1(k, m, which):
        d = sign(m)
        pos, dev = along(m, True, -d if which == 1 else d)
        i = wrap(pos + (2, -d, d)[which])
        if which == 0:
            dst, recv = tr1.at[k, m], t1r.at[k]
        else:
            dst, recv = dc1.at[k, m, which - 1], d1r.at[k]
        return remote(group(own, k, m, i), dst, s1.at[which], recv, dev)

    def ends2(k, m, which):
        if which == 0:
            return tr2.at[k, m], s2.at[0], t2r.at[k]
        return dc2.at[k, m, which - 1], s2.at[which], d2r.at[k]

    def copy2(k, m, which):
        d = sign(m)
        pos, dev = along(m, False, -d if which == 1 else d)
        i = wrap(pos + (2, -d, d)[which])
        return remote(mid.at[k, m, i], *ends2(k, m, which), dev)

    def copy2_short(k, m, which):
        step = (2, 1, 3)[which]
        pos, dev = along(m, False, step)
        return remote(mid.at[k, m, wrap(pos + step)], *ends2(k, m, which), dev)

    def z_copy(k, dz, dc):
        j = 2 * dz + dc
        src, dst = grad.at[wrap(e + dz), strip(k)], zin.at[2 * e + c, strip(k)]
        if j == 0:
            return pltpu.make_async_copy(src, dst, zl.at[0])
        return remote(src, dst, zs.at[0], zr.at[0], in_column(dz, dc))

    mine_rows = pl.ds(pl.multiple_of(ROWS * c, 8), ROWS)
    other_rows = pl.ds(pl.multiple_of(ROWS * other, 8), ROWS)
    mom_load = pltpu.make_async_copy(mom, momv, ms.at[0])
    mom_own = pltpu.make_async_copy(mom.at[c], buf.at[:, mine_rows], ms.at[1])
    mom_sib = remote(mom.at[other], buf.at[:, mine_rows], ms.at[2], ms.at[3], in_column(0, 1))

    def mom_copy(dz):
        return remote(mout.at[dz], min_.at[e], m1s.at[0], m1r.at[0], in_column(dz, 0))

    mom_pass = remote(mall.at[c], mall.at[c], m2s.at[0], m2s.at[1], in_column(0, 1))

    for k in range(CHUNKS):
        own_copy(k).start()
        if k == 0:
            mom_load.start()
    mom_own.start()
    barrier = pltpu.get_barrier_semaphore()
    for dz, dc in COLUMN:
        pl.semaphore_signal(barrier, inc=1, device_id=in_column(dz, dc))
    for dx, dy in PLANE:
        pl.semaphore_signal(barrier, inc=1, device_id=in_plane(dx, dy))
    pl.semaphore_wait(barrier, len(COLUMN) + len(PLANE))
    for k in range(CHUNKS):
        for m in range(MATS):
            sib_copy(k, m).start()
    acc[...] = jnp.zeros_like(acc)
    acc3[...] = jnp.zeros_like(acc3)

    def pair_sum(k, m, i):
        to, more = group(own, k, m, i), group(sib, k, m, i)
        for j in range(SIDE):
            to[j] = (to[j].astype(F32) + more[j].astype(F32)).astype(BF16)

    def transit(k):
        own_copy(k).wait()
        for m in range(MATS):
            sib_copy(k, m).wait_recv()
            pos, _ = along(m, True, 1)
            pair_sum(k, m, wrap(pos + 2))
            copy1(k, m, 0).start()

    def combine(k):
        arrived(t1r.at[k], tr1.at[k])
        for m in range(MATS):
            pos, _ = along(m, True, 1)
            i = wrap(pos + sign(m))
            to, more, came = group(own, k, m, i), group(sib, k, m, i), tr1.at[k, m]
            for j in range(SIDE):
                to[j] = (to[j].astype(F32) + more[j].astype(F32) + came[j].astype(F32)).astype(BF16)
            copy1(k, m, 2).start()

    def direct(k):
        for m in range(MATS):
            pos, _ = along(m, True, 1)
            pair_sum(k, m, wrap(pos - sign(m)))
            copy1(k, m, 1).start()

    def turn(k):
        arrived(d1r.at[k], dc1.at[k])
        for m in range(MATS):
            pos, _ = along(m, True, 1)
            to, more, came, came2 = group(own, k, m, pos), group(sib, k, m, pos), dc1.at[k, m, 0], dc1.at[k, m, 1]
            for j in range(SIDE):
                v = (to[j].astype(F32) + more[j].astype(F32)) + (came[j].astype(F32) + came2[j].astype(F32))
                mid[k, m, j] = v.astype(BF16)

            @pl.when(k < SHORT)
            def _():
                copy2(k, m, 0).start()
                copy2(k, m, 1).start()

            @pl.when(k >= SHORT)
            def _():
                for which in range(3):
                    copy2_short(k, m, which).start()

    def combine2(k):
        arrived(t2r.at[k], tr2.at[k])
        for m in range(MATS):
            pos, _ = along(m, False, 1)
            i = wrap(pos + sign(m))
            mid[k, m, i] = (mid[k, m, i].astype(F32) + tr2[k, m].astype(F32)).astype(BF16)
            copy2(k, m, 2).start()

    def collect(k, m, v):
        v = v.astype(BF16)
        grad[m, strip(k)] = v
        v = jnp.square(v.astype(F32))
        v = v[:8] + v[8:]
        acc[...] += v[:, :128] + v[:, 128:256] + v[:, 256:384] + v[:, 384:]

    def send_strips(k):
        for dz in (2, 1, 3, 0):
            for dc in range(2):
                z_copy(k, dz, dc).start()

    def finish_sum(k):
        arrived(d2r.at[k], dc2.at[k])
        for m in range(MATS):
            pos, _ = along(m, False, 1)
            collect(k, m, mid[k, m, pos].astype(F32) + (dc2[k, m, 0].astype(F32) + dc2[k, m, 1].astype(F32)))
        send_strips(k)

    def finish_short(k):
        arrived(t2r.at[k], tr2.at[k])
        arrived(d2r.at[k], dc2.at[k])
        for m in range(MATS):
            pos, _ = along(m, False, 1)
            v = mid[k, m, pos].astype(F32) + tr2[k, m].astype(F32)
            collect(k, m, v + (dc2[k, m, 0].astype(F32) + dc2[k, m, 1].astype(F32)))

    def mom_send(k):
        mom_load.wait()
        for dz in (2, 1, 3, 0):
            t = wrap(e + dz)
            first_is = jnp.float32(0)
            second_is = jnp.float32(0)
            for m in range(MATS):
                here = jnp.where(t == m, 1.0, 0.0).astype(F32)
                first_is = first_is + here * mask(m, 2 * e)
                second_is = second_is + here * mask(m, 2 * e + 1)
            for i in range(GROUPS):
                for h in range(2):
                    cols = slice(h * HALF, (h + 1) * HALF)
                    v = first_is * momv[0, i, :, cols] + second_is * momv[1, i, :, cols]
                    mout[dz, i, h * ROWS:(h + 1) * ROWS] = v.astype(BF16)
            if dz:
                mom_copy(dz).start()
        mom_sib.start()

    def mom_sum(k):
        arrived(m1r.at[0], min_.at[pl.ds(0, 3)])
        for i in range(GROUPS):
            v = mout[0, i].astype(F32)
            for dz in (1, 2, 3):
                v = v + min_[wrap(e + dz), i].astype(F32)
            mall[c, i] = v.astype(BF16)
        mom_pass.start()

    def finish_send(k):
        finish_short(k)
        send_strips(k)

    stages = ((transit, 0, 0, CHUNKS), (combine, 1, 0, CHUNKS), (direct, 2, 0, CHUNKS), (turn, 3, 0, CHUNKS),
              (combine2, 4, 0, SHORT), (finish_sum, 5, 0, SHORT), (finish_send, 4, SHORT, LAST), (mom_send, 1, 0, 1),
              (mom_sum, LAST + 2, 0, 1))

    def step(t, carry):
        for stage, lag, low, high in stages:
            if low < high:
                @pl.when((t >= low + lag) & (t < high + lag))
                def _():
                    stage(t - lag)
        return carry

    lax.fori_loop(0, LAST + 5, step, 0)
    finish_short(LAST)

    me_column = 2 * e + c
    me_plane = 4 * x + y

    def spread_column(src, dst, send, recv):
        copies = [remote(src, dst.at[me_column], send.at[0], recv.at[0], in_column(*d)) for d in COLUMN]
        for copy in copies:
            copy.start()
        dst[me_column] = src[...]

    def spread_plane(src, dst, send, recv):
        copies = [remote(src, dst.at[me_plane], send.at[0], recv.at[0], in_plane(*d)) for d in PLANE]
        for copy in copies:
            copy.start()
        dst[me_plane] = src[...]

    def total_of(recv, ref, count):
        arrived(recv.at[0], ref.at[pl.ds(0, count - 1)])
        v = ref[0]
        for j in range(1, count):
            v = v + ref[j]
        return v

    spread_column(acc, column, cs, cr)
    send_strips(LAST)
    acc2[...] = total_of(cr, column, 8)
    spread_plane(acc2, plane, ps, pr)
    mom_pass.wait_recv()
    arrived(zr.at[0], zin.at[pl.ds(0, 7)])
    pltpu.make_async_copy(zin.at[0], zin.at[0], zl.at[0]).wait()

    def unpack(i, carry):
        parts = [mall[k, i].astype(F32) for k in range(2)]
        for h in range(2):
            kept_rows = [v[h * ROWS:(h + 1) * ROWS] for v in parts]
            Mb[i, h] = jnp.concatenate(kept_rows, axis=0).astype(BF16)
        return carry

    lax.fori_loop(0, GROUPS, unpack, 0)
    for j in range(4):
        cols = pl.ds(pl.multiple_of((2 * (j % 2) + c) * LANES, LANES), LANES)
        gright[:, j * LANES:(j + 1) * LANES] = jnp.concatenate([zin[2 * n + j // 2, :, cols] for n in range(GROUPS)], axis=0)
        mright[:, j * LANES:(j + 1) * LANES] = Mb[:, j // 2, :, cols].reshape(GROUPS * BLOCK, LANES)

    def outer(left, right):
        return lax.dot_general(left, right, (((0,), (0,)), ((), ())), preferred_element_type=F32)

    at = 0
    for i in range(4):
        cols = slice((i % 2) * PANEL, (i % 2 + 1) * PANEL)
        gleft = jnp.concatenate([zin[2 * n + i // 2, :, cols] for n in range(GROUPS)], axis=0)
        mleft = Mb[:, i // 2, :, cols].reshape(GROUPS * BLOCK, PANEL)
        gr, mr = gright[:, i * LANES:], mright[:, i * LANES:]
        gg, gm, mm = outer(gleft, gr), outer(gleft, mr) + outer(mleft, gr), outer(mleft, mr)
        for j in range(4 - i):
            for n, v in enumerate((gg, gm, mm)):
                grams[n, at:at + PANEL] = v[:, j * LANES:(j + 1) * LANES]
            at += PANEL
    mean = whole_sum(total_of(pr, plane, 16)) / float(MATS * D * FF)
    factor = jnp.minimum(1.0, CLIP_RMS / jnp.sqrt(mean + MEAN_EPS))


    def part(ref, q, i, b):
        return ref.at[pl.ds(pl.multiple_of((8 * q + 2 * i + b) * 2 * PART, 16), 2 * PART)]

    def on(q, first, step):
        return (x, in_plane(step, 0)) if (q == 0) == first else (y, in_plane(0, step))

    def first_copy(q, step, b):
        pos, dev = on(q, True, step)
        return remote(part(packed, q, wrap(pos + step), b), rs1.at[q, b, step - 1], g1s.at[0], g1r.at[q, b], dev)

    def second_copy(q, step, b):
        _, dev = on(q, False, step)
        return remote(midg.at[q, b], rs2.at[q, b, step - 1], g2s.at[0], g2r.at[q, b], dev)

    def third_copy(q, step, b):
        pos, dev = on(q, True, step)
        ref = part(full.at[c], q, pos, b)
        return remote(ref, ref, g3s.at[0], g3r.at[q, b, step - 1], dev)

    def pair_copy(q, n, b):
        pos, _ = on(q, True, 1)
        ref = part(full.at[c], q, wrap(pos + n), b)
        return remote(ref, ref, g5s.at[0], g5r.at[0], in_column(0, 1))

    STEPS = (2, 1, 3)
    u = (1.0 + MOMENT) * factor
    w = MOMENT * MOMENT
    for q in range(2):
        def weigh(i, carry):
            rows = pl.ds(pl.multiple_of((16 * q + i) * PART, 16), PART)
            v = (u * u) * grams[0, rows] + (u * w) * grams[1, rows] + (w * w) * grams[2, rows]
            packed[rows] = v.astype(BF16)
            return carry

        lax.fori_loop(0, 16, weigh, 0)
        for s in STEPS:
            first_copy(q, s, 0).start()
    for q in range(2):
        for s in STEPS:
            first_copy(q, s, 1).start()

    def direction(i, carry):
        for h in range(2):
            v = factor * zin[2 * i + h].astype(F32)
            v = v + MOMENT * (MOMENT * Mb[i, h].astype(F32) + v)
            X[i, :, h * HALF:(h + 1) * HALF] = v.astype(BF16)
            sq = jnp.sum(jnp.square(v).reshape(BLOCK // 8, 8, HALF), axis=0)
            acc3[...] += sq[:, :128] + sq[:, 128:256] + sq[:, 256:384] + sq[:, 384:]
        return carry

    lax.fori_loop(0, GROUPS, direction, 0)

    spread_plane(acc3, plane2, ps2, pr2)
    mom_own.wait()
    mom_sib.wait_recv()

    def slot_copy(dz, dc):
        j = 2 * dz + dc
        if j == 0:
            return pltpu.make_async_copy(zout.at[0], zin2.at[2 * e + c], z2l.at[0])
        return remote(zout.at[j], zin2.at[2 * e + c], z2s.at[0], z2r.at[0], in_column(dz, dc))

    for dz in (2, 1, 3, 0):
        for dc in range(2):
            slot = wrap(e + dz) * SLOTS + lax.rem(c + dc, 2)
            v = mask(0, slot) * grad[0].astype(F32)
            for m in range(1, MATS):
                v = v + mask(m, slot) * grad[m].astype(F32)
            zout[2 * dz + dc] = v.astype(BF16)
            slot_copy(dz, dc).start()

    left(sib_s.at[0], sib)
    for which in range(3):
        left(s1.at[which], tr1)
        left(s2.at[which], tr2)
    left(zs.at[0], zin.at[pl.ds(0, 7)])
    left(m1s.at[0], mout.at[pl.ds(0, 3)])
    halves = [(q, b) for b in range(2) for q in range(2)]
    for q, b in halves:
        arrived(g1r.at[q, b], rs1.at[q, b])
        pos, _ = on(q, True, 1)
        v = part(packed, q, pos, b)[...].astype(F32) + rs1[q, b, 0].astype(F32)
        midg[q, b] = (v + (rs1[q, b, 1].astype(F32) + rs1[q, b, 2].astype(F32))).astype(BF16)
        for s in STEPS:
            second_copy(q, s, b).start()
    for q, b in halves:
        arrived(g2r.at[q, b], rs2.at[q, b])
        pos, _ = on(q, True, 1)
        v = midg[q, b].astype(F32) + rs2[q, b, 0].astype(F32)
        part(full.at[c], q, pos, b)[...] = (v + (rs2[q, b, 1].astype(F32) + rs2[q, b, 2].astype(F32))).astype(BF16)
        for s in STEPS:
            third_copy(q, s, b).start()
        pair_copy(q, 0, b).start()
    acc4[...] = total_of(pr2, plane2, 16)
    spread_column(acc4, sq_in, qs, qr)
    inv = 1.0 / (jnp.sqrt(whole_sum(acc4[...])) + NORM_EPS)
    for b in range(2):
        for s in (1, 3, 2):
            for q in range(2):
                third_copy(q, s, b).wait_recv()
                pair_copy(q, 4 - s, b).start()
    arrived(g5r.at[0], full.at[other])
    for k in range(2):
        at = 0
        for i in range(4):
            for n in range(4 - i):
                j = 2 * (i + n) + k
                block = full[k, at:at + PANEL]
                G[i * PANEL:(i + 1) * PANEL, j * LANES:(j + 1) * LANES] = block
                if n:
                    G[j * LANES:(j + 1) * LANES, i * PANEL:(i + 1) * PANEL] = block.T
                at += PANEL

    def product(lhs, rhs, out, finish):
        for i in range(4):
            low, high = i * PANEL, (i + 1) * PANEL
            v = jnp.dot(lhs[low:high], rhs[:, low:], preferred_element_type=F32)
            v = finish(v, slice(low, high), slice(low, FF)).astype(BF16)
            out[low:high, low:] = v
            for j in range(i + 1, 4):
                out[j * PANEL:(j + 1) * PANEL, low:high] = v[:, (j - i) * PANEL:(j - i + 1) * PANEL].T

    def polynomial(src, q, t, out, scale):
        b_s = COEF_B * scale
        c_s = COEF_C * scale * scale
        product(src, src, q, lambda v, i, j: b_s * src[i, j].astype(F32) + c_s * v)
        product(src, q, t, lambda v, i, j: scale * (COEF_A * src[i, j].astype(F32) + v))
        product(t, q, out, lambda v, i, j: COEF_A * t[i, j].astype(F32) + v)

    def advance(src, rhs, scale):
        v = src[...]
        w = scale * (COEF_A * v.astype(F32) + jnp.dot(v, rhs[...], preferred_element_type=F32))
        return w.astype(BF16)

    for n in range(2):
        X2[0, n * BLOCK:(n + 1) * BLOCK] = X[2 * c + n]
    polynomial(G, A, B, T, inv * inv)
    X2[1] = advance(X2.at[0], A, inv)
    polynomial(T, A, B, G, 1.0)
    X2[0] = advance(X2.at[1], A, 1.0)
    v = X2[0]
    w = jnp.dot(v, G[...], preferred_element_type=F32).astype(BF16)
    z = jnp.dot(w, G[...], preferred_element_type=F32)
    z = (COEF_A * v.astype(F32) + COEF_B * w.astype(F32) + COEF_C * z).astype(BF16)

    def return_copy(n, dc):
        src = back.at[n, lax.rem(c + dc, 2)]
        return remote(src, ret.at[e], bs.at[n, dc], br.at[e], target(2 * c + n, x, y, lax.rem(c + dc, 2)))

    def return_local(n):
        return pltpu.make_async_copy(back.at[n, c], ret.at[e], bl.at[0])

    def return_in(m):
        return remote(back.at[0, 0], ret.at[m], bs.at[0, 0], br.at[m], in_column(0, 1))

    for n in range(2):
        for h in range(2):
            for k in range(2):
                top = n * BLOCK + h * ROWS
                back[n, h, k * ROWS:(k + 1) * ROWS] = z[top:top + ROWS, k * HALF:(k + 1) * HALF]
        return_copy(n, 1).start()

        @pl.when(2 * c + n != e)
        def _():
            return_copy(n, 0).start()

        @pl.when(2 * c + n == e)
        def _():
            return_local(n).start()

    arrived(z2r.at[0], zin2.at[pl.ds(0, 7)])
    slot_copy(0, 0).wait()

    def momentum(i, carry):
        for h in range(2):
            cols = pl.ds(h * HALF, HALF)
            buf[i, :, cols] = MOMENT * buf[i, :, cols] + factor * zin2[2 * i + h].astype(F32)
        return carry

    lax.fori_loop(0, GROUPS, momentum, 0)
    new_own = pltpu.make_async_copy(buf.at[:, mine_rows], new_mom.at[c], ns.at[0])
    new_sib = remote(buf.at[:, other_rows], new_mom.at[c], ns.at[1], ns.at[2], in_column(0, 1))
    new_sib.start()
    new_own.start()

    arrived(qr.at[0], sq_in.at[pl.ds(0, 7)])
    lane = lax.broadcasted_iota(jnp.int32, (8, LANES), 1)
    mean_sq = jnp.zeros((8, LANES), F32)
    for m in range(MATS):
        mean_sq = mean_sq + jnp.where(lane == m, whole_sum(sq_in[2 * m]) / float(D * FF), 0.0)
    rms_out[...] = jnp.sqrt(mean_sq)

    mom_pass.wait_send()
    mom_sib.wait_send()
    left(g1s.at[0], rs1)
    left(g2s.at[0], rs2)
    left(g3s.at[0], rs1)
    left(g5s.at[0], full.at[0])
    left(z2s.at[0], zout.at[pl.ds(0, 7)])
    left(cs.at[0], column.at[pl.ds(0, 7)])
    left(ps.at[0], plane.at[pl.ds(0, 15)])
    left(ps2.at[0], plane2.at[pl.ds(0, 15)])
    left(qs.at[0], sq_in.at[pl.ds(0, 7)])
    for dz in (0, 1, 3, 2):
        m = wrap(e + dz)
        if dz:
            return_in(m).wait_recv()
        else:
            @pl.when(e // 2 == c)
            def _():
                return_local(0).wait()

            @pl.when(e // 2 != c)
            def _():
                return_in(m).wait_recv()
        v = ret[m].astype(F32)
        rows_out[m, :, :HALF] = v[:ROWS].astype(BF16)
        rows_out[m, :, HALF:] = v[ROWS:].astype(BF16)
    for n in range(2):
        return_copy(n, 1).wait_send()

        @pl.when(2 * c + n != e)
        def _():
            return_copy(n, 0).wait_send()

    new_own.wait()
    new_sib.wait()


ANY = pl.BlockSpec(memory_space=pl.ANY)
VMEM = pl.BlockSpec(memory_space=pltpu.VMEM)
SMEM = pl.BlockSpec(memory_space=pltpu.SMEM)
DMA = pltpu.SemaphoreType.DMA


def per_device(grad_terms, momentum, weights, owner_list):
    small = (CHUNKS, MATS, STRIP, HALF)
    large = (CHUNKS, MATS, SIDE, STRIP, HALF)
    whole = (MATS, SIDE, SIDE, BLOCK, HALF)
    tile = pltpu.VMEM((8, LANES), F32)
    square = pltpu.VMEM((FF, FF), BF16)
    new_mom, rows, rms = pl.pallas_call(
        muon_kernel,
        name="muon",
        out_shape=(
            jax.ShapeDtypeStruct((SLOTS, GROUPS, ROWS, FF), F32),
            jax.ShapeDtypeStruct((MATS, ROWS, FF), BF16),
            jax.ShapeDtypeStruct((8, LANES), F32),
        ),
        in_specs=[SMEM, ANY, ANY],
        out_specs=(ANY, VMEM, VMEM),
        scratch_shapes=[
            pltpu.VMEM(whole, BF16), pltpu.VMEM(whole, BF16),
            pltpu.VMEM(large, BF16), pltpu.VMEM((CHUNKS, MATS, 2, SIDE, STRIP, HALF), BF16), pltpu.VMEM(large, BF16),
            pltpu.VMEM(small, BF16), pltpu.VMEM((CHUNKS, MATS, 2, STRIP, HALF), BF16),
            pltpu.VMEM((MATS, BLOCK, HALF), BF16),
            pltpu.VMEM((GROUPS * 2, BLOCK, HALF), BF16),
            pltpu.VMEM((GROUPS * SLOTS, BLOCK, HALF), BF16),
            pltpu.VMEM((GROUPS * 2, BLOCK, HALF), BF16),
            pltpu.VMEM((SLOTS, GROUPS, ROWS, FF), F32),
            pltpu.VMEM((4, GROUPS, BLOCK, HALF), BF16), pltpu.VMEM((4, GROUPS, BLOCK, HALF), BF16),
            pltpu.VMEM((2, GROUPS, BLOCK, HALF), BF16),
            pltpu.VMEM((GROUPS, 2, BLOCK, HALF), BF16),
            pltpu.VMEM((GROUPS * BLOCK, HALF), BF16), pltpu.VMEM((GROUPS * BLOCK, HALF), BF16),
            pltpu.VMEM((3, 32 * PART, LANES), F32),
            pltpu.VMEM((GROUPS, BLOCK, FF), F32),
            pltpu.VMEM((GROUPS, BLOCK, FF), BF16),
            pltpu.VMEM((2, 2 * BLOCK, FF), BF16),
            pltpu.VMEM((32 * PART, LANES), BF16), pltpu.VMEM((2, 32 * PART, LANES), BF16),
            pltpu.VMEM((2, 2, 3, 2 * PART, LANES), BF16),
            pltpu.VMEM((2, 2, 2 * PART, LANES), BF16),
            pltpu.VMEM((2, 2, 3, 2 * PART, LANES), BF16),
            square, square, square, square,
            pltpu.VMEM((2, 2, BLOCK, HALF), BF16), pltpu.VMEM((MATS, BLOCK, HALF), BF16),
            tile, tile, tile, tile,
            pltpu.VMEM((8, 8, LANES), F32), pltpu.VMEM((16, 8, LANES), F32), pltpu.VMEM((16, 8, LANES), F32),
            pltpu.VMEM((8, 8, LANES), F32),
            DMA((CHUNKS,)), DMA((1,)), DMA((CHUNKS, MATS)),
            DMA((3,)), DMA((CHUNKS,)), DMA((CHUNKS,)), DMA((3,)), DMA((CHUNKS,)), DMA((CHUNKS,)),
            DMA((1,)), DMA((1,)), DMA((1,)), DMA((4,)), DMA((1,)), DMA((1,)), DMA((2,)),
            DMA((1,)), DMA((1,)), DMA((1,)), DMA((1,)), DMA((3,)),
            DMA((1,)), DMA((2, 2)), DMA((1,)), DMA((2, 2)), DMA((1,)), DMA((2, 2, 3)), DMA((1,)), DMA((1,)),
            DMA((1,)), DMA((1,)), DMA((1,)), DMA((1,)), DMA((1,)), DMA((1,)), DMA((1,)), DMA((2, 2)), DMA((4,)),
            DMA((1,)),
        ],
        compiler_params=pltpu.CompilerParams(collective_id=0, has_side_effects=True, vmem_limit_bytes=60 << 20),
    )(owner_list, grad_terms.reshape(MATS, SIDE, SIDE, BLOCK, FF), momentum[0])

    rows = rows.astype(F32)
    scale_rms = 0.2 * math.sqrt(max(D, FF))
    update = (scale_rms * rows).astype(BF16)
    new_weights = weights * (1.0 - LEARN * DECAY) - LEARN * scale_rms * rows
    return (new_weights, update, new_mom[None], rms[0, :MATS])


def solution(mesh):
    placed = (
        P("dp", None, "expert", None),
        P("expert", None, None, "dp", None),
        P(None, ("expert", "dp"), None),
        P(),
    )
    return jax.shard_map(
        per_device,
        mesh=mesh,
        in_specs=placed,
        out_specs=(
            P(None, ("expert", "dp"), None),
            P(None, ("expert", "dp"), None),
            P("expert", None, None, "dp", None),
            P(),
        ),
        check_vma=False,
    )
```

```python
import math

import jax
import jax.numpy as jnp
from jax import lax
from jax.experimental import pallas as pl
from jax.experimental.pallas import tpu as pltpu
from jax.sharding import PartitionSpec as P

D = 7168
FF = 1024
MATS = 4
SLOTS = 2
GROUPS = 4
SIDE = 4
BLOCK = 112
ROWS = 56
HALF = FF // 2
LANES = 128
STRIP = 16
CHUNKS = BLOCK // STRIP
LAST = CHUNKS - 1
SHORT = 5
PANEL = 256
PART = 80

MOMENT = 0.95
CLIP_RMS = 1.0
LEARN = 0.1
DECAY = 0.1
COEF_A = 3.4445
COEF_B = -4.775
COEF_C = 2.0315
NORM_EPS = 1e-07
MEAN_EPS = 1e-06
F32 = jnp.float32
BF16 = jnp.bfloat16

COLUMN = ((2, 0), (2, 1), (1, 0), (1, 1), (3, 0), (3, 1), (0, 1))
PLANE = tuple((dx, dy) for dx in range(4) for dy in range(4) if dx + dy)


def wrap(v):
    return lax.rem(v + 4, 4)


def remote(src, dst, send, recv, device):
    return pltpu.make_async_remote_copy(src_ref=src, dst_ref=dst, send_sem=send, recv_sem=recv, device_id=device)


def whole_sum(v):
    return jnp.sum(jnp.sum(v, axis=0, keepdims=True), axis=1, keepdims=True)


def sign(m):
    return 1 if m % 2 else -1


def muon_kernel(owners, g, mom, new_mom, rows_out, rms_out,
                own, sib, tr1, dc1, mid, tr2, dc2, grad, zin, zout, zin2, momv, mout, min_, mall, Mb, gright, mright, grams, buf, X, X2,
                packed, full, rs1, midg, rs2, G, A, B, T, back, ret, acc, acc2, acc3, acc4,
                column, plane, plane2, sq_in,
                own_s, sib_s, sib_r, s1, t1r, d1r, s2, t2r, d2r, zs, zr, zl, ms, m1s, m1r, m2s, cs, cr, ps, pr, ns, g1s, g1r,
                g2s, g2r, g3s, g3r, g5s, g5r, ps2, pr2, qs, qr, z2s, z2r, z2l, bs, br, bl):
    e = lax.axis_index("expert")
    p = lax.axis_index("dp")
    x, y, c = p // 8, (p // 2) % 4, p % 2
    other = 1 - c

    def target(te, tx, ty, tc):
        return {"expert": te, "dp": tx * 8 + ty * 2 + tc}

    def in_column(dz, dc):
        return target(wrap(e + dz), x, y, lax.rem(c + dc, 2))

    def in_plane(dx, dy):
        return target(e, wrap(x + dx), wrap(y + dy), c)

    def arrived(sem, ref):
        remote(ref, ref, sem, sem, in_column(0, 1)).wait_recv()

    def left(sem, ref):
        remote(ref, ref, sem, sem, in_column(0, 1)).wait_send()

    places = []
    for m in range(MATS):
        number = jnp.int32(0)
        for m2 in range(m):
            number = number + jnp.where(owners[m2] == owners[m], 1, 0)
        places.append(owners[m] * SLOTS + number)

    def mask(m, slot):
        return jnp.where(places[m] == slot, 1.0, 0.0).astype(F32)

    def strip(k):
        return pl.ds(pl.multiple_of(k * STRIP, STRIP), STRIP)

    def own_copy(k):
        cols = pl.ds(pl.multiple_of(c * HALF, HALF), HALF)
        return pltpu.make_async_copy(g.at[:, :, :, strip(k), cols], own.at[:, :, :, strip(k)], own_s.at[k])

    def sib_copy(k, m):
        cols = pl.ds(pl.multiple_of(other * HALF, HALF), HALF)
        return remote(g.at[m, :, :, strip(k), cols], sib.at[m, :, :, strip(k)], sib_s.at[0], sib_r.at[k, m],
                      in_column(0, 1))

    def along(m, first, step):
        on_x = (m < 2) == first
        return (x, in_plane(step, 0)) if on_x else (y, in_plane(0, step))

    def group(ref, k, m, i):
        return ref.at[m, i, :, strip(k)] if m < 2 else ref.at[m, :, i, strip(k)]

    def copy1(k, m, which):
        d = sign(m)
        pos, dev = along(m, True, -d if which == 1 else d)
        i = wrap(pos + (2, -d, d)[which])
        if which == 0:
            dst, recv = tr1.at[k, m], t1r.at[k]
        else:
            dst, recv = dc1.at[k, m, which - 1], d1r.at[k]
        return remote(group(own, k, m, i), dst, s1.at[which], recv, dev)

    def ends2(k, m, which):
        if which == 0:
            return tr2.at[k, m], s2.at[0], t2r.at[k]
        return dc2.at[k, m, which - 1], s2.at[which], d2r.at[k]

    def copy2(k, m, which):
        d = sign(m)
        pos, dev = along(m, False, -d if which == 1 else d)
        i = wrap(pos + (2, -d, d)[which])
        return remote(mid.at[k, m, i], *ends2(k, m, which), dev)

    def copy2_short(k, m, which):
        step = (2, 1, 3)[which]
        pos, dev = along(m, False, step)
        return remote(mid.at[k, m, wrap(pos + step)], *ends2(k, m, which), dev)

    def z_copy(k, dz, dc):
        j = 2 * dz + dc
        src, dst = grad.at[wrap(e + dz), strip(k)], zin.at[2 * e + c, strip(k)]
        if j == 0:
            return pltpu.make_async_copy(src, dst, zl.at[0])
        return remote(src, dst, zs.at[0], zr.at[0], in_column(dz, dc))

    mine_rows = pl.ds(pl.multiple_of(ROWS * c, 8), ROWS)
    other_rows = pl.ds(pl.multiple_of(ROWS * other, 8), ROWS)
    mom_load = pltpu.make_async_copy(mom, momv, ms.at[0])
    mom_own = pltpu.make_async_copy(mom.at[c], buf.at[:, mine_rows], ms.at[1])
    mom_sib = remote(mom.at[other], buf.at[:, mine_rows], ms.at[2], ms.at[3], in_column(0, 1))

    def mom_copy(dz):
        return remote(mout.at[dz], min_.at[e], m1s.at[0], m1r.at[0], in_column(dz, 0))

    mom_pass = remote(mall.at[c], mall.at[c], m2s.at[0], m2s.at[1], in_column(0, 1))

    for k in range(CHUNKS):
        own_copy(k).start()
        if k == 0:
            mom_load.start()
    mom_own.start()
    barrier = pltpu.get_barrier_semaphore()
    for dz, dc in COLUMN:
        pl.semaphore_signal(barrier, inc=1, device_id=in_column(dz, dc))
    for dx, dy in PLANE:
        pl.semaphore_signal(barrier, inc=1, device_id=in_plane(dx, dy))
    pl.semaphore_wait(barrier, len(COLUMN) + len(PLANE))
    for k in range(CHUNKS):
        for m in range(MATS):
            sib_copy(k, m).start()
    acc[...] = jnp.zeros_like(acc)
    acc3[...] = jnp.zeros_like(acc3)

    def pair_sum(k, m, i):
        to, more = group(own, k, m, i), group(sib, k, m, i)
        for j in range(SIDE):
            to[j] = (to[j].astype(F32) + more[j].astype(F32)).astype(BF16)

    def transit(k):
        own_copy(k).wait()
        for m in range(MATS):
            sib_copy(k, m).wait_recv()
            pos, _ = along(m, True, 1)
            pair_sum(k, m, wrap(pos + 2))
            copy1(k, m, 0).start()

    def combine(k):
        arrived(t1r.at[k], tr1.at[k])
        for m in range(MATS):
            pos, _ = along(m, True, 1)
            i = wrap(pos + sign(m))
            to, more, came = group(own, k, m, i), group(sib, k, m, i), tr1.at[k, m]
            for j in range(SIDE):
                to[j] = (to[j].astype(F32) + more[j].astype(F32) + came[j].astype(F32)).astype(BF16)
            copy1(k, m, 2).start()

    def direct(k):
        for m in range(MATS):
            pos, _ = along(m, True, 1)
            pair_sum(k, m, wrap(pos - sign(m)))
            copy1(k, m, 1).start()

    def turn(k):
        arrived(d1r.at[k], dc1.at[k])
        for m in range(MATS):
            pos, _ = along(m, True, 1)
            to, more, came, came2 = group(own, k, m, pos), group(sib, k, m, pos), dc1.at[k, m, 0], dc1.at[k, m, 1]
            for j in range(SIDE):
                v = (to[j].astype(F32) + more[j].astype(F32)) + (came[j].astype(F32) + came2[j].astype(F32))
                mid[k, m, j] = v.astype(BF16)

            @pl.when(k < SHORT)
            def _():
                copy2(k, m, 0).start()
                copy2(k, m, 1).start()

            @pl.when(k >= SHORT)
            def _():
                for which in range(3):
                    copy2_short(k, m, which).start()

    def combine2(k):
        arrived(t2r.at[k], tr2.at[k])
        for m in range(MATS):
            pos, _ = along(m, False, 1)
            i = wrap(pos + sign(m))
            mid[k, m, i] = (mid[k, m, i].astype(F32) + tr2[k, m].astype(F32)).astype(BF16)
            copy2(k, m, 2).start()

    def collect(k, m, v):
        v = v.astype(BF16)
        grad[m, strip(k)] = v
        v = jnp.square(v.astype(F32))
        v = v[:8] + v[8:]
        acc[...] += v[:, :128] + v[:, 128:256] + v[:, 256:384] + v[:, 384:]

    def send_strips(k):
        for dz in (2, 1, 3, 0):
            for dc in range(2):
                z_copy(k, dz, dc).start()

    def finish_sum(k):
        arrived(d2r.at[k], dc2.at[k])
        for m in range(MATS):
            pos, _ = along(m, False, 1)
            collect(k, m, mid[k, m, pos].astype(F32) + (dc2[k, m, 0].astype(F32) + dc2[k, m, 1].astype(F32)))
        send_strips(k)

    def finish_short(k):
        arrived(t2r.at[k], tr2.at[k])
        arrived(d2r.at[k], dc2.at[k])
        for m in range(MATS):
            pos, _ = along(m, False, 1)
            v = mid[k, m, pos].astype(F32) + tr2[k, m].astype(F32)
            collect(k, m, v + (dc2[k, m, 0].astype(F32) + dc2[k, m, 1].astype(F32)))

    def mom_send(k):
        mom_load.wait()
        for dz in (2, 1, 3, 0):
            t = wrap(e + dz)
            first_is = jnp.float32(0)
            second_is = jnp.float32(0)
            for m in range(MATS):
                here = jnp.where(t == m, 1.0, 0.0).astype(F32)
                first_is = first_is + here * mask(m, 2 * e)
                second_is = second_is + here * mask(m, 2 * e + 1)
            for i in range(GROUPS):
                for h in range(2):
                    cols = slice(h * HALF, (h + 1) * HALF)
                    v = first_is * momv[0, i, :, cols] + second_is * momv[1, i, :, cols]
                    mout[dz, i, h * ROWS:(h + 1) * ROWS] = v.astype(BF16)
            if dz:
                mom_copy(dz).start()
        mom_sib.start()

    def mom_sum(k):
        arrived(m1r.at[0], min_.at[pl.ds(0, 3)])
        for i in range(GROUPS):
            v = mout[0, i].astype(F32)
            for dz in (1, 2, 3):
                v = v + min_[wrap(e + dz), i].astype(F32)
            mall[c, i] = v.astype(BF16)
        mom_pass.start()

    def finish_send(k):
        finish_short(k)
        send_strips(k)

    stages = ((transit, 0, 0, CHUNKS), (combine, 1, 0, CHUNKS), (direct, 2, 0, CHUNKS), (turn, 3, 0, CHUNKS),
              (combine2, 4, 0, SHORT), (finish_sum, 5, 0, SHORT), (finish_send, 4, SHORT, LAST), (mom_send, 1, 0, 1),
              (mom_sum, LAST + 2, 0, 1))

    def step(t, carry):
        for stage, lag, low, high in stages:
            if low < high:
                @pl.when((t >= low + lag) & (t < high + lag))
                def _():
                    stage(t - lag)
        return carry

    lax.fori_loop(0, LAST + 5, step, 0)
    finish_short(LAST)

    me_column = 2 * e + c
    me_plane = 4 * x + y

    def spread_column(src, dst, send, recv):
        copies = [remote(src, dst.at[me_column], send.at[0], recv.at[0], in_column(*d)) for d in COLUMN]
        for copy in copies:
            copy.start()
        dst[me_column] = src[...]

    def spread_plane(src, dst, send, recv):
        copies = [remote(src, dst.at[me_plane], send.at[0], recv.at[0], in_plane(*d)) for d in PLANE]
        for copy in copies:
            copy.start()
        dst[me_plane] = src[...]

    def total_of(recv, ref, count):
        arrived(recv.at[0], ref.at[pl.ds(0, count - 1)])
        v = ref[0]
        for j in range(1, count):
            v = v + ref[j]
        return v

    spread_column(acc, column, cs, cr)
    send_strips(LAST)
    acc2[...] = total_of(cr, column, 8)
    spread_plane(acc2, plane, ps, pr)
    mom_pass.wait_recv()
    arrived(zr.at[0], zin.at[pl.ds(0, 7)])
    pltpu.make_async_copy(zin.at[0], zin.at[0], zl.at[0]).wait()

    def unpack(i, carry):
        parts = [mall[k, i].astype(F32) for k in range(2)]
        for h in range(2):
            kept_rows = [v[h * ROWS:(h + 1) * ROWS] for v in parts]
            Mb[i, h] = jnp.concatenate(kept_rows, axis=0).astype(BF16)
        return carry

    lax.fori_loop(0, GROUPS, unpack, 0)
    for j in range(4):
        cols = pl.ds(pl.multiple_of((2 * (j % 2) + c) * LANES, LANES), LANES)
        gright[:, j * LANES:(j + 1) * LANES] = jnp.concatenate([zin[2 * n + j // 2, :, cols] for n in range(GROUPS)], axis=0)
        mright[:, j * LANES:(j + 1) * LANES] = Mb[:, j // 2, :, cols].reshape(GROUPS * BLOCK, LANES)

    def outer(left, right):
        return lax.dot_general(left, right, (((0,), (0,)), ((), ())), preferred_element_type=F32)

    at = 0
    for i in range(4):
        cols = slice((i % 2) * PANEL, (i % 2 + 1) * PANEL)
        gleft = jnp.concatenate([zin[2 * n + i // 2, :, cols] for n in range(GROUPS)], axis=0)
        mleft = Mb[:, i // 2, :, cols].reshape(GROUPS * BLOCK, PANEL)
        gr, mr = gright[:, i * LANES:], mright[:, i * LANES:]
        gg, gm, mm = outer(gleft, gr), outer(gleft, mr) + outer(mleft, gr), outer(mleft, mr)
        for j in range(4 - i):
            for n, v in enumerate((gg, gm, mm)):
                grams[n, at:at + PANEL] = v[:, j * LANES:(j + 1) * LANES]
            at += PANEL
    mean = whole_sum(total_of(pr, plane, 16)) / float(MATS * D * FF)
    factor = jnp.minimum(1.0, CLIP_RMS / jnp.sqrt(mean + MEAN_EPS))


    def part(ref, q, i, b):
        return ref.at[pl.ds(pl.multiple_of((8 * q + 2 * i + b) * 2 * PART, 16), 2 * PART)]

    def on(q, first, step):
        return (x, in_plane(step, 0)) if (q == 0) == first else (y, in_plane(0, step))

    def first_copy(q, step, b):
        pos, dev = on(q, True, step)
        return remote(part(packed, q, wrap(pos + step), b), rs1.at[q, b, step - 1], g1s.at[0], g1r.at[q, b], dev)

    def second_copy(q, step, b):
        _, dev = on(q, False, step)
        return remote(midg.at[q, b], rs2.at[q, b, step - 1], g2s.at[0], g2r.at[q, b], dev)

    def third_copy(q, step, b):
        pos, dev = on(q, True, step)
        ref = part(full.at[c], q, pos, b)
        return remote(ref, ref, g3s.at[0], g3r.at[q, b, step - 1], dev)

    def pair_copy(q, n, b):
        pos, _ = on(q, True, 1)
        ref = part(full.at[c], q, wrap(pos + n), b)
        return remote(ref, ref, g5s.at[0], g5r.at[0], in_column(0, 1))

    STEPS = (2, 1, 3)
    u = (1.0 + MOMENT) * factor
    w = MOMENT * MOMENT
    for q in range(2):
        def weigh(i, carry):
            rows = pl.ds(pl.multiple_of((16 * q + i) * PART, 16), PART)
            v = (u * u) * grams[0, rows] + (u * w) * grams[1, rows] + (w * w) * grams[2, rows]
            packed[rows] = v.astype(BF16)
            return carry

        lax.fori_loop(0, 16, weigh, 0)
        for s in STEPS:
            first_copy(q, s, 0).start()
    for q in range(2):
        for s in STEPS:
            first_copy(q, s, 1).start()

    def direction(i, carry):
        for h in range(2):
            v = factor * zin[2 * i + h].astype(F32)
            v = v + MOMENT * (MOMENT * Mb[i, h].astype(F32) + v)
            X[i, :, h * HALF:(h + 1) * HALF] = v.astype(BF16)
            sq = jnp.sum(jnp.square(v).reshape(BLOCK // 8, 8, HALF), axis=0)
            acc3[...] += sq[:, :128] + sq[:, 128:256] + sq[:, 256:384] + sq[:, 384:]
        return carry

    lax.fori_loop(0, GROUPS, direction, 0)

    spread_plane(acc3, plane2, ps2, pr2)
    mom_own.wait()
    mom_sib.wait_recv()

    def slot_copy(dz, dc):
        j = 2 * dz + dc
        if j == 0:
            return pltpu.make_async_copy(zout.at[0], zin2.at[2 * e + c], z2l.at[0])
        return remote(zout.at[j], zin2.at[2 * e + c], z2s.at[0], z2r.at[0], in_column(dz, dc))

    for dz in (2, 1, 3, 0):
        for dc in range(2):
            slot = wrap(e + dz) * SLOTS + lax.rem(c + dc, 2)
            v = mask(0, slot) * grad[0].astype(F32)
            for m in range(1, MATS):
                v = v + mask(m, slot) * grad[m].astype(F32)
            zout[2 * dz + dc] = v.astype(BF16)
            slot_copy(dz, dc).start()

    left(sib_s.at[0], sib)
    for which in range(3):
        left(s1.at[which], tr1)
        left(s2.at[which], tr2)
    left(zs.at[0], zin.at[pl.ds(0, 7)])
    left(m1s.at[0], mout.at[pl.ds(0, 3)])
    halves = [(q, b) for b in range(2) for q in range(2)]
    for q, b in halves:
        arrived(g1r.at[q, b], rs1.at[q, b])
        pos, _ = on(q, True, 1)
        v = part(packed, q, pos, b)[...].astype(F32) + rs1[q, b, 0].astype(F32)
        midg[q, b] = (v + (rs1[q, b, 1].astype(F32) + rs1[q, b, 2].astype(F32))).astype(BF16)
        for s in STEPS:
            second_copy(q, s, b).start()
    for q, b in halves:
        arrived(g2r.at[q, b], rs2.at[q, b])
        pos, _ = on(q, True, 1)
        v = midg[q, b].astype(F32) + rs2[q, b, 0].astype(F32)
        part(full.at[c], q, pos, b)[...] = (v + (rs2[q, b, 1].astype(F32) + rs2[q, b, 2].astype(F32))).astype(BF16)
        for s in STEPS:
            third_copy(q, s, b).start()
        pair_copy(q, 0, b).start()
    acc4[...] = total_of(pr2, plane2, 16)
    spread_column(acc4, sq_in, qs, qr)
    inv = 1.0 / (jnp.sqrt(whole_sum(acc4[...])) + NORM_EPS)
    for b in range(2):
        for s in (1, 3, 2):
            for q in range(2):
                third_copy(q, s, b).wait_recv()
                pair_copy(q, 4 - s, b).start()
    arrived(g5r.at[0], full.at[other])
    for k in range(2):
        at = 0
        for i in range(4):
            for n in range(4 - i):
                j = 2 * (i + n) + k
                block = full[k, at:at + PANEL]
                G[i * PANEL:(i + 1) * PANEL, j * LANES:(j + 1) * LANES] = block
                if n:
                    G[j * LANES:(j + 1) * LANES, i * PANEL:(i + 1) * PANEL] = block.T
                at += PANEL

    def product(lhs, rhs, out, finish):
        for i in range(4):
            low, high = i * PANEL, (i + 1) * PANEL
            v = jnp.dot(lhs[low:high], rhs[:, low:], preferred_element_type=F32)
            v = finish(v, slice(low, high), slice(low, FF)).astype(BF16)
            out[low:high, low:] = v
            for j in range(i + 1, 4):
                out[j * PANEL:(j + 1) * PANEL, low:high] = v[:, (j - i) * PANEL:(j - i + 1) * PANEL].T

    def polynomial(src, q, t, out, scale):
        b_s = COEF_B * scale
        c_s = COEF_C * scale * scale
        product(src, src, q, lambda v, i, j: b_s * src[i, j].astype(F32) + c_s * v)
        product(src, q, t, lambda v, i, j: scale * (COEF_A * src[i, j].astype(F32) + v))
        product(t, q, out, lambda v, i, j: COEF_A * t[i, j].astype(F32) + v)

    def advance(src, rhs, scale):
        v = src[...]
        w = scale * (COEF_A * v.astype(F32) + jnp.dot(v, rhs[...], preferred_element_type=F32))
        return w.astype(BF16)

    for n in range(2):
        X2[0, n * BLOCK:(n + 1) * BLOCK] = X[2 * c + n]
    polynomial(G, A, B, T, inv * inv)
    X2[1] = advance(X2.at[0], A, inv)
    polynomial(T, A, B, G, 1.0)
    X2[0] = advance(X2.at[1], A, 1.0)
    v = X2[0]
    w = jnp.dot(v, G[...], preferred_element_type=F32).astype(BF16)
    z = jnp.dot(w, G[...], preferred_element_type=F32)
    z = (COEF_A * v.astype(F32) + COEF_B * w.astype(F32) + COEF_C * z).astype(BF16)

    def return_copy(n, dc):
        src = back.at[n, lax.rem(c + dc, 2)]
        return remote(src, ret.at[e], bs.at[n, dc], br.at[e], target(2 * c + n, x, y, lax.rem(c + dc, 2)))

    def return_local(n):
        return pltpu.make_async_copy(back.at[n, c], ret.at[e], bl.at[0])

    def return_in(m):
        return remote(back.at[0, 0], ret.at[m], bs.at[0, 0], br.at[m], in_column(0, 1))

    for n in range(2):
        for h in range(2):
            for k in range(2):
                top = n * BLOCK + h * ROWS
                back[n, h, k * ROWS:(k + 1) * ROWS] = z[top:top + ROWS, k * HALF:(k + 1) * HALF]
        return_copy(n, 1).start()

        @pl.when(2 * c + n != e)
        def _():
            return_copy(n, 0).start()

        @pl.when(2 * c + n == e)
        def _():
            return_local(n).start()

    arrived(z2r.at[0], zin2.at[pl.ds(0, 7)])
    slot_copy(0, 0).wait()

    def momentum(i, carry):
        for h in range(2):
            cols = pl.ds(h * HALF, HALF)
            buf[i, :, cols] = MOMENT * buf[i, :, cols] + factor * zin2[2 * i + h].astype(F32)
        return carry

    lax.fori_loop(0, GROUPS, momentum, 0)
    new_own = pltpu.make_async_copy(buf.at[:, mine_rows], new_mom.at[c], ns.at[0])
    new_sib = remote(buf.at[:, other_rows], new_mom.at[c], ns.at[1], ns.at[2], in_column(0, 1))
    new_sib.start()
    new_own.start()

    arrived(qr.at[0], sq_in.at[pl.ds(0, 7)])
    lane = lax.broadcasted_iota(jnp.int32, (8, LANES), 1)
    mean_sq = jnp.zeros((8, LANES), F32)
    for m in range(MATS):
        mean_sq = mean_sq + jnp.where(lane == m, whole_sum(sq_in[2 * m]) / float(D * FF), 0.0)
    rms_out[...] = jnp.sqrt(mean_sq)[:1, :MATS]

    mom_pass.wait_send()
    mom_sib.wait_send()
    left(g1s.at[0], rs1)
    left(g2s.at[0], rs2)
    left(g3s.at[0], rs1)
    left(g5s.at[0], full.at[0])
    left(z2s.at[0], zout.at[pl.ds(0, 7)])
    left(cs.at[0], column.at[pl.ds(0, 7)])
    left(ps.at[0], plane.at[pl.ds(0, 15)])
    left(ps2.at[0], plane2.at[pl.ds(0, 15)])
    left(qs.at[0], sq_in.at[pl.ds(0, 7)])
    for dz in (0, 1, 3, 2):
        m = wrap(e + dz)
        if dz:
            return_in(m).wait_recv()
        else:
            @pl.when(e // 2 == c)
            def _():
                return_local(0).wait()

            @pl.when(e // 2 != c)
            def _():
                return_in(m).wait_recv()
        v = ret[m].astype(F32)
        rows_out[m, :, :HALF] = v[:ROWS].astype(BF16)
        rows_out[m, :, HALF:] = v[ROWS:].astype(BF16)
    for n in range(2):
        return_copy(n, 1).wait_send()

        @pl.when(2 * c + n != e)
        def _():
            return_copy(n, 0).wait_send()

    new_own.wait()
    new_sib.wait()


ANY = pl.BlockSpec(memory_space=pl.ANY)
VMEM = pl.BlockSpec(memory_space=pltpu.VMEM)
SMEM = pl.BlockSpec(memory_space=pltpu.SMEM)
DMA = pltpu.SemaphoreType.DMA


def per_device(grad_terms, momentum, weights, owner_list):
    small = (CHUNKS, MATS, STRIP, HALF)
    large = (CHUNKS, MATS, SIDE, STRIP, HALF)
    whole = (MATS, SIDE, SIDE, BLOCK, HALF)
    tile = pltpu.VMEM((8, LANES), F32)
    square = pltpu.VMEM((FF, FF), BF16)
    new_mom, rows, rms = pl.pallas_call(
        muon_kernel,
        name="muon",
        out_shape=(
            jax.ShapeDtypeStruct((SLOTS, GROUPS, ROWS, FF), F32),
            jax.ShapeDtypeStruct((MATS, ROWS, FF), BF16),
            jax.ShapeDtypeStruct((1, MATS), F32),
        ),
        in_specs=[SMEM, ANY, ANY],
        out_specs=(ANY, VMEM, VMEM),
        scratch_shapes=[
            pltpu.VMEM(whole, BF16), pltpu.VMEM(whole, BF16),
            pltpu.VMEM(large, BF16), pltpu.VMEM((CHUNKS, MATS, 2, SIDE, STRIP, HALF), BF16), pltpu.VMEM(large, BF16),
            pltpu.VMEM(small, BF16), pltpu.VMEM((CHUNKS, MATS, 2, STRIP, HALF), BF16),
            pltpu.VMEM((MATS, BLOCK, HALF), BF16),
            pltpu.VMEM((GROUPS * 2, BLOCK, HALF), BF16),
            pltpu.VMEM((GROUPS * SLOTS, BLOCK, HALF), BF16),
            pltpu.VMEM((GROUPS * 2, BLOCK, HALF), BF16),
            pltpu.VMEM((SLOTS, GROUPS, ROWS, FF), F32),
            pltpu.VMEM((4, GROUPS, BLOCK, HALF), BF16), pltpu.VMEM((4, GROUPS, BLOCK, HALF), BF16),
            pltpu.VMEM((2, GROUPS, BLOCK, HALF), BF16),
            pltpu.VMEM((GROUPS, 2, BLOCK, HALF), BF16),
            pltpu.VMEM((GROUPS * BLOCK, HALF), BF16), pltpu.VMEM((GROUPS * BLOCK, HALF), BF16),
            pltpu.VMEM((3, 32 * PART, LANES), F32),
            pltpu.VMEM((GROUPS, BLOCK, FF), F32),
            pltpu.VMEM((GROUPS, BLOCK, FF), BF16),
            pltpu.VMEM((2, 2 * BLOCK, FF), BF16),
            pltpu.VMEM((32 * PART, LANES), BF16), pltpu.VMEM((2, 32 * PART, LANES), BF16),
            pltpu.VMEM((2, 2, 3, 2 * PART, LANES), BF16),
            pltpu.VMEM((2, 2, 2 * PART, LANES), BF16),
            pltpu.VMEM((2, 2, 3, 2 * PART, LANES), BF16),
            square, square, square, square,
            pltpu.VMEM((2, 2, BLOCK, HALF), BF16), pltpu.VMEM((MATS, BLOCK, HALF), BF16),
            tile, tile, tile, tile,
            pltpu.VMEM((8, 8, LANES), F32), pltpu.VMEM((16, 8, LANES), F32), pltpu.VMEM((16, 8, LANES), F32),
            pltpu.VMEM((8, 8, LANES), F32),
            DMA((CHUNKS,)), DMA((1,)), DMA((CHUNKS, MATS)),
            DMA((3,)), DMA((CHUNKS,)), DMA((CHUNKS,)), DMA((3,)), DMA((CHUNKS,)), DMA((CHUNKS,)),
            DMA((1,)), DMA((1,)), DMA((1,)), DMA((4,)), DMA((1,)), DMA((1,)), DMA((2,)),
            DMA((1,)), DMA((1,)), DMA((1,)), DMA((1,)), DMA((3,)),
            DMA((1,)), DMA((2, 2)), DMA((1,)), DMA((2, 2)), DMA((1,)), DMA((2, 2, 3)), DMA((1,)), DMA((1,)),
            DMA((1,)), DMA((1,)), DMA((1,)), DMA((1,)), DMA((1,)), DMA((1,)), DMA((1,)), DMA((2, 2)), DMA((4,)),
            DMA((1,)),
        ],
        compiler_params=pltpu.CompilerParams(collective_id=0, has_side_effects=True, vmem_limit_bytes=60 << 20),
    )(owner_list, grad_terms.reshape(MATS, SIDE, SIDE, BLOCK, FF), momentum[0])

    rows = rows.astype(F32)
    scale_rms = 0.2 * math.sqrt(max(D, FF))
    update = (scale_rms * rows).astype(BF16)
    new_weights = weights * (1.0 - LEARN * DECAY) - LEARN * scale_rms * rows
    return (new_weights, update, new_mom[None], rms.reshape(MATS))


def solution(mesh):
    placed = (
        P("dp", None, "expert", None),
        P("expert", None, None, "dp", None),
        P(None, ("expert", "dp"), None),
        P(),
    )
    return jax.shard_map(
        per_device,
        mesh=mesh,
        in_specs=placed,
        out_specs=(
            P(None, ("expert", "dp"), None),
            P(None, ("expert", "dp"), None),
            P("expert", None, None, "dp", None),
            P(),
        ),
        check_vma=False,
    )
```

```python
import math

import jax
import jax.numpy as jnp
from jax import lax
from jax.experimental import pallas as pl
from jax.experimental.pallas import tpu as pltpu
from jax.sharding import PartitionSpec as P

D = 7168
FF = 1024
MATS = 4
SLOTS = 2
GROUPS = 4
SIDE = 4
BLOCK = 112
ROWS = 56
HALF = FF // 2
LANES = 128
STRIP = 16
CHUNKS = BLOCK // STRIP
LAST = CHUNKS - 1
SHORT = 5
PANEL = 256
PART = 80

MOMENT = 0.95
CLIP_RMS = 1.0
LEARN = 0.1
DECAY = 0.1
COEF_A = 3.4445
COEF_B = -4.775
COEF_C = 2.0315
NORM_EPS = 1e-07
MEAN_EPS = 1e-06
F32 = jnp.float32
BF16 = jnp.bfloat16

COLUMN = ((2, 0), (2, 1), (1, 0), (1, 1), (3, 0), (3, 1), (0, 1))
PLANE = tuple((dx, dy) for dx in range(4) for dy in range(4) if dx + dy)


def wrap(v):
    return lax.rem(v + 4, 4)


def remote(src, dst, send, recv, device):
    return pltpu.make_async_remote_copy(src_ref=src, dst_ref=dst, send_sem=send, recv_sem=recv, device_id=device)


def whole_sum(v):
    return jnp.sum(jnp.sum(v, axis=0, keepdims=True), axis=1, keepdims=True)


def sign(m):
    return 1 if m % 2 else -1


def muon_kernel(owners, g, mom, new_mom, rows_out, rms_out,
                own, sib, tr1, dc1, mid, tr2, dc2, grad, zin, zout, zin2, momv, mout, min_, mall, Mb, gright, mright, grams, buf, X, X2,
                packed, full, rs1, midg, rs2, G, A, B, T, back, ret, acc, acc2, acc3, acc4,
                column, plane, plane2, sq_in,
                own_s, sib_s, sib_r, s1, t1r, d1r, s2, t2r, d2r, zs, zr, zl, ms, m1s, m1r, m2s, cs, cr, ps, pr, ns, g1s, g1r,
                g2s, g2r, g3s, g3r, g5s, g5r, ps2, pr2, qs, qr, z2s, z2r, z2l, bs, br, bl):
    e = lax.axis_index("expert")
    p = lax.axis_index("dp")
    x, y, c = p // 8, (p // 2) % 4, p % 2
    other = 1 - c

    def target(te, tx, ty, tc):
        return {"expert": te, "dp": tx * 8 + ty * 2 + tc}

    def in_column(dz, dc):
        return target(wrap(e + dz), x, y, lax.rem(c + dc, 2))

    def in_plane(dx, dy):
        return target(e, wrap(x + dx), wrap(y + dy), c)

    def arrived(sem, ref):
        remote(ref, ref, sem, sem, in_column(0, 1)).wait_recv()

    def left(sem, ref):
        remote(ref, ref, sem, sem, in_column(0, 1)).wait_send()

    places = []
    for m in range(MATS):
        number = jnp.int32(0)
        for m2 in range(m):
            number = number + jnp.where(owners[m2] == owners[m], 1, 0)
        places.append(owners[m] * SLOTS + number)

    def mask(m, slot):
        return jnp.where(places[m] == slot, 1.0, 0.0).astype(F32)

    def strip(k):
        return pl.ds(pl.multiple_of(k * STRIP, STRIP), STRIP)

    def own_copy(k):
        cols = pl.ds(pl.multiple_of(c * HALF, HALF), HALF)
        return pltpu.make_async_copy(g.at[:, :, :, strip(k), cols], own.at[:, :, :, strip(k)], own_s.at[k])

    def sib_copy(k, m):
        cols = pl.ds(pl.multiple_of(other * HALF, HALF), HALF)
        return remote(g.at[m, :, :, strip(k), cols], sib.at[m, :, :, strip(k)], sib_s.at[0], sib_r.at[k, m],
                      in_column(0, 1))

    def along(m, first, step):
        on_x = (m < 2) == first
        return (x, in_plane(step, 0)) if on_x else (y, in_plane(0, step))

    def group(ref, k, m, i):
        return ref.at[m, i, :, strip(k)] if m < 2 else ref.at[m, :, i, strip(k)]

    def copy1(k, m, which):
        d = sign(m)
        pos, dev = along(m, True, -d if which == 1 else d)
        i = wrap(pos + (2, -d, d)[which])
        if which == 0:
            dst, recv = tr1.at[k, m], t1r.at[k]
        else:
            dst, recv = dc1.at[k, m, which - 1], d1r.at[k]
        return remote(group(own, k, m, i), dst, s1.at[which], recv, dev)

    def ends2(k, m, which):
        if which == 0:
            return tr2.at[k, m], s2.at[0], t2r.at[k]
        return dc2.at[k, m, which - 1], s2.at[which], d2r.at[k]

    def copy2(k, m, which):
        d = sign(m)
        pos, dev = along(m, False, -d if which == 1 else d)
        i = wrap(pos + (2, -d, d)[which])
        return remote(mid.at[k, m, i], *ends2(k, m, which), dev)

    def copy2_short(k, m, which):
        step = (2, 1, 3)[which]
        pos, dev = along(m, False, step)
        return remote(mid.at[k, m, wrap(pos + step)], *ends2(k, m, which), dev)

    def z_copy(k, dz, dc):
        j = 2 * dz + dc
        src, dst = grad.at[wrap(e + dz), strip(k)], zin.at[2 * e + c, strip(k)]
        if j == 0:
            return pltpu.make_async_copy(src, dst, zl.at[0])
        return remote(src, dst, zs.at[0], zr.at[0], in_column(dz, dc))

    mine_rows = pl.ds(pl.multiple_of(ROWS * c, 8), ROWS)
    other_rows = pl.ds(pl.multiple_of(ROWS * other, 8), ROWS)
    mom_load = pltpu.make_async_copy(mom, momv, ms.at[0])
    mom_own = pltpu.make_async_copy(mom.at[c], buf.at[:, mine_rows], ms.at[1])
    mom_sib = remote(mom.at[other], buf.at[:, mine_rows], ms.at[2], ms.at[3], in_column(0, 1))

    def mom_copy(dz):
        return remote(mout.at[dz], min_.at[e], m1s.at[0], m1r.at[0], in_column(dz, 0))

    mom_pass = remote(mall.at[c], mall.at[c], m2s.at[0], m2s.at[1], in_column(0, 1))

    for k in range(CHUNKS):
        own_copy(k).start()
        if k == 0:
            mom_load.start()
    mom_own.start()
    barrier = pltpu.get_barrier_semaphore()
    for dz, dc in COLUMN:
        pl.semaphore_signal(barrier, inc=1, device_id=in_column(dz, dc))
    for dx, dy in PLANE:
        pl.semaphore_signal(barrier, inc=1, device_id=in_plane(dx, dy))
    pl.semaphore_wait(barrier, len(COLUMN) + len(PLANE))
    for k in range(CHUNKS):
        for m in range(MATS):
            sib_copy(k, m).start()
    acc[...] = jnp.zeros_like(acc)
    acc3[...] = jnp.zeros_like(acc3)

    def pair_sum(k, m, i):
        to, more = group(own, k, m, i), group(sib, k, m, i)
        for j in range(SIDE):
            to[j] = (to[j].astype(F32) + more[j].astype(F32)).astype(BF16)

    def transit(k):
        own_copy(k).wait()
        for m in range(MATS):
            sib_copy(k, m).wait_recv()
            pos, _ = along(m, True, 1)
            pair_sum(k, m, wrap(pos + 2))
            copy1(k, m, 0).start()

    def combine(k):
        arrived(t1r.at[k], tr1.at[k])
        for m in range(MATS):
            pos, _ = along(m, True, 1)
            i = wrap(pos + sign(m))
            to, more, came = group(own, k, m, i), group(sib, k, m, i), tr1.at[k, m]
            for j in range(SIDE):
                to[j] = (to[j].astype(F32) + more[j].astype(F32) + came[j].astype(F32)).astype(BF16)
            copy1(k, m, 2).start()

    def direct(k):
        for m in range(MATS):
            pos, _ = along(m, True, 1)
            pair_sum(k, m, wrap(pos - sign(m)))
            copy1(k, m, 1).start()

    def turn(k):
        arrived(d1r.at[k], dc1.at[k])
        for m in range(MATS):
            pos, _ = along(m, True, 1)
            to, more, came, came2 = group(own, k, m, pos), group(sib, k, m, pos), dc1.at[k, m, 0], dc1.at[k, m, 1]
            for j in range(SIDE):
                v = (to[j].astype(F32) + more[j].astype(F32)) + (came[j].astype(F32) + came2[j].astype(F32))
                mid[k, m, j] = v.astype(BF16)

            @pl.when(k < SHORT)
            def _():
                copy2(k, m, 0).start()
                copy2(k, m, 1).start()

            @pl.when(k >= SHORT)
            def _():
                for which in range(3):
                    copy2_short(k, m, which).start()

    def combine2(k):
        arrived(t2r.at[k], tr2.at[k])
        for m in range(MATS):
            pos, _ = along(m, False, 1)
            i = wrap(pos + sign(m))
            mid[k, m, i] = (mid[k, m, i].astype(F32) + tr2[k, m].astype(F32)).astype(BF16)
            copy2(k, m, 2).start()

    def collect(k, m, v):
        v = v.astype(BF16)
        grad[m, strip(k)] = v
        v = jnp.square(v.astype(F32))
        v = v[:8] + v[8:]
        acc[...] += v[:, :128] + v[:, 128:256] + v[:, 256:384] + v[:, 384:]

    def send_strips(k):
        for dz in (2, 1, 3, 0):
            for dc in range(2):
                z_copy(k, dz, dc).start()

    def finish_sum(k):
        arrived(d2r.at[k], dc2.at[k])
        for m in range(MATS):
            pos, _ = along(m, False, 1)
            collect(k, m, mid[k, m, pos].astype(F32) + (dc2[k, m, 0].astype(F32) + dc2[k, m, 1].astype(F32)))
        send_strips(k)

    def finish_short(k):
        arrived(t2r.at[k], tr2.at[k])
        arrived(d2r.at[k], dc2.at[k])
        for m in range(MATS):
            pos, _ = along(m, False, 1)
            v = mid[k, m, pos].astype(F32) + tr2[k, m].astype(F32)
            collect(k, m, v + (dc2[k, m, 0].astype(F32) + dc2[k, m, 1].astype(F32)))

    def mom_send(k):
        mom_load.wait()
        for dz in (2, 1, 3, 0):
            t = wrap(e + dz)
            first_is = jnp.float32(0)
            second_is = jnp.float32(0)
            for m in range(MATS):
                here = jnp.where(t == m, 1.0, 0.0).astype(F32)
                first_is = first_is + here * mask(m, 2 * e)
                second_is = second_is + here * mask(m, 2 * e + 1)
            for i in range(GROUPS):
                for h in range(2):
                    cols = slice(h * HALF, (h + 1) * HALF)
                    v = first_is * momv[0, i, :, cols] + second_is * momv[1, i, :, cols]
                    mout[dz, i, h * ROWS:(h + 1) * ROWS] = v.astype(BF16)
            if dz:
                mom_copy(dz).start()
        mom_sib.start()

    def mom_sum(k):
        arrived(m1r.at[0], min_.at[pl.ds(0, 3)])
        for i in range(GROUPS):
            v = mout[0, i].astype(F32)
            for dz in (1, 2, 3):
                v = v + min_[wrap(e + dz), i].astype(F32)
            mall[c, i] = v.astype(BF16)
        mom_pass.start()

    def finish_send(k):
        finish_short(k)
        send_strips(k)

    stages = ((transit, 0, 0, CHUNKS), (combine, 1, 0, CHUNKS), (direct, 2, 0, CHUNKS), (turn, 3, 0, CHUNKS),
              (combine2, 4, 0, SHORT), (finish_sum, 5, 0, SHORT), (finish_send, 4, SHORT, LAST), (mom_send, 1, 0, 1),
              (mom_sum, LAST + 2, 0, 1))

    def step(t, carry):
        for stage, lag, low, high in stages:
            if low < high:
                @pl.when((t >= low + lag) & (t < high + lag))
                def _():
                    stage(t - lag)
        return carry

    lax.fori_loop(0, LAST + 5, step, 0)
    finish_short(LAST)

    me_column = 2 * e + c
    me_plane = 4 * x + y

    def spread_column(src, dst, send, recv):
        copies = [remote(src, dst.at[me_column], send.at[0], recv.at[0], in_column(*d)) for d in COLUMN]
        for copy in copies:
            copy.start()
        dst[me_column] = src[...]

    def spread_plane(src, dst, send, recv):
        copies = [remote(src, dst.at[me_plane], send.at[0], recv.at[0], in_plane(*d)) for d in PLANE]
        for copy in copies:
            copy.start()
        dst[me_plane] = src[...]

    def total_of(recv, ref, count):
        arrived(recv.at[0], ref.at[pl.ds(0, count - 1)])
        v = ref[0]
        for j in range(1, count):
            v = v + ref[j]
        return v

    spread_column(acc, column, cs, cr)
    send_strips(LAST)
    mom_pass.wait_recv()

    def unpack(i, carry):
        parts = [mall[k, i].astype(F32) for k in range(2)]
        for h in range(2):
            kept_rows = [v[h * ROWS:(h + 1) * ROWS] for v in parts]
            Mb[i, h] = jnp.concatenate(kept_rows, axis=0).astype(BF16)
        return carry

    lax.fori_loop(0, GROUPS, unpack, 0)
    for j in range(4):
        cols = pl.ds(pl.multiple_of((2 * (j % 2) + c) * LANES, LANES), LANES)
        mright[:, j * LANES:(j + 1) * LANES] = Mb[:, j // 2, :, cols].reshape(GROUPS * BLOCK, LANES)

    def outer(left, right):
        return lax.dot_general(left, right, (((0,), (0,)), ((), ())), preferred_element_type=F32)

    at = 0
    for i in range(4):
        cols = slice((i % 2) * PANEL, (i % 2 + 1) * PANEL)
        mm = outer(Mb[:, i // 2, :, cols].reshape(GROUPS * BLOCK, PANEL), mright[:, i * LANES:])
        for j in range(4 - i):
            grams[2, at:at + PANEL] = mm[:, j * LANES:(j + 1) * LANES]
            at += PANEL

    acc2[...] = total_of(cr, column, 8)
    spread_plane(acc2, plane, ps, pr)
    arrived(zr.at[0], zin.at[pl.ds(0, 7)])
    pltpu.make_async_copy(zin.at[0], zin.at[0], zl.at[0]).wait()

    for j in range(4):
        cols = pl.ds(pl.multiple_of((2 * (j % 2) + c) * LANES, LANES), LANES)
        gright[:, j * LANES:(j + 1) * LANES] = jnp.concatenate([zin[2 * n + j // 2, :, cols] for n in range(GROUPS)], axis=0)

    at = 0
    for i in range(4):
        cols = slice((i % 2) * PANEL, (i % 2 + 1) * PANEL)
        gleft = jnp.concatenate([zin[2 * n + i // 2, :, cols] for n in range(GROUPS)], axis=0)
        mleft = Mb[:, i // 2, :, cols].reshape(GROUPS * BLOCK, PANEL)
        gr, mr = gright[:, i * LANES:], mright[:, i * LANES:]
        gg, gm = outer(gleft, gr), outer(gleft, mr) + outer(mleft, gr)
        for j in range(4 - i):
            for n, v in enumerate((gg, gm)):
                grams[n, at:at + PANEL] = v[:, j * LANES:(j + 1) * LANES]
            at += PANEL
    mean = whole_sum(total_of(pr, plane, 16)) / float(MATS * D * FF)
    factor = jnp.minimum(1.0, CLIP_RMS / jnp.sqrt(mean + MEAN_EPS))


    def part(ref, q, i, b):
        return ref.at[pl.ds(pl.multiple_of((8 * q + 2 * i + b) * 2 * PART, 16), 2 * PART)]

    def on(q, first, step):
        return (x, in_plane(step, 0)) if (q == 0) == first else (y, in_plane(0, step))

    def first_copy(q, step, b):
        pos, dev = on(q, True, step)
        return remote(part(packed, q, wrap(pos + step), b), rs1.at[q, b, step - 1], g1s.at[0], g1r.at[q, b], dev)

    def second_copy(q, step, b):
        _, dev = on(q, False, step)
        return remote(midg.at[q, b], rs2.at[q, b, step - 1], g2s.at[0], g2r.at[q, b], dev)

    def third_copy(q, step, b):
        pos, dev = on(q, True, step)
        ref = part(full.at[c], q, pos, b)
        return remote(ref, ref, g3s.at[0], g3r.at[q, b, step - 1], dev)

    def pair_copy(q, n, b):
        pos, _ = on(q, True, 1)
        ref = part(full.at[c], q, wrap(pos + n), b)
        return remote(ref, ref, g5s.at[0], g5r.at[0], in_column(0, 1))

    STEPS = (2, 1, 3)
    u = (1.0 + MOMENT) * factor
    w = MOMENT * MOMENT
    for q in range(2):
        def weigh(i, carry):
            rows = pl.ds(pl.multiple_of((16 * q + i) * PART, 16), PART)
            v = (u * u) * grams[0, rows] + (u * w) * grams[1, rows] + (w * w) * grams[2, rows]
            packed[rows] = v.astype(BF16)
            return carry

        lax.fori_loop(0, 16, weigh, 0)
        for s in STEPS:
            first_copy(q, s, 0).start()
    for q in range(2):
        for s in STEPS:
            first_copy(q, s, 1).start()

    def direction(i, carry):
        for h in range(2):
            v = factor * zin[2 * i + h].astype(F32)
            v = v + MOMENT * (MOMENT * Mb[i, h].astype(F32) + v)
            X[i, :, h * HALF:(h + 1) * HALF] = v.astype(BF16)
            sq = jnp.sum(jnp.square(v).reshape(BLOCK // 8, 8, HALF), axis=0)
            acc3[...] += sq[:, :128] + sq[:, 128:256] + sq[:, 256:384] + sq[:, 384:]
        return carry

    lax.fori_loop(0, GROUPS, direction, 0)

    spread_plane(acc3, plane2, ps2, pr2)
    mom_own.wait()
    mom_sib.wait_recv()

    def slot_copy(dz, dc):
        j = 2 * dz + dc
        if j == 0:
            return pltpu.make_async_copy(zout.at[0], zin2.at[2 * e + c], z2l.at[0])
        return remote(zout.at[j], zin2.at[2 * e + c], z2s.at[0], z2r.at[0], in_column(dz, dc))

    for dz in (2, 1, 3, 0):
        for dc in range(2):
            slot = wrap(e + dz) * SLOTS + lax.rem(c + dc, 2)
            v = mask(0, slot) * grad[0].astype(F32)
            for m in range(1, MATS):
                v = v + mask(m, slot) * grad[m].astype(F32)
            zout[2 * dz + dc] = v.astype(BF16)
            slot_copy(dz, dc).start()

    left(sib_s.at[0], sib)
    for which in range(3):
        left(s1.at[which], tr1)
        left(s2.at[which], tr2)
    left(zs.at[0], zin.at[pl.ds(0, 7)])
    left(m1s.at[0], mout.at[pl.ds(0, 3)])
    halves = [(q, b) for b in range(2) for q in range(2)]
    for q, b in halves:
        arrived(g1r.at[q, b], rs1.at[q, b])
        pos, _ = on(q, True, 1)
        v = part(packed, q, pos, b)[...].astype(F32) + rs1[q, b, 0].astype(F32)
        midg[q, b] = (v + (rs1[q, b, 1].astype(F32) + rs1[q, b, 2].astype(F32))).astype(BF16)
        for s in STEPS:
            second_copy(q, s, b).start()
    for q, b in halves:
        arrived(g2r.at[q, b], rs2.at[q, b])
        pos, _ = on(q, True, 1)
        v = midg[q, b].astype(F32) + rs2[q, b, 0].astype(F32)
        part(full.at[c], q, pos, b)[...] = (v + (rs2[q, b, 1].astype(F32) + rs2[q, b, 2].astype(F32))).astype(BF16)
        for s in STEPS:
            third_copy(q, s, b).start()
        pair_copy(q, 0, b).start()
    acc4[...] = total_of(pr2, plane2, 16)
    spread_column(acc4, sq_in, qs, qr)
    inv = 1.0 / (jnp.sqrt(whole_sum(acc4[...])) + NORM_EPS)
    for b in range(2):
        for s in (1, 3, 2):
            for q in range(2):
                third_copy(q, s, b).wait_recv()
                pair_copy(q, 4 - s, b).start()
    arrived(g5r.at[0], full.at[other])
    for k in range(2):
        at = 0
        for i in range(4):
            for n in range(4 - i):
                j = 2 * (i + n) + k
                block = full[k, at:at + PANEL]
                G[i * PANEL:(i + 1) * PANEL, j * LANES:(j + 1) * LANES] = block
                if n:
                    G[j * LANES:(j + 1) * LANES, i * PANEL:(i + 1) * PANEL] = block.T
                at += PANEL

    def product(lhs, rhs, out, finish):
        for i in range(4):
            low, high = i * PANEL, (i + 1) * PANEL
            v = jnp.dot(lhs[low:high], rhs[:, low:], preferred_element_type=F32)
            v = finish(v, slice(low, high), slice(low, FF)).astype(BF16)
            out[low:high, low:] = v
            for j in range(i + 1, 4):
                out[j * PANEL:(j + 1) * PANEL, low:high] = v[:, (j - i) * PANEL:(j - i + 1) * PANEL].T

    def polynomial(src, q, t, out, scale):
        b_s = COEF_B * scale
        c_s = COEF_C * scale * scale
        product(src, src, q, lambda v, i, j: b_s * src[i, j].astype(F32) + c_s * v)
        product(src, q, t, lambda v, i, j: scale * (COEF_A * src[i, j].astype(F32) + v))
        product(t, q, out, lambda v, i, j: COEF_A * t[i, j].astype(F32) + v)

    def advance(src, rhs, scale):
        v = src[...]
        w = scale * (COEF_A * v.astype(F32) + jnp.dot(v, rhs[...], preferred_element_type=F32))
        return w.astype(BF16)

    for n in range(2):
        X2[0, n * BLOCK:(n + 1) * BLOCK] = X[2 * c + n]
    polynomial(G, A, B, T, inv * inv)
    X2[1] = advance(X2.at[0], A, inv)
    polynomial(T, A, B, G, 1.0)
    X2[0] = advance(X2.at[1], A, 1.0)
    v = X2[0]
    w = jnp.dot(v, G[...], preferred_element_type=F32).astype(BF16)
    z = jnp.dot(w, G[...], preferred_element_type=F32)
    z = (COEF_A * v.astype(F32) + COEF_B * w.astype(F32) + COEF_C * z).astype(BF16)

    def return_copy(n, dc):
        src = back.at[n, lax.rem(c + dc, 2)]
        return remote(src, ret.at[e], bs.at[n, dc], br.at[e], target(2 * c + n, x, y, lax.rem(c + dc, 2)))

    def return_local(n):
        return pltpu.make_async_copy(back.at[n, c], ret.at[e], bl.at[0])

    def return_in(m):
        return remote(back.at[0, 0], ret.at[m], bs.at[0, 0], br.at[m], in_column(0, 1))

    for n in range(2):
        for h in range(2):
            for k in range(2):
                top = n * BLOCK + h * ROWS
                back[n, h, k * ROWS:(k + 1) * ROWS] = z[top:top + ROWS, k * HALF:(k + 1) * HALF]
        return_copy(n, 1).start()

        @pl.when(2 * c + n != e)
        def _():
            return_copy(n, 0).start()

        @pl.when(2 * c + n == e)
        def _():
            return_local(n).start()

    arrived(z2r.at[0], zin2.at[pl.ds(0, 7)])
    slot_copy(0, 0).wait()

    def momentum(i, carry):
        for h in range(2):
            cols = pl.ds(h * HALF, HALF)
            buf[i, :, cols] = MOMENT * buf[i, :, cols] + factor * zin2[2 * i + h].astype(F32)
        return carry

    lax.fori_loop(0, GROUPS, momentum, 0)
    new_own = pltpu.make_async_copy(buf.at[:, mine_rows], new_mom.at[c], ns.at[0])
    new_sib = remote(buf.at[:, other_rows], new_mom.at[c], ns.at[1], ns.at[2], in_column(0, 1))
    new_sib.start()
    new_own.start()

    arrived(qr.at[0], sq_in.at[pl.ds(0, 7)])
    lane = lax.broadcasted_iota(jnp.int32, (8, LANES), 1)
    mean_sq = jnp.zeros((8, LANES), F32)
    for m in range(MATS):
        mean_sq = mean_sq + jnp.where(lane == m, whole_sum(sq_in[2 * m]) / float(D * FF), 0.0)
    rms_out[...] = jnp.sqrt(mean_sq)[:1, :MATS]

    mom_pass.wait_send()
    mom_sib.wait_send()
    left(g1s.at[0], rs1)
    left(g2s.at[0], rs2)
    left(g3s.at[0], rs1)
    left(g5s.at[0], full.at[0])
    left(z2s.at[0], zout.at[pl.ds(0, 7)])
    left(cs.at[0], column.at[pl.ds(0, 7)])
    left(ps.at[0], plane.at[pl.ds(0, 15)])
    left(ps2.at[0], plane2.at[pl.ds(0, 15)])
    left(qs.at[0], sq_in.at[pl.ds(0, 7)])
    for dz in (0, 1, 3, 2):
        m = wrap(e + dz)
        if dz:
            return_in(m).wait_recv()
        else:
            @pl.when(e // 2 == c)
            def _():
                return_local(0).wait()

            @pl.when(e // 2 != c)
            def _():
                return_in(m).wait_recv()
        v = ret[m].astype(F32)
        rows_out[m, :, :HALF] = v[:ROWS].astype(BF16)
        rows_out[m, :, HALF:] = v[ROWS:].astype(BF16)
    for n in range(2):
        return_copy(n, 1).wait_send()

        @pl.when(2 * c + n != e)
        def _():
            return_copy(n, 0).wait_send()

    new_own.wait()
    new_sib.wait()


ANY = pl.BlockSpec(memory_space=pl.ANY)
VMEM = pl.BlockSpec(memory_space=pltpu.VMEM)
SMEM = pl.BlockSpec(memory_space=pltpu.SMEM)
DMA = pltpu.SemaphoreType.DMA


def per_device(grad_terms, momentum, weights, owner_list):
    small = (CHUNKS, MATS, STRIP, HALF)
    large = (CHUNKS, MATS, SIDE, STRIP, HALF)
    whole = (MATS, SIDE, SIDE, BLOCK, HALF)
    tile = pltpu.VMEM((8, LANES), F32)
    square = pltpu.VMEM((FF, FF), BF16)
    new_mom, rows, rms = pl.pallas_call(
        muon_kernel,
        name="muon",
        out_shape=(
            jax.ShapeDtypeStruct((SLOTS, GROUPS, ROWS, FF), F32),
            jax.ShapeDtypeStruct((MATS, ROWS, FF), BF16),
            jax.ShapeDtypeStruct((1, MATS), F32),
        ),
        in_specs=[SMEM, ANY, ANY],
        out_specs=(ANY, VMEM, VMEM),
        scratch_shapes=[
            pltpu.VMEM(whole, BF16), pltpu.VMEM(whole, BF16),
            pltpu.VMEM(large, BF16), pltpu.VMEM((CHUNKS, MATS, 2, SIDE, STRIP, HALF), BF16), pltpu.VMEM(large, BF16),
            pltpu.VMEM(small, BF16), pltpu.VMEM((CHUNKS, MATS, 2, STRIP, HALF), BF16),
            pltpu.VMEM((MATS, BLOCK, HALF), BF16),
            pltpu.VMEM((GROUPS * 2, BLOCK, HALF), BF16),
            pltpu.VMEM((GROUPS * SLOTS, BLOCK, HALF), BF16),
            pltpu.VMEM((GROUPS * 2, BLOCK, HALF), BF16),
            pltpu.VMEM((SLOTS, GROUPS, ROWS, FF), F32),
            pltpu.VMEM((4, GROUPS, BLOCK, HALF), BF16), pltpu.VMEM((4, GROUPS, BLOCK, HALF), BF16),
            pltpu.VMEM((2, GROUPS, BLOCK, HALF), BF16),
            pltpu.VMEM((GROUPS, 2, BLOCK, HALF), BF16),
            pltpu.VMEM((GROUPS * BLOCK, HALF), BF16), pltpu.VMEM((GROUPS * BLOCK, HALF), BF16),
            pltpu.VMEM((3, 32 * PART, LANES), F32),
            pltpu.VMEM((GROUPS, BLOCK, FF), F32),
            pltpu.VMEM((GROUPS, BLOCK, FF), BF16),
            pltpu.VMEM((2, 2 * BLOCK, FF), BF16),
            pltpu.VMEM((32 * PART, LANES), BF16), pltpu.VMEM((2, 32 * PART, LANES), BF16),
            pltpu.VMEM((2, 2, 3, 2 * PART, LANES), BF16),
            pltpu.VMEM((2, 2, 2 * PART, LANES), BF16),
            pltpu.VMEM((2, 2, 3, 2 * PART, LANES), BF16),
            square, square, square, square,
            pltpu.VMEM((2, 2, BLOCK, HALF), BF16), pltpu.VMEM((MATS, BLOCK, HALF), BF16),
            tile, tile, tile, tile,
            pltpu.VMEM((8, 8, LANES), F32), pltpu.VMEM((16, 8, LANES), F32), pltpu.VMEM((16, 8, LANES), F32),
            pltpu.VMEM((8, 8, LANES), F32),
            DMA((CHUNKS,)), DMA((1,)), DMA((CHUNKS, MATS)),
            DMA((3,)), DMA((CHUNKS,)), DMA((CHUNKS,)), DMA((3,)), DMA((CHUNKS,)), DMA((CHUNKS,)),
            DMA((1,)), DMA((1,)), DMA((1,)), DMA((4,)), DMA((1,)), DMA((1,)), DMA((2,)),
            DMA((1,)), DMA((1,)), DMA((1,)), DMA((1,)), DMA((3,)),
            DMA((1,)), DMA((2, 2)), DMA((1,)), DMA((2, 2)), DMA((1,)), DMA((2, 2, 3)), DMA((1,)), DMA((1,)),
            DMA((1,)), DMA((1,)), DMA((1,)), DMA((1,)), DMA((1,)), DMA((1,)), DMA((1,)), DMA((2, 2)), DMA((4,)),
            DMA((1,)),
        ],
        compiler_params=pltpu.CompilerParams(collective_id=0, has_side_effects=True, vmem_limit_bytes=60 << 20),
    )(owner_list, grad_terms.reshape(MATS, SIDE, SIDE, BLOCK, FF), momentum[0])

    rows = rows.astype(F32)
    scale_rms = 0.2 * math.sqrt(max(D, FF))
    update = (scale_rms * rows).astype(BF16)
    new_weights = weights * (1.0 - LEARN * DECAY) - LEARN * scale_rms * rows
    return (new_weights, update, new_mom[None], rms.reshape(MATS))


def solution(mesh):
    placed = (
        P("dp", None, "expert", None),
        P("expert", None, None, "dp", None),
        P(None, ("expert", "dp"), None),
        P(),
    )
    return jax.shard_map(
        per_device,
        mesh=mesh,
        in_specs=placed,
        out_specs=(
            P(None, ("expert", "dp"), None),
            P(None, ("expert", "dp"), None),
            P("expert", None, None, "dp", None),
            P(),
        ),
        check_vma=False,
    )
```
